32 devices in a mesh: dp: 16 (over z, y, core), tensor: 2 (over x).
Axes of the slice: x: 2, y: 2, z: 4, core: 2. Of those that a mesh axis runs over, the one named last changes fastest.
Arguments:
- block_input: bfloat16 [18688, 1024], P(('dp', 'tensor')), may hold values from -6 to 6
- image_mask: int32 [32], P('dp'), may hold values 0 or 1
- w_qkv: bfloat16 [3, 1024, 1024], P(None, 'dp', 'tensor'), may hold values from -0.1875 to 0.1875
- b_qv: float32 [2, 1024], P(None, 'tensor'), may hold values from -1.5 to 1.5
- w_out: bfloat16 [1024, 1024], P('tensor', 'dp'), may hold values from -1.5 to 1.5
- b_out: float32 [1024], replicated, may hold values from -1.5 to 1.5
- w_fc1: bfloat16 [1024, 4096], P('dp', 'tensor'), may hold values from -0.1875 to 0.1875
- b_fc1: float32 [4096], P('tensor'), may hold values from -1.5 to 1.5
- w_fc2: bfloat16 [4096, 1024], P('tensor', 'dp'), may hold values from -0.09375 to 0.09375
- b_fc2: float32 [1024], replicated, may hold values from -1.5 to 1.5
- ln1_gain: float32 [1024], replicated, may hold values from 0.5 to 1.5
- ln1_bias: float32 [1024], replicated, may hold values from -1.5 to 1.5
- ln2_gain: float32 [1024], replicated, may hold values from 0.5 to 1.5
- ln2_bias: float32 [1024], replicated, may hold values from -1.5 to 1.5
- grad_out: bfloat16 [18688, 1024], P(('dp', 'tensor')), may hold values from -6 to 6
Outputs:
- layer_output: bfloat16 [18688, 1024], P(('dp', 'tensor'))
- input_grad: bfloat16 [18688, 1024], P(('dp', 'tensor'))
- grad_w_qkv: float32 [3, 1024, 1024], P(None, 'dp', 'tensor')
- grad_b_qv: float32 [2, 1024], P(None, 'tensor')
- grad_w_out: float32 [1024, 1024], P('tensor', 'dp')
- grad_b_out: float32 [1024], replicated
- grad_w_fc1: float32 [1024, 4096], P('dp', 'tensor')
- grad_b_fc1: float32 [4096], P('tensor')
- grad_w_fc2: float32 [4096, 1024], P('tensor', 'dp')
- grad_b_fc2: float32 [1024], replicated
- grad_ln1_gain: float32 [1024], replicated
- grad_ln1_bias: float32 [1024], replicated
- grad_ln2_gain: float32 [1024], replicated
- grad_ln2_bias: float32 [1024], replicated
The draws below stay inside these ranges and needn't reach their ends.
All inputs are finite; a program needn't handle non-finite values. No bound on the sum of `image_mask` on one device may be relied on, other than what follows from the above.
Results may differ from the reference program's by a relative error of at most 0.0098.
Values may be sent and summed in bfloat16 or wider, within the bound.
No kernel may reach another device: no remote copies, remote signals or barrier semaphores. Data moves between devices by JAX's collectives and lax.ppermute only.
A program may use at most 128 MiB of HBM per device.

```python
import jax
import jax.numpy as jnp
from jax import lax

D = 1024
HEADS = 16
FF = 4096
SEQ = 584
VALID = 577
IMAGES = 32
TOKENS = 18688


def set_ends(entries, stream_key, low, top_value):
    shape = entries.shape
    place = [jax.random.randint(jax.random.fold_in(stream_key, axis), (), 0, shape[axis]) for axis in range(len(shape))]
    entries = entries.at[tuple(place)].set(low)
    longest = shape.index(max(shape))
    place[longest] = (place[longest] + 1) % shape[longest]
    return entries.at[tuple(place)].set(top_value)


def block_levels(stream_key, extent, cuts, smallest, largest):
    def one(axis_at, shards_of):
        draws = jax.random.uniform(jax.random.fold_in(jax.random.fold_in(stream_key, 6), axis_at), (shards_of,), jnp.float32, smallest / len(cuts), largest / len(cuts))
        return jnp.repeat(jnp.exp(draws), extent[axis_at] // shards_of).reshape((-1,) + (1,) * (len(extent) - axis_at - 1))

    loudness = one(*cuts[0])
    for cut in cuts[1:]:
        loudness = loudness * one(*cut)
    return loudness


def gaussian(stream_key, shape, width, limit, shards=(), held_as=jnp.bfloat16):
    loudness = block_levels(stream_key, shape, shards, -0.22, 0.18) if shards else 1.0
    array = jax.random.normal(stream_key, shape, jnp.float32) * width * loudness
    return jnp.minimum(jnp.maximum(array, -limit), limit).astype(held_as)


def setup_inputs(seed: int = 0) -> dict:
    seeds = jax.random.split(jax.random.key(seed), 16)
    return {
        "block_input": gaussian(seeds[0], (TOKENS, D), 1.0, 6.0, ((0, 32),)),
        "image_mask": set_ends((jax.random.randint(seeds[1], (IMAGES,), 0, 4) < 3).astype(jnp.int32), jax.random.fold_in(seeds[1], 1), 0, 1),
        "w_qkv": gaussian(seeds[2], (3, D, D), D ** -0.5, 0.1875, ((1, 16), (2, 2))),
        "b_qv": gaussian(seeds[3], (2, D), 0.3, 1.5, ((1, 2),), jnp.float32),
        "w_out": gaussian(seeds[4], (D, D), (D // 64) ** -0.5, 1.5, ((0, 2), (1, 16))),
        "b_out": gaussian(seeds[5], (D,), 0.3, 1.5, (), jnp.float32),
        "w_fc1": gaussian(seeds[6], (D, FF), D ** -0.5, 0.1875, ((0, 16), (1, 2))),
        "b_fc1": gaussian(seeds[7], (FF,), 0.3, 1.5, ((0, 2),), jnp.float32),
        "w_fc2": gaussian(seeds[8], (FF, D), FF ** -0.5, 0.09375, ((0, 2), (1, 16))),
        "b_fc2": gaussian(seeds[9], (D,), 0.3, 1.5, (), jnp.float32),
        "ln1_gain": jnp.clip(1.0 + 0.1 * jax.random.normal(seeds[10], (D,), jnp.float32), 0.5, 1.5),
        "ln1_bias": gaussian(seeds[11], (D,), 0.3, 1.5, (), jnp.float32),
        "ln2_gain": jnp.clip(1.0 + 0.1 * jax.random.normal(seeds[12], (D,), jnp.float32), 0.5, 1.5),
        "ln2_bias": gaussian(seeds[13], (D,), 0.3, 1.5, (), jnp.float32),
        "grad_out": gaussian(seeds[14], (TOKENS, D), 1.0, 6.0, ((0, 32),)),
    }


@jax.custom_vjp
def low(v):
    return lax.optimization_barrier(v.astype(jnp.bfloat16)).astype(jnp.float32)

@jax.custom_vjp
def low_back(v):
    return v

def low_keep(v):
    return (low(v), None)

def low_pass(kept, grad):
    return (grad,)

def back_keep(v):
    return (v, None)

def back_low(kept, grad):
    return (low(grad),)
low.defvjp(low_keep, low_pass)
low_back.defvjp(back_keep, back_low)
layer_eps = 1e-06
masked_score = -1e+30
highest = lax.Precision.HIGHEST

def normalize(signal, gain_vec, bias_vec):
    row_mean = lax.optimization_barrier(jnp.mean(signal, axis=-1, keepdims=True))
    centred = signal - row_mean
    row_spread = lax.optimization_barrier(jnp.mean(centred * centred, axis=-1, keepdims=True))
    return centred * lax.rsqrt(row_spread + layer_eps) * gain_vec + bias_vec

def image_block(signal, keep_rows, params):
    w_qkv, b_qv, w_out, b_out, w_fc1, b_fc1, w_fc2, b_fc2, gain_one, bias_one, gain_two, bias_two = params
    head_dim = signal.shape[1] // HEADS
    normed_one = low(normalize(signal, gain_one, bias_one))
    projected = jnp.einsum('td,cde->cte', normed_one, w_qkv, precision=highest)
    queries = low_back(low(projected[0] + b_qv[0]))
    key_proj = low_back(low(projected[1]))
    value_proj = low_back(low(projected[2] + b_qv[1]))
    head_shape = (SEQ, HEADS, head_dim)
    scores = jnp.einsum('qhe,khe->hqk', queries.reshape(head_shape), key_proj.reshape(head_shape), precision=highest)
    scores = low_back(scores * head_dim ** (-0.5))
    valid_keys = jnp.arange(SEQ) < VALID
    logits = jnp.where(valid_keys[None, None, :], scores, masked_score)
    weights = low(jax.nn.softmax(logits, axis=-1))
    head_mixed = jnp.einsum('hqk,khe->qhe', weights, value_proj.reshape(head_shape), precision=highest)
    head_mixed = low_back(low(head_mixed.reshape(SEQ, HEADS * head_dim)))
    attn_branch = low_back(jnp.dot(head_mixed, w_out, precision=highest)) + b_out
    resid = signal + attn_branch
    normed_two = low(normalize(resid, gain_two, bias_two))
    hidden_pre = low_back(jnp.dot(normed_two, w_fc1, precision=highest) + b_fc1)
    hidden = low(jax.nn.gelu(hidden_pre, approximate=False))
    mlp_branch = jnp.dot(hidden, w_fc2, precision=highest) + b_fc2
    return (resid + mlp_branch) * keep_rows[:, None]

def reference(block_input, image_mask, w_qkv, b_qv, w_out, b_out, w_fc1, b_fc1, w_fc2, b_fc2, ln1_gain, ln1_bias, ln2_gain, ln2_bias, grad_out):
    slot_keep = jnp.repeat(image_mask, SEQ).reshape(IMAGES, SEQ)
    token_keep = (slot_keep * (jnp.arange(SEQ) < VALID)[None, :].astype(jnp.int32)).astype(jnp.float32)
    floats = [item.astype(jnp.float32) for item in (block_input, w_qkv, b_qv, w_out, b_out, w_fc1, b_fc1, w_fc2, b_fc2, ln1_gain, ln1_bias, ln2_gain, ln2_bias)]

    def forward(signal, *params):
        stacked = signal.reshape(IMAGES, SEQ, signal.shape[1])

        def one_image(pair):
            return image_block(pair[0], pair[1], params)
        result = lax.map(jax.checkpoint(one_image), (stacked, token_keep))
        return result.reshape(TOKENS, signal.shape[1])
    result, backward = jax.vjp(forward, *floats)
    grads = backward(grad_out.astype(jnp.float32))
    return (result.astype(jnp.bfloat16), grads[0].astype(jnp.bfloat16), grads[1], grads[2], grads[3], grads[4], grads[5], grads[6], grads[7], grads[8], grads[9], grads[10], grads[11], grads[12])
```

```python
import functools

import jax
import jax.numpy as jnp
from jax import lax
from jax.experimental import pallas as pl
from jax.experimental.pallas import tpu as pltpu
from jax.sharding import PartitionSpec as P

HEADS = 16
SEQ = 584
VALID = 577


layer_eps = 1e-06
masked_score = -1e30


def normalize(signal, gain_vec, bias_vec):
    row_mean = jnp.mean(signal, axis=-1, keepdims=True)
    centred = signal - row_mean
    row_spread = jnp.mean(centred * centred, axis=-1, keepdims=True)
    return centred * lax.rsqrt(row_spread + layer_eps) * gain_vec + bias_vec


def gelu_exact(signal):
    return jax.nn.gelu(signal, approximate=False)


def masked_scores(queries, key_proj):
    score_scale = queries.shape[-1] ** (-0.5)
    scores = (
        jnp.einsum("qhe,khe->hqk", queries, key_proj, preferred_element_type=jnp.float32)
        * score_scale
    )
    valid_keys = jnp.arange(scores.shape[-1]) < VALID
    return jnp.where(valid_keys[None, None, :], scores, masked_score)


def attend_image(operands):
    queries, key_proj, value_proj = operands
    logits = masked_scores(queries, key_proj)
    row_top = jnp.max(logits, axis=-1, keepdims=True)
    row_expo = jnp.exp(logits - row_top)
    row_total = jnp.sum(row_expo, axis=-1, keepdims=True)
    weights = (row_expo / row_total).astype(jnp.bfloat16)
    head_mixed = jnp.einsum("hqk,khe->qhe", weights, value_proj, preferred_element_type=jnp.float32)
    return (head_mixed.astype(jnp.bfloat16), (row_top + jnp.log(row_total))[..., 0])


def attend_back(operands):
    queries, key_proj, value_proj, mixed_grad, row_lse = operands
    score_scale = queries.shape[-1] ** (-0.5)
    logits = masked_scores(queries, key_proj)
    probs = jnp.exp(logits - row_lse[..., None])
    value_grad = jnp.einsum(
        "hqk,qhe->khe", probs.astype(jnp.bfloat16), mixed_grad, preferred_element_type=jnp.float32
    )
    prob_grad = jnp.einsum(
        "qhe,khe->hqk", mixed_grad, value_proj, preferred_element_type=jnp.float32
    )
    score_grad = probs * (prob_grad - jnp.sum(probs * prob_grad, axis=-1, keepdims=True))
    score_grad = score_grad.astype(jnp.bfloat16)
    query_grad = (
        jnp.einsum("hqk,khe->qhe", score_grad, key_proj, preferred_element_type=jnp.float32)
        * score_scale
    )
    key_grad = (
        jnp.einsum("hqk,qhe->khe", score_grad, queries, preferred_element_type=jnp.float32)
        * score_scale
    )
    return (
        query_grad.astype(jnp.bfloat16),
        key_grad.astype(jnp.bfloat16),
        value_grad.astype(jnp.bfloat16),
    )


def split_heads(
    block_input,
    image_mask,
    w_qkv,
    b_qv,
    w_out,
    b_out,
    w_fc1,
    b_fc1,
    w_fc2,
    b_fc2,
    ln1_gain,
    ln1_bias,
    ln2_gain,
    ln2_bias,
    grad_out,
):
    local_rows = block_input.shape[0]
    model_width = block_input.shape[1]
    image_count = image_mask.shape[0]
    head_dim = model_width // HEADS
    local_width = w_qkv.shape[2]
    local_heads = local_width // head_dim
    tensor_index = lax.axis_index("tensor")
    token_index = tensor_index * local_rows + jnp.arange(local_rows)
    image_of = token_index // SEQ
    position = token_index % SEQ
    image_pick = (image_of[:, None] == jnp.arange(image_count)[None, :]).astype(jnp.float32)
    token_keep = jnp.sum(image_pick * image_mask.astype(jnp.float32)[None, :], axis=1)
    token_keep = token_keep * (position < VALID).astype(jnp.float32)
    contract_rows = (((0,), (0,)), ((), ()))
    contract_cols = (((1,), (1,)), ((), ()))
    full_qkv, full_out, full_fc1, full_fc2 = (
        lax.all_gather(w_qkv, "dp", axis=1, tiled=True),
        lax.all_gather(w_out, "dp", axis=1, tiled=True),
        lax.all_gather(w_fc1, "dp", axis=0, tiled=True),
        lax.all_gather(w_fc2, "dp", axis=1, tiled=True),
    )
    input_float = block_input.astype(jnp.float32)
    normed_one = normalize(input_float, ln1_gain, ln1_bias).astype(jnp.bfloat16)
    inputs_one = lax.all_gather(normed_one, "tensor", axis=0, tiled=True)
    group_rows = inputs_one.shape[0]
    projected = jnp.einsum("td,cde->cte", inputs_one, full_qkv, preferred_element_type=jnp.float32)
    queries = (projected[0] + b_qv[0]).astype(jnp.bfloat16)
    key_proj = projected[1].astype(jnp.bfloat16)
    value_proj = (projected[2] + b_qv[1]).astype(jnp.bfloat16)
    head_shape = (group_rows // SEQ, SEQ, local_heads, head_dim)
    query_heads = queries.reshape(head_shape)
    key_heads = key_proj.reshape(head_shape)
    value_heads = value_proj.reshape(head_shape)
    head_mixed, row_lse = lax.map(attend_image, (query_heads, key_heads, value_heads))
    head_mixed = head_mixed.reshape(group_rows, local_width)
    row_block = head_mixed
    attn_sum = lax.psum_scatter(
        jnp.dot(row_block, full_out, preferred_element_type=jnp.float32),
        "tensor",
        scatter_dimension=0,
        tiled=True,
    )
    resid = input_float + (attn_sum + b_out)
    normed_two = normalize(resid, ln2_gain, ln2_bias).astype(jnp.bfloat16)
    inputs_two = lax.all_gather(normed_two, "tensor", axis=0, tiled=True)
    hidden_pre = jnp.dot(inputs_two, full_fc1, preferred_element_type=jnp.float32) + b_fc1
    hidden = gelu_exact(hidden_pre).astype(jnp.bfloat16)
    row_block = hidden
    mlp_sum = lax.psum_scatter(
        jnp.dot(row_block, full_fc2, preferred_element_type=jnp.float32).astype(jnp.bfloat16),
        "tensor",
        scatter_dimension=0,
        tiled=True,
    ).astype(jnp.float32)
    layer_output = ((resid + (mlp_sum + b_fc2)) * token_keep[:, None]).astype(jnp.bfloat16)
    cot_rows = grad_out * token_keep.astype(jnp.bfloat16)[:, None]
    cot_float = cot_rows.astype(jnp.float32)
    cot_group = lax.all_gather(cot_rows, "tensor", axis=0, tiled=True)
    fc2_grad_group = lax.dot_general(
        hidden, cot_group, contract_rows, preferred_element_type=jnp.float32
    )
    hidden_grad = lax.dot_general(
        cot_group, full_fc2, contract_cols, preferred_element_type=jnp.float32
    )
    gelu_value, gelu_back = jax.vjp(gelu_exact, hidden_pre)
    pre_grad = gelu_back(hidden_grad)[0].astype(jnp.bfloat16)
    fc1_bias_grad = jnp.sum(pre_grad, axis=0, dtype=jnp.float32)
    fc1_grad_group = lax.dot_general(
        inputs_two, pre_grad, contract_rows, preferred_element_type=jnp.float32
    )
    row_block = pre_grad
    normed_two_grad = lax.psum_scatter(
        lax.dot_general(row_block, full_fc1, contract_cols, preferred_element_type=jnp.float32),
        "tensor",
        scatter_dimension=0,
        tiled=True,
    )
    norm_two_value, norm_two_back = jax.vjp(normalize, resid, ln2_gain, ln2_bias)
    resid_back, gain_two_grad, bias_two_grad = norm_two_back(normed_two_grad)
    resid_grad = cot_float + resid_back
    out_bias_grad = jnp.sum(resid_grad, axis=0)
    fc2_bias_grad = jnp.sum(cot_float, axis=0)
    resid_low = resid_grad.astype(jnp.bfloat16)
    resid_group = lax.all_gather(resid_low, "tensor", axis=0, tiled=True)
    out_grad_group = lax.dot_general(
        head_mixed, resid_group, contract_rows, preferred_element_type=jnp.float32
    )
    mixed_grad = lax.dot_general(
        resid_group, full_out, contract_cols, preferred_element_type=jnp.float32
    ).astype(jnp.bfloat16)
    query_grad, key_grad, value_grad = lax.map(
        attend_back, (query_heads, key_heads, value_heads, mixed_grad.reshape(head_shape), row_lse)
    )
    stacked_grads = jnp.stack(
        [
            query_grad.reshape(group_rows, local_width),
            key_grad.reshape(group_rows, local_width),
            value_grad.reshape(group_rows, local_width),
        ]
    )
    qkv_grad_group = jnp.einsum(
        "td,cte->cde", inputs_one, stacked_grads, preferred_element_type=jnp.float32
    )
    qv_bias_grad = jnp.stack(
        [
            jnp.sum(stacked_grads[0], axis=0, dtype=jnp.float32),
            jnp.sum(stacked_grads[2], axis=0, dtype=jnp.float32),
        ]
    )
    row_block = stacked_grads
    normed_one_grad = lax.psum_scatter(
        jnp.einsum("cte,cde->td", row_block, full_qkv, preferred_element_type=jnp.float32),
        "tensor",
        scatter_dimension=0,
        tiled=True,
    )
    norm_one_value, norm_one_back = jax.vjp(normalize, input_float, ln1_gain, ln1_bias)
    input_back, gain_one_grad, bias_one_grad = norm_one_back(normed_one_grad)
    input_grad = (resid_grad + input_back).astype(jnp.bfloat16)
    grad_w_qkv, grad_w_out, grad_w_fc1, grad_w_fc2 = (
        lax.psum_scatter(qkv_grad_group, "dp", scatter_dimension=1, tiled=True),
        lax.psum_scatter(out_grad_group, "dp", scatter_dimension=1, tiled=True),
        lax.psum_scatter(fc1_grad_group, "dp", scatter_dimension=0, tiled=True),
        lax.psum_scatter(fc2_grad_group, "dp", scatter_dimension=1, tiled=True),
    )
    vector_sums = lax.psum(
        (gain_one_grad, bias_one_grad, gain_two_grad, bias_two_grad, out_bias_grad, fc2_bias_grad),
        ("dp", "tensor"),
    )
    qv_sum, fc1_sum = lax.psum((qv_bias_grad, fc1_bias_grad), "dp")
    return (
        layer_output,
        input_grad,
        grad_w_qkv,
        qv_sum,
        grad_w_out,
        vector_sums[4],
        grad_w_fc1,
        fc1_sum,
        grad_w_fc2,
        vector_sums[5],
        vector_sums[0],
        vector_sums[1],
        vector_sums[2],
        vector_sums[3],
    )


BIT_X, BIT_CORE, BIT_Y, BIT_Z_LOW, BIT_Z_HIGH = 1, 2, 4, 8, 16
AXES = ("dp", "tensor")


def exchange(block, bit):
    return lax.ppermute(block, AXES, [(src, src ^ bit) for src in range(32)])


def gather_weights(shard):
    half = shard.shape[1] // 2
    block = jnp.concatenate([shard, exchange(shard, BIT_Z_HIGH)], axis=0)
    first = exchange(block[:, :half], BIT_X)
    second = exchange(block[:, half:], BIT_Y)
    block = jnp.stack([block, jnp.concatenate([first, second], axis=1)])
    block = jnp.concatenate([block, exchange(block, BIT_Z_LOW)], axis=1)
    first = exchange(block[:, :, :half], BIT_Y)
    second = exchange(block[:, :, half:], BIT_X)
    near = (block, first, second)
    far = tuple(exchange(piece, BIT_CORE) for piece in near)
    return near, far


def assemble(pieces):
    sides = []
    for side in range(2):
        columns = []
        low, high = [], []
        for block, first, second in pieces:
            half = first.shape[2]
            low += [block[side, :, :half], first[side]]
            high += [block[0, :, half:], block[1, :, half:]] if side == 0 else [second[0], second[1]]
        sides.append(jnp.concatenate([jnp.concatenate(low, axis=0), jnp.concatenate(high, axis=0)], axis=1))
    return sides


def scatter_grads(sides):
    grads = jnp.stack(sides)
    half = grads.shape[2] // 2
    low = jnp.bfloat16
    block = (grads[:, :512] + exchange(grads[:, 512:], BIT_CORE)).astype(low)
    first = block[:, :256, :half] + exchange(block[:, 256:, :half], BIT_Y)
    second = block[0, :, half:] + exchange(block[1, :, half:], BIT_X)
    block = jnp.concatenate([first, second.reshape(2, 256, half)], axis=2)
    block = block[:, :128] + exchange(block[:, 128:], BIT_Z_LOW)
    first = block[0, :, :half] + exchange(block[1, :, :half], BIT_X)
    second = block[0, :, half:] + exchange(block[1, :, half:], BIT_Y)
    block = jnp.concatenate([first, second], axis=1)
    other = exchange(block[64:], BIT_Z_HIGH)
    return block[:64].astype(jnp.float32) + other.astype(jnp.float32)


def total(vectors, bits):
    for bit in bits:
        vectors = vectors + exchange(vectors, bit)
    return vectors


def place_matrix():
    relative = lax.broadcasted_iota(jnp.int32, (1024, 1024), 1)
    feature = lax.broadcasted_iota(jnp.int32, (1024, 1024), 0)
    block = relative // 64
    shard = (block // 8) + 2 * (block // 4 % 2) + 4 * (block // 2 % 2) + 8 * (block % 2)
    shard = shard ^ lax.axis_index("dp")
    return (feature == shard * 64 + relative % 64).astype(jnp.bfloat16)


def attend_kernel(q_ref, k_ref, v_ref, o_ref, lse_ref):
    queries, keys, values = q_ref[...], k_ref[...], v_ref[...]
    queries = queries * jnp.bfloat16(0.125)
    lane = lax.broadcasted_iota(jnp.int32, keys.shape, 1)
    mixed = []
    for head in range(2):
        own = (lane // 64) == head
        scores = lax.dot_general(
            jnp.where(own, keys, 0), queries, (((1,), (1,)), ((), ())), preferred_element_type=jnp.float32
        )
        valid = lax.broadcasted_iota(jnp.int32, scores.shape, 0) < VALID
        scores = jnp.where(valid, scores, masked_score)
        top = jnp.max(scores, axis=0, keepdims=True)
        expo = jnp.exp(scores - top)
        norm = jnp.sum(expo, axis=0, keepdims=True)
        out = lax.dot_general(
            values, expo.astype(jnp.bfloat16), (((0,), (0,)), ((), ())), preferred_element_type=jnp.float32
        )
        mixed.append(out[head * 64 : head * 64 + 64] / norm)
        lse_ref[0, head : head + 1, :] = top + jnp.log(norm)
    o_ref[...] = jnp.concatenate(mixed, axis=0).T.astype(jnp.bfloat16)


def attend(projected):
    rows = projected.shape[0]
    images = rows // SEQ

    def column(offset):
        return lambda image, pair: (image, (pair // 4) * 12 + offset + pair % 4)

    return pl.pallas_call(
        attend_kernel,
        grid=(images, 8),
        in_specs=[pl.BlockSpec((SEQ, 128), column(4 * c)) for c in range(3)],
        out_specs=[
            pl.BlockSpec((SEQ, 128), lambda image, pair: (image, pair)),
            pl.BlockSpec((1, 2, SEQ), lambda image, pair: (image * 8 + pair, 0, 0)),
        ],
        out_shape=[
            jax.ShapeDtypeStruct((rows, 1024), jnp.bfloat16),
            jax.ShapeDtypeStruct((images * 8, 2, SEQ), jnp.float32),
        ],
        compiler_params=pltpu.CompilerParams(vmem_limit_bytes=24 << 20),
        cost_estimate=pl.CostEstimate(flops=images * 14 * 10**9, bytes_accessed=images * 5 * 10**6, transcendentals=images * 6 * 10**6),
    )(projected, projected, projected)


def attend_back_kernel(q_ref, k_ref, v_ref, do_ref, lse_ref, dq_ref, dk_ref, dv_ref):
    queries, keys, values, mixed_grad = q_ref[...], k_ref[...], v_ref[...], do_ref[...]
    queries = queries * jnp.bfloat16(0.125)
    lane = lax.broadcasted_iota(jnp.int32, keys.shape, 1)
    dq, dk, dv = [], [], []
    for head in range(2):
        own = (lane // 64) == head
        scores = lax.dot_general(
            jnp.where(own, keys, 0), queries, (((1,), (1,)), ((), ())), preferred_element_type=jnp.float32
        )
        valid = lax.broadcasted_iota(jnp.int32, scores.shape, 0) < VALID
        probs = jnp.where(valid, jnp.exp(scores - lse_ref[0, head : head + 1, :]), 0)
        dv.append(jnp.dot(probs.astype(jnp.bfloat16), mixed_grad, preferred_element_type=jnp.float32))
        back = lax.dot_general(
            jnp.where(own, values, 0), mixed_grad, (((1,), (1,)), ((), ())), preferred_element_type=jnp.float32
        )
        row = jnp.sum(probs * back, axis=0, keepdims=True)
        score_grad = (probs * (back - row)).astype(jnp.bfloat16)
        dk.append(jnp.dot(score_grad, queries, preferred_element_type=jnp.float32))
        out = lax.dot_general(
            keys, score_grad, (((0,), (0,)), ((), ())), preferred_element_type=jnp.float32
        )
        dq.append(out[head * 64 : head * 64 + 64] * 0.125)
    low = lane < 64
    dq_ref[...] = jnp.concatenate(dq, axis=0).T.astype(jnp.bfloat16)
    dk_ref[...] = jnp.where(low, dk[0], dk[1]).astype(jnp.bfloat16)
    dv_ref[...] = jnp.where(low, dv[0], dv[1]).astype(jnp.bfloat16)


def attend_back_all(projected, mixed_grad, lse):
    rows = projected.shape[0]
    images = rows // SEQ

    def column(offset):
        return lambda image, pair: (image, (pair // 4) * 12 + offset + pair % 4)

    return pl.pallas_call(
        attend_back_kernel,
        grid=(images, 8),
        in_specs=[pl.BlockSpec((SEQ, 128), column(4 * c)) for c in range(3)]
        + [
            pl.BlockSpec((SEQ, 128), lambda image, pair: (image, pair)),
            pl.BlockSpec((1, 2, SEQ), lambda image, pair: (image * 8 + pair, 0, 0)),
        ],
        out_specs=[pl.BlockSpec((SEQ, 128), lambda image, pair: (image, pair))] * 3,
        out_shape=[jax.ShapeDtypeStruct((rows, 1024), jnp.bfloat16)] * 3,
        compiler_params=pltpu.CompilerParams(vmem_limit_bytes=32 << 20),
        cost_estimate=pl.CostEstimate(flops=images * 28 * 10**9, bytes_accessed=images * 9 * 10**6, transcendentals=images * 6 * 10**6),
    )(projected, projected, projected, mixed_grad, lse)


def own_images(
    block_input,
    image_mask,
    w_qkv,
    b_qv,
    w_out,
    b_out,
    w_fc1,
    b_fc1,
    w_fc2,
    b_fc2,
    ln1_gain,
    ln1_bias,
    ln2_gain,
    ln2_bias,
    grad_out,
):
    f32, low = jnp.float32, jnp.bfloat16
    rows = block_input.shape[0]
    tensor_index = lax.axis_index("tensor")
    token_index = tensor_index * rows + jnp.arange(rows)
    image_pick = ((token_index // SEQ)[:, None] == jnp.arange(image_mask.shape[0])[None, :]).astype(f32)
    token_keep = jnp.sum(image_pick * image_mask.astype(f32)[None, :], axis=1)
    token_keep = token_keep * (token_index % SEQ < VALID).astype(f32)

    def rows_of(left, right):
        return lax.dot_general(left, right, (((0,), (0,)), ((), ())), preferred_element_type=f32)

    def cols_of(left, right):
        return lax.dot_general(left, right, (((1,), (1,)), ((), ())), preferred_element_type=f32)

    def dot(left, right):
        return jnp.dot(left, right, preferred_element_type=f32)

    attn_shard = jnp.concatenate([w_qkv[0], w_qkv[1], w_qkv[2], w_out.T], axis=1)
    attn_pieces = gather_weights(attn_shard)
    fc1_pieces = gather_weights(w_fc1)
    fc2_pieces = gather_weights(w_fc2.T)
    bias_own = jnp.concatenate([b_qv.reshape(-1), b_fc1])[None, :]
    bias_sides = jnp.concatenate([bias_own, exchange(bias_own, BIT_X)], axis=0)

    place = place_matrix()
    vectors = jnp.stack([b_out, b_fc2, ln1_gain, ln1_bias, ln2_gain, ln2_bias])
    vectors = jnp.dot(vectors, place.astype(f32), precision=lax.Precision.HIGHEST)
    b_out, b_fc2, ln1_gain, ln1_bias, ln2_gain, ln2_bias = vectors
    signal = dot(block_input, place)
    cot_low = dot(grad_out * token_keep.astype(low)[:, None], place).astype(low)
    cot = cot_low.astype(f32)

    normed_one = normalize(signal, ln1_gain, ln1_bias).astype(low)
    w_attn = assemble(attn_pieces)
    projected = []
    for side in range(2):
        bias = bias_sides[side]
        bias = jnp.concatenate([bias[:512], jnp.zeros((512,), f32), bias[512:1024]])
        projected.append((dot(normed_one, w_attn[side][:, :1536]) + bias).astype(low))
    projected = jnp.concatenate(projected, axis=1)
    mixed, lse = attend(projected)
    attn = sum(cols_of(mixed[:, side * 512 : side * 512 + 512], w_attn[side][:, 1536:]) for side in range(2))
    resid = signal + (attn + b_out)
    normed_two = normalize(resid, ln2_gain, ln2_bias).astype(low)
    w_one = assemble(fc1_pieces)
    hidden, slope = [], []
    for side in range(2):
        pre = dot(normed_two, w_one[side]) + bias_sides[side, 1024:]
        phi = 0.5 * (1.0 + lax.erf(pre * (0.5**0.5)))
        hidden.append((pre * phi).astype(low))
        slope.append((phi + pre * (jnp.exp(-0.5 * pre * pre) * (0.5 / 3.141592653589793) ** 0.5)).astype(low))
    fc2_grad = scatter_grads([rows_of(cot_low, hidden[side]).astype(low) for side in range(2)])
    w_two = assemble(fc2_pieces)
    pre_grad = [(dot(cot_low, w_two[side]) * slope[side].astype(f32)).astype(low) for side in range(2)]
    fc1_grad = scatter_grads([rows_of(normed_two, pre_grad[side]).astype(low) for side in range(2)])
    fc1_bias_grad = jnp.stack([jnp.sum(pre_grad[side], axis=0, dtype=f32) for side in range(2)])
    normed_two_grad = sum(cols_of(pre_grad[side], w_one[side]) for side in range(2))
    _, norm_two_back = jax.vjp(normalize, resid, ln2_gain, ln2_bias)
    resid_back, gain_two_grad, bias_two_grad = norm_two_back(normed_two_grad)
    resid_grad = cot + resid_back
    resid_low = resid_grad.astype(low)
    mixed_grad = jnp.concatenate([dot(resid_low, w_attn[side][:, 1536:]).astype(low) for side in range(2)], axis=1)
    query_grad, key_grad, value_grad = attend_back_all(projected, mixed_grad, lse)
    attn_grads, normed_one_grad = [], 0.0
    for side in range(2):
        part = slice(side * 512, side * 512 + 512)
        side_grads = jnp.concatenate([query_grad[:, part], key_grad[:, part], value_grad[:, part]], axis=1)
        attn_grads.append(
            jnp.concatenate([rows_of(normed_one, side_grads), rows_of(resid_low, mixed[:, part])], axis=1).astype(low)
        )
        normed_one_grad = normed_one_grad + cols_of(side_grads, w_attn[side][:, :1536])
    attn_grad = scatter_grads(attn_grads)
    _, norm_one_back = jax.vjp(normalize, signal, ln1_gain, ln1_bias)
    input_back, gain_one_grad, bias_one_grad = norm_one_back(normed_one_grad)
    input_grad = cols_of((resid_grad + input_back).astype(low), place).astype(low)

    mlp = sum(cols_of(hidden[side], w_two[side]) for side in range(2))
    layer_output = ((resid + (mlp + b_fc2)) * token_keep[:, None]).astype(low)
    layer_output = cols_of(layer_output, place).astype(low)

    sums = jnp.stack(
        [
            gain_one_grad,
            bias_one_grad,
            gain_two_grad,
            bias_two_grad,
            jnp.sum(resid_grad, axis=0),
            jnp.sum(cot, axis=0),
        ]
    )
    sums = lax.dot_general(
        sums, place.astype(f32), (((1,), (1,)), ((), ())), precision=lax.Precision.HIGHEST
    )
    sums = total(sums, (BIT_X, BIT_CORE, BIT_Y, BIT_Z_LOW, BIT_Z_HIGH))
    side_sums = jnp.concatenate(
        [
            jnp.sum(query_grad, axis=0, dtype=f32).reshape(2, 512),
            jnp.sum(value_grad, axis=0, dtype=f32).reshape(2, 512),
            fc1_bias_grad,
        ],
        axis=1,
    )
    side_sums = side_sums[:1] + exchange(side_sums[1:], BIT_X)
    side_sums = total(side_sums, (BIT_CORE, BIT_Y, BIT_Z_LOW, BIT_Z_HIGH))[0]
    return (
        layer_output,
        input_grad,
        attn_grad[:, :1536].reshape(64, 3, 512).transpose(1, 0, 2),
        side_sums[:1024].reshape(2, 512),
        attn_grad[:, 1536:].T,
        sums[4],
        fc1_grad,
        side_sums[1024:],
        fc2_grad.T,
        sums[5],
        sums[0],
        sums[1],
        sums[2],
        sums[3],
    )


def solution(mesh):
    def plan(block_input, *others):
        whole_images = block_input.shape[0] % SEQ == 0
        if whole_images and mesh.shape["dp"] == 16 and mesh.shape["tensor"] == 2:
            return own_images(block_input, *others)
        return split_heads(block_input, *others)

    return jax.shard_map(
        plan,
        mesh=mesh,
        in_specs=(
            P(("dp", "tensor"), None),
            P("dp"),
            P(None, "dp", "tensor"),
            P(None, "tensor"),
            P("tensor", "dp"),
            P(),
            P("dp", "tensor"),
            P("tensor"),
            P("tensor", "dp"),
            P(),
            P(),
            P(),
            P(),
            P(),
            P(("dp", "tensor"), None),
        ),
        out_specs=(
            P(("dp", "tensor"), None),
            P(("dp", "tensor"), None),
            P(None, "dp", "tensor"),
            P(None, "tensor"),
            P("tensor", "dp"),
            P(),
            P("dp", "tensor"),
            P("tensor"),
            P("tensor", "dp"),
            P(),
            P(),
            P(),
            P(),
            P(),
        ),
        check_vma=False,
    )
```

```python
import functools

import jax
import jax.numpy as jnp
from jax import lax
from jax.experimental import pallas as pl
from jax.experimental.pallas import tpu as pltpu
from jax.sharding import PartitionSpec as P

HEADS = 16
SEQ = 584
VALID = 577


layer_eps = 1e-06
masked_score = -1e30


def normalize(signal, gain_vec, bias_vec):
    row_mean = jnp.mean(signal, axis=-1, keepdims=True)
    centred = signal - row_mean
    row_spread = jnp.mean(centred * centred, axis=-1, keepdims=True)
    return centred * lax.rsqrt(row_spread + layer_eps) * gain_vec + bias_vec


def gelu_exact(signal):
    return jax.nn.gelu(signal, approximate=False)


def masked_scores(queries, key_proj):
    score_scale = queries.shape[-1] ** (-0.5)
    scores = (
        jnp.einsum("qhe,khe->hqk", queries, key_proj, preferred_element_type=jnp.float32)
        * score_scale
    )
    valid_keys = jnp.arange(scores.shape[-1]) < VALID
    return jnp.where(valid_keys[None, None, :], scores, masked_score)


def attend_image(operands):
    queries, key_proj, value_proj = operands
    logits = masked_scores(queries, key_proj)
    row_top = jnp.max(logits, axis=-1, keepdims=True)
    row_expo = jnp.exp(logits - row_top)
    row_total = jnp.sum(row_expo, axis=-1, keepdims=True)
    weights = (row_expo / row_total).astype(jnp.bfloat16)
    head_mixed = jnp.einsum("hqk,khe->qhe", weights, value_proj, preferred_element_type=jnp.float32)
    return (head_mixed.astype(jnp.bfloat16), (row_top + jnp.log(row_total))[..., 0])


def attend_back(operands):
    queries, key_proj, value_proj, mixed_grad, row_lse = operands
    score_scale = queries.shape[-1] ** (-0.5)
    logits = masked_scores(queries, key_proj)
    probs = jnp.exp(logits - row_lse[..., None])
    value_grad = jnp.einsum(
        "hqk,qhe->khe", probs.astype(jnp.bfloat16), mixed_grad, preferred_element_type=jnp.float32
    )
    prob_grad = jnp.einsum(
        "qhe,khe->hqk", mixed_grad, value_proj, preferred_element_type=jnp.float32
    )
    score_grad = probs * (prob_grad - jnp.sum(probs * prob_grad, axis=-1, keepdims=True))
    score_grad = score_grad.astype(jnp.bfloat16)
    query_grad = (
        jnp.einsum("hqk,khe->qhe", score_grad, key_proj, preferred_element_type=jnp.float32)
        * score_scale
    )
    key_grad = (
        jnp.einsum("hqk,qhe->khe", score_grad, queries, preferred_element_type=jnp.float32)
        * score_scale
    )
    return (
        query_grad.astype(jnp.bfloat16),
        key_grad.astype(jnp.bfloat16),
        value_grad.astype(jnp.bfloat16),
    )


def split_heads(
    block_input,
    image_mask,
    w_qkv,
    b_qv,
    w_out,
    b_out,
    w_fc1,
    b_fc1,
    w_fc2,
    b_fc2,
    ln1_gain,
    ln1_bias,
    ln2_gain,
    ln2_bias,
    grad_out,
):
    local_rows = block_input.shape[0]
    model_width = block_input.shape[1]
    image_count = image_mask.shape[0]
    head_dim = model_width // HEADS
    local_width = w_qkv.shape[2]
    local_heads = local_width // head_dim
    tensor_index = lax.axis_index("tensor")
    token_index = tensor_index * local_rows + jnp.arange(local_rows)
    image_of = token_index // SEQ
    position = token_index % SEQ
    image_pick = (image_of[:, None] == jnp.arange(image_count)[None, :]).astype(jnp.float32)
    token_keep = jnp.sum(image_pick * image_mask.astype(jnp.float32)[None, :], axis=1)
    token_keep = token_keep * (position < VALID).astype(jnp.float32)
    contract_rows = (((0,), (0,)), ((), ()))
    contract_cols = (((1,), (1,)), ((), ()))
    full_qkv, full_out, full_fc1, full_fc2 = (
        lax.all_gather(w_qkv, "dp", axis=1, tiled=True),
        lax.all_gather(w_out, "dp", axis=1, tiled=True),
        lax.all_gather(w_fc1, "dp", axis=0, tiled=True),
        lax.all_gather(w_fc2, "dp", axis=1, tiled=True),
    )
    input_float = block_input.astype(jnp.float32)
    normed_one = normalize(input_float, ln1_gain, ln1_bias).astype(jnp.bfloat16)
    inputs_one = lax.all_gather(normed_one, "tensor", axis=0, tiled=True)
    group_rows = inputs_one.shape[0]
    projected = jnp.einsum("td,cde->cte", inputs_one, full_qkv, preferred_element_type=jnp.float32)
    queries = (projected[0] + b_qv[0]).astype(jnp.bfloat16)
    key_proj = projected[1].astype(jnp.bfloat16)
    value_proj = (projected[2] + b_qv[1]).astype(jnp.bfloat16)
    head_shape = (group_rows // SEQ, SEQ, local_heads, head_dim)
    query_heads = queries.reshape(head_shape)
    key_heads = key_proj.reshape(head_shape)
    value_heads = value_proj.reshape(head_shape)
    head_mixed, row_lse = lax.map(attend_image, (query_heads, key_heads, value_heads))
    head_mixed = head_mixed.reshape(group_rows, local_width)
    row_block = head_mixed
    attn_sum = lax.psum_scatter(
        jnp.dot(row_block, full_out, preferred_element_type=jnp.float32),
        "tensor",
        scatter_dimension=0,
        tiled=True,
    )
    resid = input_float + (attn_sum + b_out)
    normed_two = normalize(resid, ln2_gain, ln2_bias).astype(jnp.bfloat16)
    inputs_two = lax.all_gather(normed_two, "tensor", axis=0, tiled=True)
    hidden_pre = jnp.dot(inputs_two, full_fc1, preferred_element_type=jnp.float32) + b_fc1
    hidden = gelu_exact(hidden_pre).astype(jnp.bfloat16)
    row_block = hidden
    mlp_sum = lax.psum_scatter(
        jnp.dot(row_block, full_fc2, preferred_element_type=jnp.float32).astype(jnp.bfloat16),
        "tensor",
        scatter_dimension=0,
        tiled=True,
    ).astype(jnp.float32)
    layer_output = ((resid + (mlp_sum + b_fc2)) * token_keep[:, None]).astype(jnp.bfloat16)
    cot_rows = grad_out * token_keep.astype(jnp.bfloat16)[:, None]
    cot_float = cot_rows.astype(jnp.float32)
    cot_group = lax.all_gather(cot_rows, "tensor", axis=0, tiled=True)
    fc2_grad_group = lax.dot_general(
        hidden, cot_group, contract_rows, preferred_element_type=jnp.float32
    )
    hidden_grad = lax.dot_general(
        cot_group, full_fc2, contract_cols, preferred_element_type=jnp.float32
    )
    gelu_value, gelu_back = jax.vjp(gelu_exact, hidden_pre)
    pre_grad = gelu_back(hidden_grad)[0].astype(jnp.bfloat16)
    fc1_bias_grad = jnp.sum(pre_grad, axis=0, dtype=jnp.float32)
    fc1_grad_group = lax.dot_general(
        inputs_two, pre_grad, contract_rows, preferred_element_type=jnp.float32
    )
    row_block = pre_grad
    normed_two_grad = lax.psum_scatter(
        lax.dot_general(row_block, full_fc1, contract_cols, preferred_element_type=jnp.float32),
        "tensor",
        scatter_dimension=0,
        tiled=True,
    )
    norm_two_value, norm_two_back = jax.vjp(normalize, resid, ln2_gain, ln2_bias)
    resid_back, gain_two_grad, bias_two_grad = norm_two_back(normed_two_grad)
    resid_grad = cot_float + resid_back
    out_bias_grad = jnp.sum(resid_grad, axis=0)
    fc2_bias_grad = jnp.sum(cot_float, axis=0)
    resid_low = resid_grad.astype(jnp.bfloat16)
    resid_group = lax.all_gather(resid_low, "tensor", axis=0, tiled=True)
    out_grad_group = lax.dot_general(
        head_mixed, resid_group, contract_rows, preferred_element_type=jnp.float32
    )
    mixed_grad = lax.dot_general(
        resid_group, full_out, contract_cols, preferred_element_type=jnp.float32
    ).astype(jnp.bfloat16)
    query_grad, key_grad, value_grad = lax.map(
        attend_back, (query_heads, key_heads, value_heads, mixed_grad.reshape(head_shape), row_lse)
    )
    stacked_grads = jnp.stack(
        [
            query_grad.reshape(group_rows, local_width),
            key_grad.reshape(group_rows, local_width),
            value_grad.reshape(group_rows, local_width),
        ]
    )
    qkv_grad_group = jnp.einsum(
        "td,cte->cde", inputs_one, stacked_grads, preferred_element_type=jnp.float32
    )
    qv_bias_grad = jnp.stack(
        [
            jnp.sum(stacked_grads[0], axis=0, dtype=jnp.float32),
            jnp.sum(stacked_grads[2], axis=0, dtype=jnp.float32),
        ]
    )
    row_block = stacked_grads
    normed_one_grad = lax.psum_scatter(
        jnp.einsum("cte,cde->td", row_block, full_qkv, preferred_element_type=jnp.float32),
        "tensor",
        scatter_dimension=0,
        tiled=True,
    )
    norm_one_value, norm_one_back = jax.vjp(normalize, input_float, ln1_gain, ln1_bias)
    input_back, gain_one_grad, bias_one_grad = norm_one_back(normed_one_grad)
    input_grad = (resid_grad + input_back).astype(jnp.bfloat16)
    grad_w_qkv, grad_w_out, grad_w_fc1, grad_w_fc2 = (
        lax.psum_scatter(qkv_grad_group, "dp", scatter_dimension=1, tiled=True),
        lax.psum_scatter(out_grad_group, "dp", scatter_dimension=1, tiled=True),
        lax.psum_scatter(fc1_grad_group, "dp", scatter_dimension=0, tiled=True),
        lax.psum_scatter(fc2_grad_group, "dp", scatter_dimension=1, tiled=True),
    )
    vector_sums = lax.psum(
        (gain_one_grad, bias_one_grad, gain_two_grad, bias_two_grad, out_bias_grad, fc2_bias_grad),
        ("dp", "tensor"),
    )
    qv_sum, fc1_sum = lax.psum((qv_bias_grad, fc1_bias_grad), "dp")
    return (
        layer_output,
        input_grad,
        grad_w_qkv,
        qv_sum,
        grad_w_out,
        vector_sums[4],
        grad_w_fc1,
        fc1_sum,
        grad_w_fc2,
        vector_sums[5],
        vector_sums[0],
        vector_sums[1],
        vector_sums[2],
        vector_sums[3],
    )


BIT_X, BIT_CORE, BIT_Y, BIT_Z_LOW, BIT_Z_HIGH = 1, 2, 4, 8, 16
AXES = ("dp", "tensor")


def exchange(block, bit):
    return lax.ppermute(block, AXES, [(src, src ^ bit) for src in range(32)])


def leaves(deps):
    return jax.tree.leaves(deps)


ANYWHERE = pl.BlockSpec(memory_space=pl.ANY)
VMEM = pl.BlockSpec(memory_space=pltpu.VMEM)
FREE = pl.CostEstimate(flops=2 * 10**8, bytes_accessed=1, transcendentals=0)
STEP = pl.CostEstimate(flops=10**10, bytes_accessed=1, transcendentals=0)


def after(value, *deps):
    deps = leaves(deps)
    return pl.pallas_call(
        lambda *refs: None,
        in_specs=[ANYWHERE] * (1 + len(deps)),
        out_specs=ANYWHERE,
        out_shape=jax.ShapeDtypeStruct(value.shape, value.dtype),
        input_output_aliases={0: 0},
        compiler_params=pltpu.CompilerParams(vmem_limit_bytes=1 << 20),
    )(value, *deps)


def one_after(*deps):
    deps = leaves(deps)

    def kernel(*refs):
        refs[-1][...] = jnp.ones_like(refs[-1])

    return pl.pallas_call(
        kernel,
        in_specs=[ANYWHERE] * len(deps),
        out_shape=jax.ShapeDtypeStruct((1, 128), jnp.float32),
        compiler_params=pltpu.CompilerParams(vmem_limit_bytes=1 << 20),
    )(*deps)[0, 0]


def place_blocks(arrays, shapes, moves, deps=(), cost=None):
    deps = leaves(deps)

    def kernel(*refs):
        outs, sem = refs[len(arrays) + len(deps) : -1], refs[-1]
        copies = [
            pltpu.make_async_copy(refs[src].at[at], outs[dst].at[to], sem.at[i])
            for i, (src, at, dst, to) in enumerate(moves)
        ]
        for copy in copies:
            copy.start()
        for copy in copies:
            copy.wait()

    size = 4 * sum(v.size for v in arrays)
    return pl.pallas_call(
        kernel,
        in_specs=[ANYWHERE] * (len(arrays) + len(deps)),
        out_specs=[ANYWHERE] * len(shapes),
        out_shape=[jax.ShapeDtypeStruct(shape, jnp.bfloat16) for shape in shapes],
        scratch_shapes=[pltpu.SemaphoreType.DMA((len(moves),))],
        compiler_params=pltpu.CompilerParams(vmem_limit_bytes=1 << 20),
        cost_estimate=cost or STEP,
    )(*arrays, *deps)


class Gather:
    def __init__(self, shard, *deps):
        self.columns = shard.shape[1]
        self.shard = place_blocks([shard], [shard.shape], [(0, ..., 0, ...)], deps, FREE)[0] if deps else shard
        self.moving = exchange(self.shard, BIT_Z_HIGH)

    def step_one(self, *deps):
        rows = self.shard.shape[0]
        moves = [(got, ..., 0, slice(got * rows, got * rows + rows)) for got in range(2)]
        (self.block,) = place_blocks([self.shard, self.moving], [(2 * rows, self.columns)], moves, deps)
        self.moving = exchange(self.block, BIT_Z_LOW)
        return self.block

    def step_two(self, *deps):
        half = self.columns // 2
        moves = []
        for got in range(2):
            for part in range(2):
                columns = slice(part * half, part * half + half)
                moves.append((got, (slice(None), columns), part, slice(got * 128, got * 128 + 128)))
        self.blocks = place_blocks([self.block, self.moving], [(256, half)] * 2, moves, deps)
        self.moving = [exchange(self.blocks[0], BIT_X), exchange(self.blocks[1], BIT_Y)]
        return self.blocks

    def step_three(self, *deps):
        half = self.columns // 2
        moves = [(2 * got + part, ..., part, got) for got in range(2) for part in range(2)]
        self.blocks = place_blocks([*self.blocks, *self.moving], [(2, 256, half)] * 2, moves, deps)
        self.moving = [exchange(self.blocks[0], BIT_Y), exchange(self.blocks[1], BIT_X)]
        return self.blocks

    def step_four(self, *deps):
        half = self.columns // 2
        moves = []
        for got, part, lead in [(j, k, m) for j in range(2) for k in range(2) for m in range(2)]:
            side, y = (lead, got) if part == 0 else (got, lead)
            column = side * self.columns + part * half
            moves.append((2 * got + part, lead, 0, (slice(y * 256, y * 256 + 256), slice(column, column + half))))
        (self.block,) = place_blocks([*self.blocks, *self.moving], [(512, 2 * self.columns)], moves, deps)
        self.moving = exchange(self.block, BIT_CORE)
        return self.block

    def finish(self, *deps):
        moves = [(got, ..., 0, slice(got * 512, got * 512 + 512)) for got in range(2)]
        return place_blocks([self.block, self.moving], [(1024, 2 * self.columns)], moves, deps, FREE)[0]


def relative_weights(gathered, ranges, *deps):
    deps = leaves(deps)

    def kernel(*refs):
        source, outs, sem = refs[0], refs[1 + len(deps) : -1], refs[-1]
        device = lax.axis_index("dp") * 2 + lax.axis_index("tensor")
        copies = []
        for row in range(16):
            for side in range(2):
                apart = side + 2 * (row // 8) + 4 * (row // 4 % 2) + 8 * (row // 2 % 2) + 16 * (row % 2)
                for out, (lo, hi) in zip(outs, ranges):
                    width = hi - lo
                    copies.append(
                        pltpu.make_async_copy(
                            source.at[device ^ apart, :, lo:hi],
                            out.at[row * 64 : row * 64 + 64, side * width : side * width + width],
                            sem.at[len(copies)],
                        )
                    )
        for copy in copies:
            copy.start()
        for copy in copies:
            copy.wait()

    return pl.pallas_call(
        kernel,
        in_specs=[ANYWHERE] * (1 + len(deps)),
        out_specs=[pl.BlockSpec(memory_space=pltpu.VMEM)] * len(ranges),
        out_shape=[jax.ShapeDtypeStruct((1024, 2 * (hi - lo)), jnp.bfloat16) for lo, hi in ranges],
        scratch_shapes=[pltpu.SemaphoreType.DMA((32 * len(ranges),))],
        compiler_params=pltpu.CompilerParams(vmem_limit_bytes=44 << 20),
        cost_estimate=FREE,
    )(gathered, *deps)


def hidden_grads(cot, gathered, first, slope, *deps):
    deps = leaves(deps)
    width = slope.shape[1] // 2

    def kernel(cot_ref, slope_ref, source, *refs):
        out_ref, weights_ref, sem = refs[-3:]
        device = lax.axis_index("dp") * 2 + lax.axis_index("tensor")
        copies = [[], []]
        for side in range(2):
            for row in range(16):
                apart = side + 2 * (row // 8) + 4 * (row // 4 % 2) + 8 * (row // 2 % 2) + 16 * (row % 2)
                copies[side].append(
                    pltpu.make_async_copy(
                        source.at[device ^ apart, :, first : first + width],
                        weights_ref.at[row * 64 : row * 64 + 64, side * width : side * width + width],
                        sem.at[side * 16 + row],
                    )
                )
                copies[side][-1].start()
        for side in range(2):
            for copy in copies[side]:
                copy.wait()
            for block in range(2):
                columns = slice(side * width + block * width // 2, side * width + (block + 1) * width // 2)
                product = jnp.dot(cot_ref[...], weights_ref[:, columns], preferred_element_type=jnp.float32)
                out_ref[:, columns] = (product * slope_ref[:, columns].astype(jnp.float32)).astype(jnp.bfloat16)

    return pl.pallas_call(
        kernel,
        in_specs=[VMEM, VMEM] + [ANYWHERE] * (1 + len(deps)),
        out_specs=[VMEM, VMEM],
        out_shape=[
            jax.ShapeDtypeStruct(slope.shape, jnp.bfloat16),
            jax.ShapeDtypeStruct((1024, slope.shape[1]), jnp.bfloat16),
        ],
        scratch_shapes=[pltpu.SemaphoreType.DMA((32,))],
        compiler_params=pltpu.CompilerParams(vmem_limit_bytes=40 << 20),
        cost_estimate=FREE,
    )(cot, slope, gathered, *deps)


def weight_grads(left, right, keep, *deps):
    deps = leaves(deps)
    columns = right.shape[1]
    width = columns // (4 if columns > 2048 else 2)

    def kernel(left_ref, right_ref, *refs):
        out_ref = refs[-1]
        part = left_ref[:, :512] if keep else left_ref[:, 512:]

        @pl.loop(0, columns // width)
        def _(block):
            at = pl.ds(pl.multiple_of(block * width, width), width)
            product = lax.dot_general(
                part, right_ref[:, at], (((0,), (0,)), ((), ())), preferred_element_type=jnp.float32
            )
            out_ref[:, at] = product.astype(jnp.bfloat16)

    return pl.pallas_call(
        kernel,
        in_specs=[VMEM, VMEM] + [ANYWHERE] * len(deps),
        out_specs=VMEM,
        out_shape=jax.ShapeDtypeStruct((512, columns), jnp.bfloat16),
        compiler_params=pltpu.CompilerParams(vmem_limit_bytes=20 << 20),
        cost_estimate=FREE,
    )(left, right, *deps)


def back_through(grads, weights, *deps):
    deps = leaves(deps)
    width = 512

    def kernel(grads_ref, weights_ref, *refs):
        out_ref = refs[-1]
        for block in range(1024 // width):
            at = slice(block * width, block * width + width)
            out_ref[:, at] = lax.dot_general(
                grads_ref[...], weights_ref[at], (((1,), (1,)), ((), ())), preferred_element_type=jnp.float32
            )

    return pl.pallas_call(
        kernel,
        in_specs=[VMEM, VMEM] + [ANYWHERE] * len(deps),
        out_specs=VMEM,
        out_shape=jax.ShapeDtypeStruct((grads.shape[0], 1024), jnp.float32),
        compiler_params=pltpu.CompilerParams(vmem_limit_bytes=24 << 20),
        cost_estimate=FREE,
    )(grads, weights, *deps)


class Scatter:
    def __init__(self, pieces):
        width, moves = 0, []
        for i, piece in enumerate(pieces):
            moves.append((i, ..., 0, (slice(None), slice(width, width + piece.shape[1]))))
            width += piece.shape[1]
        self.sent = place_blocks(pieces, [(512, width)], moves, (), FREE)[0] if len(pieces) > 1 else pieces[0]
        self.got = exchange(self.sent, BIT_CORE)

    def call(self, kernel, ins, deps, shapes, dtype=jnp.bfloat16):
        deps = leaves(deps)
        outs = [jax.ShapeDtypeStruct(shape, dtype) for shape in shapes]
        size = 2 * sum(v.size for v in ins) + dtype(0).nbytes * sum(v.size for v in outs)
        count = len(ins)
        return pl.pallas_call(
            lambda *refs: kernel(refs[:count], refs[count + len(deps) :]),
            in_specs=[pl.BlockSpec(memory_space=pltpu.VMEM)] * count + [ANYWHERE] * len(deps),
            out_specs=[pl.BlockSpec(memory_space=pltpu.VMEM)] * len(outs),
            out_shape=outs,
            compiler_params=pltpu.CompilerParams(vmem_limit_bytes=size + (2 << 20)),
            cost_estimate=STEP,
        )(*ins, *deps)

    def step_one(self, pieces, *deps):
        widths = [piece.shape[1] // 2 for piece in pieces]
        self.columns = sum(widths)
        half = self.columns // 2

        def kernel(ins, outs):
            first = 0
            for i, width in enumerate(widths):
                for part in range(2):
                    start, stop = max(first, part * half), min(first + width, part * half + half)
                    if start >= stop:
                        continue
                    to = slice(start - part * half, stop - part * half)
                    for side in range(2):
                        columns = slice(side * width + start - first, side * width + stop - first)
                        came = slice(2 * first + columns.start, 2 * first + columns.stop)
                        for y in range(2):
                            rows = slice(y * 256, y * 256 + 256)
                            lead, send = (side, y) if part == 0 else (y, side)
                            value = ins[i][rows, columns] + ins[-1][rows, came]
                            outs[2 * part + send][lead, :, to] = value
                first += width

        outs = self.call(kernel, [*pieces, self.got], deps, [(2, 256, half)] * 4)
        self.kept = outs[0::2]
        self.moving = [exchange(outs[1], BIT_Y), exchange(outs[3], BIT_X)]
        return outs

    def step_two(self, *deps):
        half = self.columns // 2

        def kernel(ins, outs):
            for part in range(2):
                for send in range(2):
                    outs[2 * part + send][...] = ins[part][send] + ins[2 + part][send]

        outs = self.call(kernel, [*self.kept, *self.moving], deps, [(256, half)] * 4)
        self.kept = outs[0::2]
        self.moving = [exchange(outs[1], BIT_X), exchange(outs[3], BIT_Y)]
        return outs

    def step_three(self, *deps):
        half = self.columns // 2

        def kernel(ins, outs):
            for part in range(2):
                for send in range(2):
                    rows = slice(send * 128, send * 128 + 128)
                    outs[send][:, part * half : part * half + half] = ins[part][rows] + ins[2 + part][rows]

        outs = self.call(kernel, [*self.kept, *self.moving], deps, [(128, self.columns)] * 2)
        self.kept, self.moving = outs[0], exchange(outs[1], BIT_Z_LOW)
        return outs

    def step_four(self, *deps):
        def kernel(ins, outs):
            for send in range(2):
                rows = slice(send * 64, send * 64 + 64)
                outs[send][...] = ins[0][rows] + ins[1][rows]

        outs = self.call(kernel, [self.kept, self.moving], deps, [(64, self.columns)] * 2)
        self.kept, self.moving = outs[0], exchange(outs[1], BIT_Z_HIGH)
        return outs

    def finish(self, *deps):
        def kernel(ins, outs):
            outs[0][...] = ins[0][...].astype(jnp.float32) + ins[1][...].astype(jnp.float32)

        return self.call(kernel, [self.kept, self.moving], deps, [(64, self.columns)], jnp.float32)[0]


def place_matrix():
    relative = lax.broadcasted_iota(jnp.int32, (1024, 1024), 1)
    feature = lax.broadcasted_iota(jnp.int32, (1024, 1024), 0)
    block = relative // 64
    shard = (block // 8) + 2 * (block // 4 % 2) + 4 * (block // 2 % 2) + 8 * (block % 2)
    shard = shard ^ lax.axis_index("dp")
    return (feature == shard * 64 + relative % 64).astype(jnp.bfloat16)


def attend_kernel(q_ref, k_ref, v_ref, *refs):
    o_ref, lse_ref = refs[-2:]
    queries, keys, values = q_ref[...], k_ref[...], v_ref[...]
    queries = queries * jnp.bfloat16(0.125)
    lane = lax.broadcasted_iota(jnp.int32, keys.shape, 1)
    mixed = []
    for head in range(2):
        own = (lane // 64) == head
        scores = lax.dot_general(
            jnp.where(own, keys, 0), queries, (((1,), (1,)), ((), ())), preferred_element_type=jnp.float32
        )
        valid = lax.broadcasted_iota(jnp.int32, scores.shape, 0) < VALID
        scores = jnp.where(valid, scores, masked_score)
        top = jnp.max(scores, axis=0, keepdims=True)
        expo = jnp.exp(scores - top)
        norm = jnp.sum(expo, axis=0, keepdims=True)
        out = lax.dot_general(
            values, expo.astype(jnp.bfloat16), (((0,), (0,)), ((), ())), preferred_element_type=jnp.float32
        )
        mixed.append(out[head * 64 : head * 64 + 64] / norm)
        lse_ref[0, head : head + 1, :] = top + jnp.log(norm)
    o_ref[...] = jnp.concatenate(mixed, axis=0).T.astype(jnp.bfloat16)


def head_specs():
    return [pl.BlockSpec((SEQ, 128), lambda image, pair, c=c: (image, pair // 2 * 6 + 2 * c + pair % 2)) for c in range(3)]


def mixed_spec(half):
    return pl.BlockSpec((SEQ, 128), lambda image, pair: (image, pair // 2 * 4 + 2 * half + pair % 2))


def attend_pairs(projected, half, mixed, *deps):
    deps = ([] if mixed is None else [mixed]) + leaves(deps)
    rows = projected.shape[0]
    images = rows // SEQ
    return pl.pallas_call(
        attend_kernel,
        grid=(images, 4),
        in_specs=head_specs() + [ANYWHERE] * len(deps),
        out_specs=[
            mixed_spec(half),
            pl.BlockSpec((1, 2, SEQ), lambda image, pair: (image * 4 + pair, 0, 0)),
        ],
        out_shape=[
            jax.ShapeDtypeStruct((rows, 1024), jnp.bfloat16),
            jax.ShapeDtypeStruct((images * 4, 2, SEQ), jnp.float32),
        ],
        input_output_aliases={} if mixed is None else {3: 0},
        compiler_params=pltpu.CompilerParams(vmem_limit_bytes=24 << 20),
        cost_estimate=FREE,
    )(projected, projected, projected, *deps)


def attend_back_kernel(q_ref, k_ref, v_ref, do_ref, lse_ref, *refs):
    out_ref = refs[-1]
    queries, keys, values, mixed_grad = q_ref[...], k_ref[...], v_ref[...], do_ref[...]
    queries = queries * jnp.bfloat16(0.125)
    lane = lax.broadcasted_iota(jnp.int32, keys.shape, 1)
    dq, dk, dv = [], [], []
    for head in range(2):
        own = (lane // 64) == head
        scores = lax.dot_general(
            jnp.where(own, keys, 0), queries, (((1,), (1,)), ((), ())), preferred_element_type=jnp.float32
        )
        valid = lax.broadcasted_iota(jnp.int32, scores.shape, 0) < VALID
        probs = jnp.where(valid, jnp.exp(scores - lse_ref[0, head : head + 1, :]), 0)
        dv.append(jnp.dot(probs.astype(jnp.bfloat16), mixed_grad, preferred_element_type=jnp.float32))
        back = lax.dot_general(
            jnp.where(own, values, 0), mixed_grad, (((1,), (1,)), ((), ())), preferred_element_type=jnp.float32
        )
        row = jnp.sum(probs * back, axis=0, keepdims=True)
        score_grad = (probs * (back - row)).astype(jnp.bfloat16)
        dk.append(jnp.dot(score_grad, queries, preferred_element_type=jnp.float32))
        out = lax.dot_general(
            keys, score_grad, (((0,), (0,)), ((), ())), preferred_element_type=jnp.float32
        )
        dq.append(out[head * 64 : head * 64 + 64] * 0.125)
    low = lane < 64
    results = (
        jnp.concatenate(dq, axis=0).T.astype(jnp.bfloat16),
        jnp.where(low, dk[0], dk[1]).astype(jnp.bfloat16),
        jnp.where(low, dv[0], dv[1]).astype(jnp.bfloat16),
    )
    pair = pl.program_id(1)
    for c, result in enumerate(results):
        column = (pair // 2 * 6 + 2 * c + pair % 2) * 128
        out_ref[:, pl.ds(pl.multiple_of(column, 128), 128)] = result


def attend_back_pairs(projected, mixed_grad, lse, half, *deps):
    deps = leaves(deps)
    rows = projected.shape[0]
    images = rows // SEQ
    return pl.pallas_call(
        attend_back_kernel,
        grid=(images, 4),
        in_specs=head_specs()
        + [
            mixed_spec(half),
            pl.BlockSpec((1, 2, SEQ), lambda image, pair: (image * 4 + pair, 0, 0)),
        ]
        + [ANYWHERE] * len(deps),
        out_specs=pl.BlockSpec((SEQ, 1536), lambda image, pair: (image, 0)),
        out_shape=jax.ShapeDtypeStruct((rows, 1536), jnp.bfloat16),
        compiler_params=pltpu.CompilerParams(vmem_limit_bytes=32 << 20),
        cost_estimate=FREE,
    )(projected, projected, projected, mixed_grad, lse, *deps)


def own_images(
    block_input,
    image_mask,
    w_qkv,
    b_qv,
    w_out,
    b_out,
    w_fc1,
    b_fc1,
    w_fc2,
    b_fc2,
    ln1_gain,
    ln1_bias,
    ln2_gain,
    ln2_bias,
    grad_out,
):
    f32, low = jnp.float32, jnp.bfloat16
    both = range(2)
    rows = block_input.shape[0]
    tensor_index = lax.axis_index("tensor")
    token_index = tensor_index * rows + jnp.arange(rows)
    image_pick = ((token_index // SEQ)[:, None] == jnp.arange(image_mask.shape[0])[None, :]).astype(f32)
    token_keep = jnp.sum(image_pick * image_mask.astype(f32)[None, :], axis=1)
    token_keep = token_keep * (token_index % SEQ < VALID).astype(f32)

    def rows_of(left, right):
        return lax.dot_general(left, right, (((0,), (0,)), ((), ())), preferred_element_type=f32)

    def cols_of(left, right):
        return lax.dot_general(left, right, (((1,), (1,)), ((), ())), preferred_element_type=f32)

    def dot(left, right):
        return jnp.dot(left, right, preferred_element_type=f32)

    def qkv_columns(half):
        part = slice(half * 256, half * 256 + 256)
        return jnp.concatenate([w_qkv[0][:, part], w_qkv[1][:, part], w_qkv[2][:, part]], axis=1)

    bias_own = jnp.concatenate([b_qv.reshape(-1), b_fc1])[None, :]
    bias_sides = jnp.concatenate([bias_own, exchange(bias_own, BIT_X)], axis=0)
    qkv = [Gather(qkv_columns(0))]
    gathered = lax.all_gather(jnp.concatenate([w_fc1, w_fc2.T], axis=1), AXES, axis=0, tiled=False)

    place = place_matrix()
    vectors = jnp.stack([b_out, b_fc2, ln1_gain, ln1_bias, ln2_gain, ln2_bias])
    vectors = jnp.dot(vectors, place.astype(f32), precision=lax.Precision.HIGHEST)
    b_out, b_fc2, ln1_gain, ln1_bias, ln2_gain, ln2_bias = vectors
    signal = dot(block_input, place)
    cot_low = dot(grad_out * token_keep.astype(low)[:, None], place).astype(low)
    cot = cot_low.astype(f32)
    normed_one = normalize(signal, ln1_gain, ln1_bias).astype(low)

    go = qkv[0].step_one(bias_sides)
    qkv.append(Gather(qkv_columns(1), go))
    go = qkv[0].step_two(qkv[1].shard, normed_one, cot_low, b_fc2)
    go = qkv[1].step_one(go)
    go = qkv[0].step_three(go)
    go = qkv[1].step_two(go)
    out = Gather(w_out.T, go)
    go = qkv[0].step_four(out.shard)
    w_heads, projected, lse = [], [], []

    def project(half, *deps):
        part = slice(half * 256, half * 256 + 256)
        w_heads.append(qkv[half].finish(*deps))
        bias = jnp.concatenate(
            [jnp.concatenate([b[:512][part], jnp.zeros((256,), f32), b[512:1024][part]]) for b in bias_sides]
        )
        projected.append((dot(normed_one, w_heads[half]) + bias).astype(low))
        return projected[half]

    go = project(0, go)
    go = qkv[1].step_three(go)
    go = out.step_one(go)
    mixed, lse_half = attend_pairs(projected[0], 0, None, go)
    lse.append(lse_half)
    go = qkv[1].step_four(mixed)
    go = project(1, go)
    go = out.step_two(go)
    mixed, lse_half = attend_pairs(projected[1], 1, mixed, go)
    lse.append(lse_half)
    go = out.step_three(mixed)
    go = out.step_four(go)
    w_mix = out.finish(go)
    attn = cols_of(mixed, w_mix)
    resid = signal + (attn + b_out)
    normed_two = normalize(resid, ln2_gain, ln2_bias).astype(low)
    (w_one,) = relative_weights(gathered, [(0, 2048)], normed_two)
    pre = dot(normed_two, w_one) + jnp.concatenate([b[1024:] for b in bias_sides])
    phi = 0.5 * (1.0 + lax.erf(pre * (0.5**0.5)))
    hidden = (pre * phi).astype(low)
    slope = (phi + pre * (jnp.exp(-0.5 * pre * pre) * (0.5 / 3.141592653589793) ** 0.5)).astype(low)

    fc2_far = weight_grads(cot_low, hidden, False)
    fc2_sum = Scatter([fc2_far])
    go = fc2_sum.step_one([weight_grads(cot_low, hidden, True, fc2_far)])
    pre_grad, w_two = hidden_grads(cot_low, gathered, 2048, slope, go)
    fc1_far = weight_grads(normed_two, pre_grad, False)
    go = fc2_sum.step_two(fc1_far)
    fc1_sum = Scatter([after(fc1_far, go)])
    normed_two_grad = back_through(pre_grad, w_one, go)
    fc1_near = weight_grads(normed_two, pre_grad, True, normed_two_grad)
    go = fc1_sum.step_one([fc1_near])
    go = fc2_sum.step_three(go)
    fc1_bias_grad = rows_of(jnp.ones((rows, 8), low), pre_grad)[0]
    _, norm_two_back = jax.vjp(normalize, resid, ln2_gain, ln2_bias)
    resid_back, gain_two_grad, bias_two_grad = norm_two_back(after(normed_two_grad, go))
    resid_grad = cot + resid_back
    resid_low = resid_grad.astype(low)
    mixed_grad = dot(resid_low, w_mix).astype(low)
    head_grads = [attend_back_pairs(projected[0], mixed_grad, lse[0], 0, fc1_bias_grad)]
    go = fc2_sum.step_four(head_grads)
    go = fc1_sum.step_two(go)

    def first_pieces(keep, go):
        heads_part = weight_grads(normed_one, head_grads[0], keep, go)
        return [heads_part, weight_grads(resid_low, mixed, keep, heads_part)]

    heads_sum = [Scatter(first_pieces(False, go))]
    go = heads_sum[0].step_one(first_pieces(True, heads_sum[0].sent))
    head_grads.append(attend_back_pairs(projected[1], mixed_grad, lse[1], 1, go))
    fc2_grad = fc2_sum.finish(head_grads[1])
    go = fc1_sum.step_three(fc2_grad)
    heads_far = weight_grads(normed_one, head_grads[1], False, go)
    heads_sum.append(Scatter([heads_far]))
    heads_near = weight_grads(normed_one, head_grads[1], True, heads_far)
    go = heads_sum[0].step_two(heads_near)
    go = heads_sum[1].step_one([heads_near], go)
    normed_one_grad = sum(
        cols_of(head_grads[half], w_heads[half]) * one_after(go) for half in both
    )
    go = fc1_sum.step_four(normed_one_grad)
    go = heads_sum[0].step_three(go)
    go = heads_sum[1].step_two(go)
    _, norm_one_back = jax.vjp(normalize, signal, ln1_gain, ln1_bias)
    input_back, gain_one_grad, bias_one_grad = norm_one_back(after(normed_one_grad, go))
    sums = jnp.stack(
        [
            gain_one_grad,
            bias_one_grad,
            gain_two_grad,
            bias_two_grad,
            jnp.sum(resid_grad, axis=0),
            jnp.sum(cot, axis=0),
        ]
    )
    sums = lax.dot_general(
        sums, place.astype(f32), (((1,), (1,)), ((), ())), precision=lax.Precision.HIGHEST
    ).reshape(1, 6144)
    head_sums = [jnp.sum(head_grads[half], axis=0, dtype=f32).reshape(2, 3, 256) for half in both]
    side_sums = jnp.concatenate(
        [head_sums[half][:, c] for c in (0, 2) for half in both] + [fc1_bias_grad.reshape(2, 2048)], axis=1
    )
    own, other = [jnp.concatenate([sums, side_sums[side : side + 1]], axis=1) for side in both]
    sums = own + exchange(other, BIT_X)
    input_grad = cols_of((resid_grad + input_back).astype(low), place).astype(low)
    go = heads_sum[0].step_four(input_grad)
    go = heads_sum[1].step_three(go)
    sums = sums + after(exchange(sums, BIT_CORE), go)
    mlp = cols_of(hidden, w_two) * one_after(go)
    go = heads_sum[1].step_four(mlp)
    sums = sums + after(exchange(sums, BIT_Y), go)
    layer_output = ((resid + (after(mlp, go) + b_fc2)) * token_keep[:, None]).astype(low)
    layer_output = cols_of(layer_output, place).astype(low)
    sums = sums + after(exchange(sums, BIT_Z_LOW), layer_output)
    sums = sums + exchange(sums, BIT_Z_HIGH)
    sums, side_sums = sums[0, :6144].reshape(6, 1024), sums[0, 6144:]
    fc1_grad = fc1_sum.finish(input_grad)
    heads_grad = [h.finish(layer_output) for h in heads_sum]
    qkv_grad = jnp.concatenate([g[:, :768].reshape(64, 3, 256) for g in heads_grad], axis=2)
    return (
        layer_output,
        input_grad,
        qkv_grad.transpose(1, 0, 2),
        side_sums[:1024].reshape(2, 512),
        heads_grad[0][:, 768:].T,
        sums[4],
        fc1_grad,
        side_sums[1024:],
        fc2_grad.T,
        sums[5],
        sums[0],
        sums[1],
        sums[2],
        sums[3],
    )


def solution(mesh):
    def plan(block_input, *others):
        whole_images = block_input.shape[0] % SEQ == 0
        if whole_images and mesh.shape["dp"] == 16 and mesh.shape["tensor"] == 2:
            return own_images(block_input, *others)
        return split_heads(block_input, *others)

    return jax.shard_map(
        plan,
        mesh=mesh,
        in_specs=(
            P(("dp", "tensor"), None),
            P("dp"),
            P(None, "dp", "tensor"),
            P(None, "tensor"),
            P("tensor", "dp"),
            P(),
            P("dp", "tensor"),
            P("tensor"),
            P("tensor", "dp"),
            P(),
            P(),
            P(),
            P(),
            P(),
            P(("dp", "tensor"), None),
        ),
        out_specs=(
            P(("dp", "tensor"), None),
            P(("dp", "tensor"), None),
            P(None, "dp", "tensor"),
            P(None, "tensor"),
            P("tensor", "dp"),
            P(),
            P("dp", "tensor"),
            P("tensor"),
            P("tensor", "dp"),
            P(),
            P(),
            P(),
            P(),
            P(),
        ),
        check_vma=False,
    )
```

```python
import functools

import jax
import jax.numpy as jnp
from jax import lax
from jax.experimental import pallas as pl
from jax.experimental.pallas import tpu as pltpu
from jax.sharding import PartitionSpec as P

HEADS = 16
SEQ = 584
VALID = 577


layer_eps = 1e-06
masked_score = -1e30


def normalize(signal, gain_vec, bias_vec):
    row_mean = jnp.mean(signal, axis=-1, keepdims=True)
    centred = signal - row_mean
    row_spread = jnp.mean(centred * centred, axis=-1, keepdims=True)
    return centred * lax.rsqrt(row_spread + layer_eps) * gain_vec + bias_vec


def gelu_exact(signal):
    return jax.nn.gelu(signal, approximate=False)


def masked_scores(queries, key_proj):
    score_scale = queries.shape[-1] ** (-0.5)
    scores = (
        jnp.einsum("qhe,khe->hqk", queries, key_proj, preferred_element_type=jnp.float32)
        * score_scale
    )
    valid_keys = jnp.arange(scores.shape[-1]) < VALID
    return jnp.where(valid_keys[None, None, :], scores, masked_score)


def attend_image(operands):
    queries, key_proj, value_proj = operands
    logits = masked_scores(queries, key_proj)
    row_top = jnp.max(logits, axis=-1, keepdims=True)
    row_expo = jnp.exp(logits - row_top)
    row_total = jnp.sum(row_expo, axis=-1, keepdims=True)
    weights = (row_expo / row_total).astype(jnp.bfloat16)
    head_mixed = jnp.einsum("hqk,khe->qhe", weights, value_proj, preferred_element_type=jnp.float32)
    return (head_mixed.astype(jnp.bfloat16), (row_top + jnp.log(row_total))[..., 0])


def attend_back(operands):
    queries, key_proj, value_proj, mixed_grad, row_lse = operands
    score_scale = queries.shape[-1] ** (-0.5)
    logits = masked_scores(queries, key_proj)
    probs = jnp.exp(logits - row_lse[..., None])
    value_grad = jnp.einsum(
        "hqk,qhe->khe", probs.astype(jnp.bfloat16), mixed_grad, preferred_element_type=jnp.float32
    )
    prob_grad = jnp.einsum(
        "qhe,khe->hqk", mixed_grad, value_proj, preferred_element_type=jnp.float32
    )
    score_grad = probs * (prob_grad - jnp.sum(probs * prob_grad, axis=-1, keepdims=True))
    score_grad = score_grad.astype(jnp.bfloat16)
    query_grad = (
        jnp.einsum("hqk,khe->qhe", score_grad, key_proj, preferred_element_type=jnp.float32)
        * score_scale
    )
    key_grad = (
        jnp.einsum("hqk,qhe->khe", score_grad, queries, preferred_element_type=jnp.float32)
        * score_scale
    )
    return (
        query_grad.astype(jnp.bfloat16),
        key_grad.astype(jnp.bfloat16),
        value_grad.astype(jnp.bfloat16),
    )


def split_heads(
    block_input,
    image_mask,
    w_qkv,
    b_qv,
    w_out,
    b_out,
    w_fc1,
    b_fc1,
    w_fc2,
    b_fc2,
    ln1_gain,
    ln1_bias,
    ln2_gain,
    ln2_bias,
    grad_out,
):
    local_rows = block_input.shape[0]
    model_width = block_input.shape[1]
    image_count = image_mask.shape[0]
    head_dim = model_width // HEADS
    local_width = w_qkv.shape[2]
    local_heads = local_width // head_dim
    tensor_index = lax.axis_index("tensor")
    token_index = tensor_index * local_rows + jnp.arange(local_rows)
    image_of = token_index // SEQ
    position = token_index % SEQ
    image_pick = (image_of[:, None] == jnp.arange(image_count)[None, :]).astype(jnp.float32)
    token_keep = jnp.sum(image_pick * image_mask.astype(jnp.float32)[None, :], axis=1)
    token_keep = token_keep * (position < VALID).astype(jnp.float32)
    contract_rows = (((0,), (0,)), ((), ()))
    contract_cols = (((1,), (1,)), ((), ()))
    full_qkv, full_out, full_fc1, full_fc2 = (
        lax.all_gather(w_qkv, "dp", axis=1, tiled=True),
        lax.all_gather(w_out, "dp", axis=1, tiled=True),
        lax.all_gather(w_fc1, "dp", axis=0, tiled=True),
        lax.all_gather(w_fc2, "dp", axis=1, tiled=True),
    )
    input_float = block_input.astype(jnp.float32)
    normed_one = normalize(input_float, ln1_gain, ln1_bias).astype(jnp.bfloat16)
    inputs_one = lax.all_gather(normed_one, "tensor", axis=0, tiled=True)
    group_rows = inputs_one.shape[0]
    projected = jnp.einsum("td,cde->cte", inputs_one, full_qkv, preferred_element_type=jnp.float32)
    queries = (projected[0] + b_qv[0]).astype(jnp.bfloat16)
    key_proj = projected[1].astype(jnp.bfloat16)
    value_proj = (projected[2] + b_qv[1]).astype(jnp.bfloat16)
    head_shape = (group_rows // SEQ, SEQ, local_heads, head_dim)
    query_heads = queries.reshape(head_shape)
    key_heads = key_proj.reshape(head_shape)
    value_heads = value_proj.reshape(head_shape)
    head_mixed, row_lse = lax.map(attend_image, (query_heads, key_heads, value_heads))
    head_mixed = head_mixed.reshape(group_rows, local_width)
    row_block = head_mixed
    attn_sum = lax.psum_scatter(
        jnp.dot(row_block, full_out, preferred_element_type=jnp.float32),
        "tensor",
        scatter_dimension=0,
        tiled=True,
    )
    resid = input_float + (attn_sum + b_out)
    normed_two = normalize(resid, ln2_gain, ln2_bias).astype(jnp.bfloat16)
    inputs_two = lax.all_gather(normed_two, "tensor", axis=0, tiled=True)
    hidden_pre = jnp.dot(inputs_two, full_fc1, preferred_element_type=jnp.float32) + b_fc1
    hidden = gelu_exact(hidden_pre).astype(jnp.bfloat16)
    row_block = hidden
    mlp_sum = lax.psum_scatter(
        jnp.dot(row_block, full_fc2, preferred_element_type=jnp.float32).astype(jnp.bfloat16),
        "tensor",
        scatter_dimension=0,
        tiled=True,
    ).astype(jnp.float32)
    layer_output = ((resid + (mlp_sum + b_fc2)) * token_keep[:, None]).astype(jnp.bfloat16)
    cot_rows = grad_out * token_keep.astype(jnp.bfloat16)[:, None]
    cot_float = cot_rows.astype(jnp.float32)
    cot_group = lax.all_gather(cot_rows, "tensor", axis=0, tiled=True)
    fc2_grad_group = lax.dot_general(
        hidden, cot_group, contract_rows, preferred_element_type=jnp.float32
    )
    hidden_grad = lax.dot_general(
        cot_group, full_fc2, contract_cols, preferred_element_type=jnp.float32
    )
    gelu_value, gelu_back = jax.vjp(gelu_exact, hidden_pre)
    pre_grad = gelu_back(hidden_grad)[0].astype(jnp.bfloat16)
    fc1_bias_grad = jnp.sum(pre_grad, axis=0, dtype=jnp.float32)
    fc1_grad_group = lax.dot_general(
        inputs_two, pre_grad, contract_rows, preferred_element_type=jnp.float32
    )
    row_block = pre_grad
    normed_two_grad = lax.psum_scatter(
        lax.dot_general(row_block, full_fc1, contract_cols, preferred_element_type=jnp.float32),
        "tensor",
        scatter_dimension=0,
        tiled=True,
    )
    norm_two_value, norm_two_back = jax.vjp(normalize, resid, ln2_gain, ln2_bias)
    resid_back, gain_two_grad, bias_two_grad = norm_two_back(normed_two_grad)
    resid_grad = cot_float + resid_back
    out_bias_grad = jnp.sum(resid_grad, axis=0)
    fc2_bias_grad = jnp.sum(cot_float, axis=0)
    resid_low = resid_grad.astype(jnp.bfloat16)
    resid_group = lax.all_gather(resid_low, "tensor", axis=0, tiled=True)
    out_grad_group = lax.dot_general(
        head_mixed, resid_group, contract_rows, preferred_element_type=jnp.float32
    )
    mixed_grad = lax.dot_general(
        resid_group, full_out, contract_cols, preferred_element_type=jnp.float32
    ).astype(jnp.bfloat16)
    query_grad, key_grad, value_grad = lax.map(
        attend_back, (query_heads, key_heads, value_heads, mixed_grad.reshape(head_shape), row_lse)
    )
    stacked_grads = jnp.stack(
        [
            query_grad.reshape(group_rows, local_width),
            key_grad.reshape(group_rows, local_width),
            value_grad.reshape(group_rows, local_width),
        ]
    )
    qkv_grad_group = jnp.einsum(
        "td,cte->cde", inputs_one, stacked_grads, preferred_element_type=jnp.float32
    )
    qv_bias_grad = jnp.stack(
        [
            jnp.sum(stacked_grads[0], axis=0, dtype=jnp.float32),
            jnp.sum(stacked_grads[2], axis=0, dtype=jnp.float32),
        ]
    )
    row_block = stacked_grads
    normed_one_grad = lax.psum_scatter(
        jnp.einsum("cte,cde->td", row_block, full_qkv, preferred_element_type=jnp.float32),
        "tensor",
        scatter_dimension=0,
        tiled=True,
    )
    norm_one_value, norm_one_back = jax.vjp(normalize, input_float, ln1_gain, ln1_bias)
    input_back, gain_one_grad, bias_one_grad = norm_one_back(normed_one_grad)
    input_grad = (resid_grad + input_back).astype(jnp.bfloat16)
    grad_w_qkv, grad_w_out, grad_w_fc1, grad_w_fc2 = (
        lax.psum_scatter(qkv_grad_group, "dp", scatter_dimension=1, tiled=True),
        lax.psum_scatter(out_grad_group, "dp", scatter_dimension=1, tiled=True),
        lax.psum_scatter(fc1_grad_group, "dp", scatter_dimension=0, tiled=True),
        lax.psum_scatter(fc2_grad_group, "dp", scatter_dimension=1, tiled=True),
    )
    vector_sums = lax.psum(
        (gain_one_grad, bias_one_grad, gain_two_grad, bias_two_grad, out_bias_grad, fc2_bias_grad),
        ("dp", "tensor"),
    )
    qv_sum, fc1_sum = lax.psum((qv_bias_grad, fc1_bias_grad), "dp")
    return (
        layer_output,
        input_grad,
        grad_w_qkv,
        qv_sum,
        grad_w_out,
        vector_sums[4],
        grad_w_fc1,
        fc1_sum,
        grad_w_fc2,
        vector_sums[5],
        vector_sums[0],
        vector_sums[1],
        vector_sums[2],
        vector_sums[3],
    )


BIT_X, BIT_CORE, BIT_Y, BIT_Z_LOW, BIT_Z_HIGH = 1, 2, 4, 8, 16
AXES = ("dp", "tensor")


def exchange(block, bit):
    return lax.ppermute(block, AXES, [(src, src ^ bit) for src in range(32)])


def leaves(deps):
    return jax.tree.leaves(deps)


ANYWHERE = pl.BlockSpec(memory_space=pl.ANY)
VMEM = pl.BlockSpec(memory_space=pltpu.VMEM)
FREE = pl.CostEstimate(flops=2 * 10**8, bytes_accessed=1, transcendentals=0)
STEP = pl.CostEstimate(flops=10**10, bytes_accessed=1, transcendentals=0)


def after(value, *deps):
    deps = leaves(deps)
    return pl.pallas_call(
        lambda *refs: None,
        in_specs=[ANYWHERE] * (1 + len(deps)),
        out_specs=ANYWHERE,
        out_shape=jax.ShapeDtypeStruct(value.shape, value.dtype),
        input_output_aliases={0: 0},
        compiler_params=pltpu.CompilerParams(vmem_limit_bytes=1 << 20),
    )(value, *deps)


def one_after(*deps):
    deps = leaves(deps)

    def kernel(*refs):
        refs[-1][...] = jnp.ones_like(refs[-1])

    return pl.pallas_call(
        kernel,
        in_specs=[ANYWHERE] * len(deps),
        out_shape=jax.ShapeDtypeStruct((1, 128), jnp.float32),
        compiler_params=pltpu.CompilerParams(vmem_limit_bytes=1 << 20),
    )(*deps)[0, 0]


def place_blocks(arrays, shapes, moves, deps=(), cost=None):
    deps = leaves(deps)

    def kernel(*refs):
        outs, sem = refs[len(arrays) + len(deps) : -1], refs[-1]
        copies = [
            pltpu.make_async_copy(refs[src].at[at], outs[dst].at[to], sem.at[i])
            for i, (src, at, dst, to) in enumerate(moves)
        ]
        for copy in copies:
            copy.start()
        for copy in copies:
            copy.wait()

    size = 4 * sum(v.size for v in arrays)
    return pl.pallas_call(
        kernel,
        in_specs=[ANYWHERE] * (len(arrays) + len(deps)),
        out_specs=[ANYWHERE] * len(shapes),
        out_shape=[jax.ShapeDtypeStruct(shape, jnp.bfloat16) for shape in shapes],
        scratch_shapes=[pltpu.SemaphoreType.DMA((len(moves),))],
        compiler_params=pltpu.CompilerParams(vmem_limit_bytes=1 << 20),
        cost_estimate=cost or STEP,
    )(*arrays, *deps)


class Gather:
    def __init__(self, shard, *deps):
        self.columns = shard.shape[1]
        self.shard = place_blocks([shard], [shard.shape], [(0, ..., 0, ...)], deps, FREE)[0] if deps else shard
        self.moving = exchange(self.shard, BIT_Z_HIGH)

    def step_one(self, *deps):
        rows = self.shard.shape[0]
        moves = [(got, ..., 0, slice(got * rows, got * rows + rows)) for got in range(2)]
        (self.block,) = place_blocks([self.shard, self.moving], [(2 * rows, self.columns)], moves, deps)
        self.moving = exchange(self.block, BIT_Z_LOW)
        return self.block

    def step_two(self, *deps):
        half = self.columns // 2
        moves = []
        for got in range(2):
            for part in range(2):
                columns = slice(part * half, part * half + half)
                moves.append((got, (slice(None), columns), part, slice(got * 128, got * 128 + 128)))
        self.blocks = place_blocks([self.block, self.moving], [(256, half)] * 2, moves, deps)
        self.moving = [exchange(self.blocks[0], BIT_X), exchange(self.blocks[1], BIT_Y)]
        return self.blocks

    def step_three(self, *deps):
        half = self.columns // 2
        moves = [(2 * got + part, ..., part, got) for got in range(2) for part in range(2)]
        self.blocks = place_blocks([*self.blocks, *self.moving], [(2, 256, half)] * 2, moves, deps)
        self.moving = [exchange(self.blocks[0], BIT_Y), exchange(self.blocks[1], BIT_X)]
        return self.blocks

    def step_four(self, *deps, cost=None):
        half = self.columns // 2
        moves = []
        for got, part, lead in [(j, k, m) for j in range(2) for k in range(2) for m in range(2)]:
            side, y = (lead, got) if part == 0 else (got, lead)
            column = side * self.columns + part * half
            moves.append((2 * got + part, lead, 0, (slice(y * 256, y * 256 + 256), slice(column, column + half))))
        (self.block,) = place_blocks([*self.blocks, *self.moving], [(512, 2 * self.columns)], moves, deps, cost)
        self.moving = exchange(self.block, BIT_CORE)
        return self.block

    def finish(self, *deps):
        moves = [(got, ..., 0, slice(got * 512, got * 512 + 512)) for got in range(2)]
        return place_blocks([self.block, self.moving], [(1024, 2 * self.columns)], moves, deps, FREE)[0]


def relative_weights(gathered, ranges, *deps):
    deps = leaves(deps)

    def kernel(*refs):
        source, outs, sem = refs[0], refs[1 + len(deps) : -1], refs[-1]
        device = lax.axis_index("dp") * 2 + lax.axis_index("tensor")
        copies = []
        for row in range(16):
            for side in range(2):
                apart = side + 2 * (row // 8) + 4 * (row // 4 % 2) + 8 * (row // 2 % 2) + 16 * (row % 2)
                for out, (lo, hi) in zip(outs, ranges):
                    width = hi - lo
                    copies.append(
                        pltpu.make_async_copy(
                            source.at[device ^ apart, :, lo:hi],
                            out.at[row * 64 : row * 64 + 64, side * width : side * width + width],
                            sem.at[len(copies)],
                        )
                    )
        for copy in copies:
            copy.start()
        for copy in copies:
            copy.wait()

    return pl.pallas_call(
        kernel,
        in_specs=[ANYWHERE] * (1 + len(deps)),
        out_specs=[pl.BlockSpec(memory_space=pltpu.VMEM)] * len(ranges),
        out_shape=[jax.ShapeDtypeStruct((1024, 2 * (hi - lo)), jnp.bfloat16) for lo, hi in ranges],
        scratch_shapes=[pltpu.SemaphoreType.DMA((32 * len(ranges),))],
        compiler_params=pltpu.CompilerParams(vmem_limit_bytes=44 << 20),
        cost_estimate=FREE,
    )(gathered, *deps)


def hidden_grads(cot, gathered, first, rest, slope, *deps):
    deps = leaves(deps)
    columns = slope.shape[1] // 2
    later = rest.shape[1] // 2
    width = columns - later
    blocks = []
    for side in range(2):
        middle = side * columns + width // 2
        blocks += [(side, side * columns, middle), (side, middle, side * columns + width)]
        blocks.insert(side, (side + 2, side * columns + width, (side + 1) * columns))

    def kernel(cot_ref, slope_ref, rest_ref, source, *refs):
        out_ref, sum_ref, weights_ref, sem = refs[-4:]
        device = lax.axis_index("dp") * 2 + lax.axis_index("tensor")
        copies = [[], [], [], []]
        for side in range(2):
            start = side * columns
            copies[side + 2].append(
                pltpu.make_async_copy(
                    rest_ref.at[:, side * later : (side + 1) * later],
                    weights_ref.at[:, start + width : start + columns],
                    sem.at[32 + side],
                )
            )
            for row in range(16):
                apart = side + 2 * (row // 8) + 4 * (row // 4 % 2) + 8 * (row // 2 % 2) + 16 * (row % 2)
                copies[side].append(
                    pltpu.make_async_copy(
                        source.at[device ^ apart, :, first : first + width],
                        weights_ref.at[row * 64 : row * 64 + 64, start : start + width],
                        sem.at[side * 16 + row],
                    )
                )
        for group in (2, 3, 0, 1):
            for copy in copies[group]:
                copy.start()
        for group, start, stop in blocks:
            for copy in copies[group]:
                copy.wait()
            copies[group] = []
            at = slice(start, stop)
            product = jnp.dot(cot_ref[...], weights_ref[:, at], preferred_element_type=jnp.float32)
            result = (product * slope_ref[:, at].astype(jnp.float32)).astype(jnp.bfloat16)
            out_ref[:, at] = result
            sum_ref[:, at] = jnp.sum(result.astype(jnp.float32), axis=0, keepdims=True)

    return pl.pallas_call(
        kernel,
        in_specs=[VMEM, VMEM] + [ANYWHERE] * (2 + len(deps)),
        out_specs=[VMEM, VMEM, VMEM],
        out_shape=[
            jax.ShapeDtypeStruct(slope.shape, jnp.bfloat16),
            jax.ShapeDtypeStruct((1, slope.shape[1]), jnp.float32),
            jax.ShapeDtypeStruct((1024, slope.shape[1]), jnp.bfloat16),
        ],
        scratch_shapes=[pltpu.SemaphoreType.DMA((34,))],
        compiler_params=pltpu.CompilerParams(vmem_limit_bytes=12 << 20),
        cost_estimate=FREE,
    )(cot, slope, rest, gathered, *deps)


def bias_rows(own, other):
    width = own.shape[1] - 1024

    def kernel(own_ref, other_ref, first_ref, second_ref, hidden_ref):
        for side, ref in enumerate((own_ref, other_ref)):
            for half, out_ref in enumerate((first_ref, second_ref)):
                start = side * 768
                out_ref[:, start : start + 256] = ref[:, half * 256 : half * 256 + 256]
                out_ref[:, start + 256 : start + 512] = jnp.zeros((1, 256), jnp.float32)
                out_ref[:, start + 512 : start + 768] = ref[:, 512 + half * 256 : 768 + half * 256]
            hidden_ref[:, side * width : side * width + width] = ref[:, 1024:]

    return pl.pallas_call(
        kernel,
        in_specs=[VMEM] * 2,
        out_specs=[VMEM] * 3,
        out_shape=[jax.ShapeDtypeStruct((1, size), jnp.float32) for size in (1536, 1536, 2 * width)],
        compiler_params=pltpu.CompilerParams(vmem_limit_bytes=2 << 20),
        cost_estimate=FREE,
    )(own, other)


def vector_rows(vectors, place, head_sums, hidden_sums, *deps):
    deps = leaves(deps)
    width = hidden_sums.shape[1] // 2

    def kernel(vectors_ref, place_ref, first_ref, second_ref, hidden_ref, *refs):
        left = vectors_ref[...]
        restored = jnp.zeros_like(left)
        for _ in range(3):
            part = left.astype(jnp.bfloat16)
            restored += lax.dot_general(
                part, place_ref[...], (((1,), (1,)), ((), ())), preferred_element_type=jnp.float32
            )
            left = left - part.astype(jnp.float32)
        for side, ref in enumerate(refs[-2:]):
            ref[0:8, :] = restored
            ref[8:16, :] = jnp.zeros_like(restored)
            for i, c in enumerate((0, 2)):
                for half, sums_ref in enumerate((first_ref, second_ref)):
                    source, target = side * 768 + c * 256, i * 512 + half * 256
                    ref[8:9, target : target + 256] = sums_ref[:, source : source + 256]
            for i in range(width // 1024):
                source = side * width + i * 1024
                ref[9 + i : 10 + i, :] = hidden_ref[:, source : source + 1024]

    return pl.pallas_call(
        kernel,
        in_specs=[VMEM] * 5 + [ANYWHERE] * len(deps),
        out_specs=[VMEM] * 2,
        out_shape=[jax.ShapeDtypeStruct((16, 1024), jnp.float32)] * 2,
        compiler_params=pltpu.CompilerParams(vmem_limit_bytes=8 << 20),
        cost_estimate=FREE,
    )(vectors, place, *head_sums, hidden_sums, *deps)


def weight_grads(left, right, keep, *deps):
    deps = leaves(deps)
    columns = right.shape[1]
    width = columns // (4 if columns > 2048 else 2)

    def kernel(left_ref, right_ref, *refs):
        out_ref = refs[-1]
        part = left_ref[:, :512] if keep else left_ref[:, 512:]

        @pl.loop(0, columns // width)
        def _(block):
            at = pl.ds(pl.multiple_of(block * width, width), width)
            product = lax.dot_general(
                part, right_ref[:, at], (((0,), (0,)), ((), ())), preferred_element_type=jnp.float32
            )
            out_ref[:, at] = product.astype(jnp.bfloat16)

    return pl.pallas_call(
        kernel,
        in_specs=[VMEM, VMEM] + [ANYWHERE] * len(deps),
        out_specs=VMEM,
        out_shape=jax.ShapeDtypeStruct((512, columns), jnp.bfloat16),
        compiler_params=pltpu.CompilerParams(vmem_limit_bytes=10 << 20),
        cost_estimate=FREE,
    )(left, right, *deps)


def back_through(grads, weights, *deps):
    deps = leaves(deps)
    width = 512

    def kernel(grads_ref, weights_ref, *refs):
        out_ref = refs[-1]
        for block in range(1024 // width):
            at = slice(block * width, block * width + width)
            out_ref[:, at] = lax.dot_general(
                grads_ref[...], weights_ref[at], (((1,), (1,)), ((), ())), preferred_element_type=jnp.float32
            )

    return pl.pallas_call(
        kernel,
        in_specs=[VMEM, VMEM] + [ANYWHERE] * len(deps),
        out_specs=VMEM,
        out_shape=jax.ShapeDtypeStruct((grads.shape[0], 1024), jnp.float32),
        compiler_params=pltpu.CompilerParams(vmem_limit_bytes=10 << 20),
        cost_estimate=FREE,
    )(grads, weights, *deps)


class Scatter:
    def __init__(self, pieces):
        width, moves = 0, []
        for i, piece in enumerate(pieces):
            moves.append((i, ..., 0, (slice(None), slice(width, width + piece.shape[1]))))
            width += piece.shape[1]
        self.sent = place_blocks(pieces, [(512, width)], moves, (), FREE)[0] if len(pieces) > 1 else pieces[0]
        self.got = exchange(self.sent, BIT_CORE)

    def call(self, kernel, ins, deps, shapes, dtype=jnp.bfloat16):
        deps = leaves(deps)
        outs = [jax.ShapeDtypeStruct(shape, dtype) for shape in shapes]
        size = 2 * sum(v.size for v in ins) + dtype(0).nbytes * sum(v.size for v in outs)
        count = len(ins)
        return pl.pallas_call(
            lambda *refs: kernel(refs[:count], refs[count + len(deps) :]),
            in_specs=[pl.BlockSpec(memory_space=pltpu.VMEM)] * count + [ANYWHERE] * len(deps),
            out_specs=[pl.BlockSpec(memory_space=pltpu.VMEM)] * len(outs),
            out_shape=outs,
            compiler_params=pltpu.CompilerParams(vmem_limit_bytes=4 << 20),
            cost_estimate=STEP,
        )(*ins, *deps)

    def step_one(self, pieces, *deps):
        widths = [piece.shape[1] // 2 for piece in pieces]
        self.columns = sum(widths)
        half = self.columns // 2

        def kernel(ins, outs):
            first = 0
            for i, width in enumerate(widths):
                for part in range(2):
                    start, stop = max(first, part * half), min(first + width, part * half + half)
                    if start >= stop:
                        continue
                    to = slice(start - part * half, stop - part * half)
                    for side in range(2):
                        columns = slice(side * width + start - first, side * width + stop - first)
                        came = slice(2 * first + columns.start, 2 * first + columns.stop)
                        for y in range(2):
                            rows = slice(y * 256, y * 256 + 256)
                            lead, send = (side, y) if part == 0 else (y, side)
                            value = ins[i][rows, columns] + ins[-1][rows, came]
                            outs[2 * part + send][lead, :, to] = value
                first += width

        outs = self.call(kernel, [*pieces, self.got], deps, [(2, 256, half)] * 4)
        self.kept = outs[0::2]
        self.moving = [exchange(outs[1], BIT_Y), exchange(outs[3], BIT_X)]
        return outs

    def step_two(self, *deps):
        half = self.columns // 2

        def kernel(ins, outs):
            for part in range(2):
                for send in range(2):
                    outs[2 * part + send][...] = ins[part][send] + ins[2 + part][send]

        outs = self.call(kernel, [*self.kept, *self.moving], deps, [(256, half)] * 4)
        self.kept = outs[0::2]
        self.moving = [exchange(outs[1], BIT_X), exchange(outs[3], BIT_Y)]
        return outs

    def step_three(self, *deps):
        half = self.columns // 2

        def kernel(ins, outs):
            for part in range(2):
                for send in range(2):
                    rows = slice(send * 128, send * 128 + 128)
                    outs[send][:, part * half : part * half + half] = ins[part][rows] + ins[2 + part][rows]

        outs = self.call(kernel, [*self.kept, *self.moving], deps, [(128, self.columns)] * 2)
        self.kept, self.moving = outs[0], exchange(outs[1], BIT_Z_LOW)
        return outs

    def step_four(self, *deps):
        def kernel(ins, outs):
            for send in range(2):
                rows = slice(send * 64, send * 64 + 64)
                outs[send][...] = ins[0][rows] + ins[1][rows]

        outs = self.call(kernel, [self.kept, self.moving], deps, [(64, self.columns)] * 2)
        self.kept, self.moving = outs[0], exchange(outs[1], BIT_Z_HIGH)
        return outs

    def finish(self, *deps):
        def kernel(ins, outs):
            outs[0][...] = ins[0][...].astype(jnp.float32) + ins[1][...].astype(jnp.float32)

        return self.call(kernel, [self.kept, self.moving], deps, [(64, self.columns)], jnp.float32)[0]


def place_matrix():
    relative = lax.broadcasted_iota(jnp.int32, (1024, 1024), 1)
    feature = lax.broadcasted_iota(jnp.int32, (1024, 1024), 0)
    block = relative // 64
    shard = (block // 8) + 2 * (block // 4 % 2) + 4 * (block // 2 % 2) + 8 * (block % 2)
    shard = shard ^ lax.axis_index("dp")
    return (feature == shard * 64 + relative % 64).astype(jnp.bfloat16)


def head_scores(queries, keys, lane, head):
    spare = (1 - head) * 64
    position = lax.broadcasted_iota(jnp.int32, keys.shape, 0)
    mask = jnp.where((lane == spare) & (position >= VALID), masked_score, 0.0).astype(keys.dtype)
    keys = jnp.where((lane // 64) == head, keys, mask)
    queries = jnp.where(lane == spare, jnp.ones_like(queries), queries)
    return lax.dot_general(keys, queries, (((1,), (1,)), ((), ())), preferred_element_type=jnp.float32)


def attend_kernel(q_ref, k_ref, v_ref, *refs):
    o_ref, lse_ref = refs[-2:]
    queries, keys, values = q_ref[...], k_ref[...], v_ref[...]
    queries = queries * jnp.bfloat16(0.125)
    lane = lax.broadcasted_iota(jnp.int32, keys.shape, 1)
    mixed = []
    for head in range(2):
        scores = head_scores(queries, keys, lane, head)
        top = jnp.max(scores, axis=0, keepdims=True)
        expo = jnp.exp(scores - top)
        norm = jnp.sum(expo, axis=0, keepdims=True)
        out = lax.dot_general(
            values, expo.astype(jnp.bfloat16), (((0,), (0,)), ((), ())), preferred_element_type=jnp.float32
        )
        mixed.append(out[head * 64 : head * 64 + 64] / norm)
        lse_ref[0, head : head + 1, :] = top + jnp.log(norm)
    o_ref[...] = jnp.concatenate(mixed, axis=0).T.astype(jnp.bfloat16)


def head_specs():
    return [pl.BlockSpec((SEQ, 128), lambda image, pair, c=c: (image, pair // 2 * 6 + 2 * c + pair % 2)) for c in range(3)]


def mixed_spec(half):
    return pl.BlockSpec((SEQ, 128), lambda image, pair: (image, pair // 2 * 4 + 2 * half + pair % 2))


def attend_pairs(projected, half, mixed, *deps):
    deps = ([] if mixed is None else [mixed]) + leaves(deps)
    rows = projected.shape[0]
    images = rows // SEQ
    return pl.pallas_call(
        attend_kernel,
        grid=(images, 4),
        in_specs=head_specs() + [ANYWHERE] * len(deps),
        out_specs=[
            mixed_spec(half),
            pl.BlockSpec((1, 2, SEQ), lambda image, pair: (image * 4 + pair, 0, 0)),
        ],
        out_shape=[
            jax.ShapeDtypeStruct((rows, 1024), jnp.bfloat16),
            jax.ShapeDtypeStruct((images * 4, 2, SEQ), jnp.float32),
        ],
        input_output_aliases={} if mixed is None else {3: 0},
        compiler_params=pltpu.CompilerParams(vmem_limit_bytes=14 << 20),
        cost_estimate=FREE,
    )(projected, projected, projected, *deps)


def attend_back_kernel(q_ref, k_ref, v_ref, do_ref, lse_ref, *refs):
    out_ref, sum_ref = refs[-2:]
    queries, keys, values, mixed_grad = q_ref[...], k_ref[...], v_ref[...], do_ref[...]
    queries = queries * jnp.bfloat16(0.125)
    lane = lax.broadcasted_iota(jnp.int32, keys.shape, 1)
    dq, dk, dv = [], [], []
    for head in range(2):
        own = (lane // 64) == head
        probs = jnp.exp(head_scores(queries, keys, lane, head) - lse_ref[0, head : head + 1, :])
        dv.append(jnp.dot(probs.astype(jnp.bfloat16), mixed_grad, preferred_element_type=jnp.float32))
        back = lax.dot_general(
            jnp.where(own, values, 0), mixed_grad, (((1,), (1,)), ((), ())), preferred_element_type=jnp.float32
        )
        row = jnp.sum(probs * back, axis=0, keepdims=True)
        score_grad = (probs * (back - row)).astype(jnp.bfloat16)
        dk.append(jnp.dot(score_grad, queries, preferred_element_type=jnp.float32))
        out = lax.dot_general(
            keys, score_grad, (((0,), (0,)), ((), ())), preferred_element_type=jnp.float32
        )
        dq.append(out[head * 64 : head * 64 + 64] * 0.125)
    low = lane < 64
    results = (
        jnp.concatenate(dq, axis=0).T.astype(jnp.bfloat16),
        jnp.where(low, dk[0], dk[1]).astype(jnp.bfloat16),
        jnp.where(low, dv[0], dv[1]).astype(jnp.bfloat16),
    )
    pair = pl.program_id(1)
    for c, result in enumerate(results):
        column = (pair // 2 * 6 + 2 * c + pair % 2) * 128
        at = pl.ds(pl.multiple_of(column, 128), 128)
        out_ref[:, at] = result
        total = jnp.sum(result.astype(jnp.float32), axis=0, keepdims=True)
        sum_ref[0, :, at] = total


def attend_back_pairs(projected, mixed_grad, lse, half, *deps):
    deps = leaves(deps)
    rows = projected.shape[0]
    images = rows // SEQ
    return pl.pallas_call(
        attend_back_kernel,
        grid=(images, 4),
        in_specs=head_specs()
        + [
            mixed_spec(half),
            pl.BlockSpec((1, 2, SEQ), lambda image, pair: (image * 4 + pair, 0, 0)),
        ]
        + [ANYWHERE] * len(deps),
        out_specs=[
            pl.BlockSpec((SEQ, 1536), lambda image, pair: (image, 0)),
            pl.BlockSpec((1, 1, 1536), lambda image, pair: (image, 0, 0)),
        ],
        out_shape=[
            jax.ShapeDtypeStruct((rows, 1536), jnp.bfloat16),
            jax.ShapeDtypeStruct((images, 1, 1536), jnp.float32),
        ],
        compiler_params=pltpu.CompilerParams(vmem_limit_bytes=20 << 20),
        cost_estimate=FREE,
    )(projected, projected, projected, mixed_grad, lse, *deps)


def own_images(
    block_input,
    image_mask,
    w_qkv,
    b_qv,
    w_out,
    b_out,
    w_fc1,
    b_fc1,
    w_fc2,
    b_fc2,
    ln1_gain,
    ln1_bias,
    ln2_gain,
    ln2_bias,
    grad_out,
):
    f32, low = jnp.float32, jnp.bfloat16
    both = range(2)
    rows = block_input.shape[0]
    tensor_index = lax.axis_index("tensor")
    token_index = tensor_index * rows + jnp.arange(rows)
    image_pick = ((token_index // SEQ)[:, None] == jnp.arange(image_mask.shape[0])[None, :]).astype(f32)
    token_keep = jnp.sum(image_pick * image_mask.astype(f32)[None, :], axis=1)
    token_keep = token_keep * (token_index % SEQ < VALID).astype(f32)

    def rows_of(left, right):
        return lax.dot_general(left, right, (((0,), (0,)), ((), ())), preferred_element_type=f32)

    def cols_of(left, right):
        return lax.dot_general(left, right, (((1,), (1,)), ((), ())), preferred_element_type=f32)

    def dot(left, right):
        return jnp.dot(left, right, preferred_element_type=f32)

    def qkv_columns(half):
        part = slice(half * 256, half * 256 + 256)
        return jnp.concatenate([w_qkv[0][:, part], w_qkv[1][:, part], w_qkv[2][:, part]], axis=1)

    bias_own = jnp.concatenate([b_qv.reshape(-1), b_fc1])[None, :]
    *b_heads, b_hidden = bias_rows(bias_own, exchange(bias_own, BIT_X))
    qkv = [Gather(qkv_columns(0))]
    gathered = lax.all_gather(jnp.concatenate([w_fc1, w_fc2.T[:, :1536]], axis=1), AXES, axis=0, tiled=False)

    go = qkv[0].step_one(b_hidden)
    place = after(place_matrix(), go)
    vectors = jnp.stack([b_out, b_fc2, ln1_gain, ln1_bias, ln2_gain, ln2_bias])
    vectors = jnp.dot(vectors, place.astype(f32), precision=lax.Precision.HIGHEST)
    b_out, b_fc2, ln1_gain, ln1_bias, ln2_gain, ln2_bias = vectors
    signal = dot(block_input, place)
    cot_low = dot(grad_out * token_keep.astype(low)[:, None], place).astype(low)
    cot = cot_low.astype(f32)
    normed_one = normalize(signal, ln1_gain, ln1_bias).astype(low)

    qkv.append(Gather(qkv_columns(1), go))
    go = qkv[0].step_two(qkv[1].shard, normed_one, cot_low, b_fc2)
    go = qkv[1].step_one(go)
    go = qkv[0].step_three(go)
    go = qkv[1].step_two(go)
    out = Gather(w_out.T, go)
    go = qkv[0].step_four(out.shard)
    w_heads, projected, lse = [], [], []

    def project(half, *deps):
        w_heads.append(qkv[half].finish(*deps))
        projected.append((dot(normed_one, w_heads[half]) + b_heads[half]).astype(low))
        return projected[half]

    go = project(0, go)
    go = qkv[1].step_three(go)
    go = out.step_one(go)
    mixed, lse_half = attend_pairs(projected[0], 0, None, go)
    lse.append(lse_half)
    go = out.step_two(mixed)
    go = qkv[1].step_four(go, cost=FREE)
    go = project(1, go)
    go = out.step_three(go)
    two = Gather(w_fc2.T[:, 1536:], go)
    mixed, lse_half = attend_pairs(projected[1], 1, mixed, go, two.shard)
    lse.append(lse_half)
    go = two.step_one(mixed)
    go = out.step_four(go)
    w_mix = out.finish(go)
    attn = cols_of(mixed, w_mix)
    resid = signal + (attn + b_out)
    normed_two = normalize(resid, ln2_gain, ln2_bias).astype(low)
    go = two.step_two(normed_two)
    (w_one,) = relative_weights(gathered, [(0, 2048)], go)
    pre = dot(normed_two, w_one) + b_hidden
    phi = 0.5 * (1.0 + lax.erf(pre * (0.5**0.5)))
    hidden = (pre * phi).astype(low)
    slope = (phi + pre * (jnp.exp(-0.5 * pre * pre) * (0.5 / 3.141592653589793) ** 0.5)).astype(low)

    go = two.step_three(hidden)
    fc2_far = weight_grads(cot_low, hidden, False, go)
    fc2_sum = Scatter([fc2_far])
    go = fc2_sum.step_one([weight_grads(cot_low, hidden, True, fc2_far)])
    go = two.step_four(go)
    pre_grad, fc1_bias_grad, w_two = hidden_grads(cot_low, gathered, 2048, two.finish(go), slope)
    fc1_far = weight_grads(normed_two, pre_grad, False)
    normed_two_grad = back_through(pre_grad, w_one, fc1_far)
    mlp = back_through(hidden, w_two, normed_two_grad)
    layer_output = ((resid + (mlp + b_fc2)) * token_keep[:, None]).astype(low)
    layer_output = cols_of(layer_output, place).astype(low)
    go = fc2_sum.step_two(mlp)
    fc1_sum = Scatter([after(fc1_far, go)])
    fc1_near = weight_grads(normed_two, pre_grad, True, go)
    go = fc1_sum.step_one([fc1_near])
    go = fc2_sum.step_three(go, layer_output)
    _, norm_two_back = jax.vjp(normalize, resid, ln2_gain, ln2_bias)
    resid_back, gain_two_grad, bias_two_grad = norm_two_back(after(normed_two_grad, go))
    resid_grad = cot + resid_back
    resid_low = resid_grad.astype(low)
    mixed_grad = dot(resid_low, w_mix).astype(low)
    grads, sums = attend_back_pairs(projected[0], mixed_grad, lse[0], 0)
    head_grads, head_sums = [grads], [sums.sum(0)]
    go = fc2_sum.step_four(grads)
    go = fc1_sum.step_two(go)

    def first_pieces(keep, go):
        heads_part = weight_grads(normed_one, head_grads[0], keep, go)
        return [heads_part, weight_grads(resid_low, mixed, keep, heads_part)]

    heads_sum = [Scatter(first_pieces(False, go))]
    go = heads_sum[0].step_one(first_pieces(True, heads_sum[0].sent))
    grads, sums = attend_back_pairs(projected[1], mixed_grad, lse[1], 1, go)
    head_grads.append(grads)
    head_sums.append(sums.sum(0))
    fc2_grad = fc2_sum.finish(head_grads[1])
    go = fc1_sum.step_three(fc2_grad)
    heads_far = weight_grads(normed_one, head_grads[1], False, go)
    heads_sum.append(Scatter([heads_far]))
    heads_near = weight_grads(normed_one, head_grads[1], True, heads_far)
    go = heads_sum[0].step_two(heads_near)
    go = heads_sum[1].step_one([heads_near], go)
    normed_one_grad = sum(
        cols_of(head_grads[half], w_heads[half]) * one_after(go) for half in both
    )
    go = fc1_sum.step_four(normed_one_grad)
    go = heads_sum[0].step_three(go)
    _, norm_one_back = jax.vjp(normalize, signal, ln1_gain, ln1_bias)
    input_back, gain_one_grad, bias_one_grad = norm_one_back(normed_one_grad)
    out_sum, cot_sum = jnp.sum(resid_grad, axis=0), jnp.sum(cot, axis=0)
    zeros = jnp.zeros_like(out_sum)
    vectors = jnp.stack(
        [gain_one_grad, bias_one_grad, gain_two_grad, bias_two_grad, out_sum, cot_sum, zeros, zeros]
    )
    own, other = vector_rows(vectors, place, head_sums, fc1_bias_grad, go)
    sums = own + exchange(other, BIT_X)
    go = heads_sum[1].step_two(own)
    input_grad = cols_of((resid_grad + input_back).astype(low), place).astype(low)
    sums = after(sums, go)
    sums = sums + exchange(sums, BIT_Y)
    fc1_grad = fc1_sum.finish(go)
    go = heads_sum[0].step_four(fc1_grad)
    go = heads_sum[1].step_three(input_grad, go)
    sums = after(sums, go)
    sums = sums + exchange(sums, BIT_Z_HIGH) + exchange(sums, BIT_Z_LOW) + exchange(sums, BIT_Z_HIGH | BIT_Z_LOW)
    go = heads_sum[1].step_four(go)
    sums = after(sums, go)
    sums = sums + exchange(sums, BIT_CORE)
    side_sums = sums[8:11].reshape(3072)
    heads_grad = [heads_sum[0].finish(go), heads_sum[1].finish()]
    qkv_grad = jnp.concatenate([g[:, :768].reshape(64, 3, 256) for g in heads_grad], axis=2)
    return (
        layer_output,
        input_grad,
        qkv_grad.transpose(1, 0, 2),
        side_sums[:1024].reshape(2, 512),
        heads_grad[0][:, 768:].T,
        sums[4],
        fc1_grad,
        side_sums[1024:],
        fc2_grad.T,
        sums[5],
        sums[0],
        sums[1],
        sums[2],
        sums[3],
    )


def solution(mesh):
    def plan(block_input, *others):
        whole_images = block_input.shape[0] % SEQ == 0
        if whole_images and mesh.shape["dp"] == 16 and mesh.shape["tensor"] == 2:
            return own_images(block_input, *others)
        return split_heads(block_input, *others)

    return jax.shard_map(
        plan,
        mesh=mesh,
        in_specs=(
            P(("dp", "tensor"), None),
            P("dp"),
            P(None, "dp", "tensor"),
            P(None, "tensor"),
            P("tensor", "dp"),
            P(),
            P("dp", "tensor"),
            P("tensor"),
            P("tensor", "dp"),
            P(),
            P(),
            P(),
            P(),
            P(),
            P(("dp", "tensor"), None),
        ),
        out_specs=(
            P(("dp", "tensor"), None),
            P(("dp", "tensor"), None),
            P(None, "dp", "tensor"),
            P(None, "tensor"),
            P("tensor", "dp"),
            P(),
            P("dp", "tensor"),
            P("tensor"),
            P("tensor", "dp"),
            P(),
            P(),
            P(),
            P(),
            P(),
        ),
        check_vma=False,
    )
```

```python
import functools

import jax
import jax.numpy as jnp
from jax import lax
from jax.experimental import pallas as pl
from jax.experimental.pallas import tpu as pltpu
from jax.sharding import PartitionSpec as P

HEADS = 16
SEQ = 584
VALID = 577


layer_eps = 1e-06
masked_score = -1e30


def normalize(signal, gain_vec, bias_vec):
    row_mean = jnp.mean(signal, axis=-1, keepdims=True)
    centred = signal - row_mean
    row_spread = jnp.mean(centred * centred, axis=-1, keepdims=True)
    return centred * lax.rsqrt(row_spread + layer_eps) * gain_vec + bias_vec


def gelu_exact(signal):
    return jax.nn.gelu(signal, approximate=False)


def masked_scores(queries, key_proj):
    score_scale = queries.shape[-1] ** (-0.5)
    scores = (
        jnp.einsum("qhe,khe->hqk", queries, key_proj, preferred_element_type=jnp.float32)
        * score_scale
    )
    valid_keys = jnp.arange(scores.shape[-1]) < VALID
    return jnp.where(valid_keys[None, None, :], scores, masked_score)


def attend_image(operands):
    queries, key_proj, value_proj = operands
    logits = masked_scores(queries, key_proj)
    row_top = jnp.max(logits, axis=-1, keepdims=True)
    row_expo = jnp.exp(logits - row_top)
    row_total = jnp.sum(row_expo, axis=-1, keepdims=True)
    weights = (row_expo / row_total).astype(jnp.bfloat16)
    head_mixed = jnp.einsum("hqk,khe->qhe", weights, value_proj, preferred_element_type=jnp.float32)
    return (head_mixed.astype(jnp.bfloat16), (row_top + jnp.log(row_total))[..., 0])


def attend_back(operands):
    queries, key_proj, value_proj, mixed_grad, row_lse = operands
    score_scale = queries.shape[-1] ** (-0.5)
    logits = masked_scores(queries, key_proj)
    probs = jnp.exp(logits - row_lse[..., None])
    value_grad = jnp.einsum(
        "hqk,qhe->khe", probs.astype(jnp.bfloat16), mixed_grad, preferred_element_type=jnp.float32
    )
    prob_grad = jnp.einsum(
        "qhe,khe->hqk", mixed_grad, value_proj, preferred_element_type=jnp.float32
    )
    score_grad = probs * (prob_grad - jnp.sum(probs * prob_grad, axis=-1, keepdims=True))
    score_grad = score_grad.astype(jnp.bfloat16)
    query_grad = (
        jnp.einsum("hqk,khe->qhe", score_grad, key_proj, preferred_element_type=jnp.float32)
        * score_scale
    )
    key_grad = (
        jnp.einsum("hqk,qhe->khe", score_grad, queries, preferred_element_type=jnp.float32)
        * score_scale
    )
    return (
        query_grad.astype(jnp.bfloat16),
        key_grad.astype(jnp.bfloat16),
        value_grad.astype(jnp.bfloat16),
    )


def split_heads(
    block_input,
    image_mask,
    w_qkv,
    b_qv,
    w_out,
    b_out,
    w_fc1,
    b_fc1,
    w_fc2,
    b_fc2,
    ln1_gain,
    ln1_bias,
    ln2_gain,
    ln2_bias,
    grad_out,
):
    local_rows = block_input.shape[0]
    model_width = block_input.shape[1]
    image_count = image_mask.shape[0]
    head_dim = model_width // HEADS
    local_width = w_qkv.shape[2]
    local_heads = local_width // head_dim
    tensor_index = lax.axis_index("tensor")
    token_index = tensor_index * local_rows + jnp.arange(local_rows)
    image_of = token_index // SEQ
    position = token_index % SEQ
    image_pick = (image_of[:, None] == jnp.arange(image_count)[None, :]).astype(jnp.float32)
    token_keep = jnp.sum(image_pick * image_mask.astype(jnp.float32)[None, :], axis=1)
    token_keep = token_keep * (position < VALID).astype(jnp.float32)
    contract_rows = (((0,), (0,)), ((), ()))
    contract_cols = (((1,), (1,)), ((), ()))
    full_qkv, full_out, full_fc1, full_fc2 = (
        lax.all_gather(w_qkv, "dp", axis=1, tiled=True),
        lax.all_gather(w_out, "dp", axis=1, tiled=True),
        lax.all_gather(w_fc1, "dp", axis=0, tiled=True),
        lax.all_gather(w_fc2, "dp", axis=1, tiled=True),
    )
    input_float = block_input.astype(jnp.float32)
    normed_one = normalize(input_float, ln1_gain, ln1_bias).astype(jnp.bfloat16)
    inputs_one = lax.all_gather(normed_one, "tensor", axis=0, tiled=True)
    group_rows = inputs_one.shape[0]
    projected = jnp.einsum("td,cde->cte", inputs_one, full_qkv, preferred_element_type=jnp.float32)
    queries = (projected[0] + b_qv[0]).astype(jnp.bfloat16)
    key_proj = projected[1].astype(jnp.bfloat16)
    value_proj = (projected[2] + b_qv[1]).astype(jnp.bfloat16)
    head_shape = (group_rows // SEQ, SEQ, local_heads, head_dim)
    query_heads = queries.reshape(head_shape)
    key_heads = key_proj.reshape(head_shape)
    value_heads = value_proj.reshape(head_shape)
    head_mixed, row_lse = lax.map(attend_image, (query_heads, key_heads, value_heads))
    head_mixed = head_mixed.reshape(group_rows, local_width)
    row_block = head_mixed
    attn_sum = lax.psum_scatter(
        jnp.dot(row_block, full_out, preferred_element_type=jnp.float32),
        "tensor",
        scatter_dimension=0,
        tiled=True,
    )
    resid = input_float + (attn_sum + b_out)
    normed_two = normalize(resid, ln2_gain, ln2_bias).astype(jnp.bfloat16)
    inputs_two = lax.all_gather(normed_two, "tensor", axis=0, tiled=True)
    hidden_pre = jnp.dot(inputs_two, full_fc1, preferred_element_type=jnp.float32) + b_fc1
    hidden = gelu_exact(hidden_pre).astype(jnp.bfloat16)
    row_block = hidden
    mlp_sum = lax.psum_scatter(
        jnp.dot(row_block, full_fc2, preferred_element_type=jnp.float32).astype(jnp.bfloat16),
        "tensor",
        scatter_dimension=0,
        tiled=True,
    ).astype(jnp.float32)
    layer_output = ((resid + (mlp_sum + b_fc2)) * token_keep[:, None]).astype(jnp.bfloat16)
    cot_rows = grad_out * token_keep.astype(jnp.bfloat16)[:, None]
    cot_float = cot_rows.astype(jnp.float32)
    cot_group = lax.all_gather(cot_rows, "tensor", axis=0, tiled=True)
    fc2_grad_group = lax.dot_general(
        hidden, cot_group, contract_rows, preferred_element_type=jnp.float32
    )
    hidden_grad = lax.dot_general(
        cot_group, full_fc2, contract_cols, preferred_element_type=jnp.float32
    )
    gelu_value, gelu_back = jax.vjp(gelu_exact, hidden_pre)
    pre_grad = gelu_back(hidden_grad)[0].astype(jnp.bfloat16)
    fc1_bias_grad = jnp.sum(pre_grad, axis=0, dtype=jnp.float32)
    fc1_grad_group = lax.dot_general(
        inputs_two, pre_grad, contract_rows, preferred_element_type=jnp.float32
    )
    row_block = pre_grad
    normed_two_grad = lax.psum_scatter(
        lax.dot_general(row_block, full_fc1, contract_cols, preferred_element_type=jnp.float32),
        "tensor",
        scatter_dimension=0,
        tiled=True,
    )
    norm_two_value, norm_two_back = jax.vjp(normalize, resid, ln2_gain, ln2_bias)
    resid_back, gain_two_grad, bias_two_grad = norm_two_back(normed_two_grad)
    resid_grad = cot_float + resid_back
    out_bias_grad = jnp.sum(resid_grad, axis=0)
    fc2_bias_grad = jnp.sum(cot_float, axis=0)
    resid_low = resid_grad.astype(jnp.bfloat16)
    resid_group = lax.all_gather(resid_low, "tensor", axis=0, tiled=True)
    out_grad_group = lax.dot_general(
        head_mixed, resid_group, contract_rows, preferred_element_type=jnp.float32
    )
    mixed_grad = lax.dot_general(
        resid_group, full_out, contract_cols, preferred_element_type=jnp.float32
    ).astype(jnp.bfloat16)
    query_grad, key_grad, value_grad = lax.map(
        attend_back, (query_heads, key_heads, value_heads, mixed_grad.reshape(head_shape), row_lse)
    )
    stacked_grads = jnp.stack(
        [
            query_grad.reshape(group_rows, local_width),
            key_grad.reshape(group_rows, local_width),
            value_grad.reshape(group_rows, local_width),
        ]
    )
    qkv_grad_group = jnp.einsum(
        "td,cte->cde", inputs_one, stacked_grads, preferred_element_type=jnp.float32
    )
    qv_bias_grad = jnp.stack(
        [
            jnp.sum(stacked_grads[0], axis=0, dtype=jnp.float32),
            jnp.sum(stacked_grads[2], axis=0, dtype=jnp.float32),
        ]
    )
    row_block = stacked_grads
    normed_one_grad = lax.psum_scatter(
        jnp.einsum("cte,cde->td", row_block, full_qkv, preferred_element_type=jnp.float32),
        "tensor",
        scatter_dimension=0,
        tiled=True,
    )
    norm_one_value, norm_one_back = jax.vjp(normalize, input_float, ln1_gain, ln1_bias)
    input_back, gain_one_grad, bias_one_grad = norm_one_back(normed_one_grad)
    input_grad = (resid_grad + input_back).astype(jnp.bfloat16)
    grad_w_qkv, grad_w_out, grad_w_fc1, grad_w_fc2 = (
        lax.psum_scatter(qkv_grad_group, "dp", scatter_dimension=1, tiled=True),
        lax.psum_scatter(out_grad_group, "dp", scatter_dimension=1, tiled=True),
        lax.psum_scatter(fc1_grad_group, "dp", scatter_dimension=0, tiled=True),
        lax.psum_scatter(fc2_grad_group, "dp", scatter_dimension=1, tiled=True),
    )
    vector_sums = lax.psum(
        (gain_one_grad, bias_one_grad, gain_two_grad, bias_two_grad, out_bias_grad, fc2_bias_grad),
        ("dp", "tensor"),
    )
    qv_sum, fc1_sum = lax.psum((qv_bias_grad, fc1_bias_grad), "dp")
    return (
        layer_output,
        input_grad,
        grad_w_qkv,
        qv_sum,
        grad_w_out,
        vector_sums[4],
        grad_w_fc1,
        fc1_sum,
        grad_w_fc2,
        vector_sums[5],
        vector_sums[0],
        vector_sums[1],
        vector_sums[2],
        vector_sums[3],
    )


BIT_X, BIT_CORE, BIT_Y, BIT_Z_LOW, BIT_Z_HIGH = 1, 2, 4, 8, 16
AXES = ("dp", "tensor")


def exchange(block, bit):
    return lax.ppermute(block, AXES, [(src, src ^ bit) for src in range(32)])


def leaves(deps):
    return jax.tree.leaves(deps)


ANYWHERE = pl.BlockSpec(memory_space=pl.ANY)
VMEM = pl.BlockSpec(memory_space=pltpu.VMEM)
FREE = pl.CostEstimate(flops=2 * 10**8, bytes_accessed=1, transcendentals=0)
STEP = pl.CostEstimate(flops=10**10, bytes_accessed=1, transcendentals=0)


def after(value, *deps):
    deps = leaves(deps)
    return pl.pallas_call(
        lambda *refs: None,
        in_specs=[ANYWHERE] * (1 + len(deps)),
        out_specs=ANYWHERE,
        out_shape=jax.ShapeDtypeStruct(value.shape, value.dtype),
        input_output_aliases={0: 0},
        compiler_params=pltpu.CompilerParams(vmem_limit_bytes=1 << 20),
    )(value, *deps)


def one_after(*deps):
    deps = leaves(deps)

    def kernel(*refs):
        refs[-1][...] = jnp.ones_like(refs[-1])

    return pl.pallas_call(
        kernel,
        in_specs=[ANYWHERE] * len(deps),
        out_shape=jax.ShapeDtypeStruct((1, 128), jnp.float32),
        compiler_params=pltpu.CompilerParams(vmem_limit_bytes=1 << 20),
    )(*deps)[0, 0]


def place_blocks(arrays, shapes, moves, deps=(), cost=None):
    deps = leaves(deps)

    def kernel(*refs):
        outs, sem = refs[len(arrays) + len(deps) : -1], refs[-1]
        copies = [
            pltpu.make_async_copy(refs[src].at[at], outs[dst].at[to], sem.at[i])
            for i, (src, at, dst, to) in enumerate(moves)
        ]
        for copy in copies:
            copy.start()
        for copy in copies:
            copy.wait()

    size = 4 * sum(v.size for v in arrays)
    return pl.pallas_call(
        kernel,
        in_specs=[ANYWHERE] * (len(arrays) + len(deps)),
        out_specs=[ANYWHERE] * len(shapes),
        out_shape=[jax.ShapeDtypeStruct(shape, jnp.bfloat16) for shape in shapes],
        scratch_shapes=[pltpu.SemaphoreType.DMA((len(moves),))],
        compiler_params=pltpu.CompilerParams(vmem_limit_bytes=1 << 20),
        cost_estimate=cost or STEP,
    )(*arrays, *deps)


class Gather:
    def __init__(self, shard, *deps):
        self.columns = shard.shape[1]
        self.shard = place_blocks([shard], [shard.shape], [(0, ..., 0, ...)], deps, FREE)[0] if deps else shard
        self.moving = exchange(self.shard, BIT_Z_HIGH)

    def step_one(self, *deps):
        rows = self.shard.shape[0]
        moves = [(got, ..., 0, slice(got * rows, got * rows + rows)) for got in range(2)]
        (self.block,) = place_blocks([self.shard, self.moving], [(2 * rows, self.columns)], moves, deps)
        self.moving = exchange(self.block, BIT_Z_LOW)
        return self.block

    def step_two(self, *deps):
        half = self.columns // 2
        moves = []
        for got in range(2):
            for part in range(2):
                columns = slice(part * half, part * half + half)
                moves.append((got, (slice(None), columns), part, slice(got * 128, got * 128 + 128)))
        self.blocks = place_blocks([self.block, self.moving], [(256, half)] * 2, moves, deps)
        self.moving = [exchange(self.blocks[0], BIT_X), exchange(self.blocks[1], BIT_Y)]
        return self.blocks

    def step_three(self, *deps):
        half = self.columns // 2
        moves = [(2 * got + part, ..., part, got) for got in range(2) for part in range(2)]
        self.blocks = place_blocks([*self.blocks, *self.moving], [(2, 256, half)] * 2, moves, deps)
        self.moving = [exchange(self.blocks[0], BIT_Y), exchange(self.blocks[1], BIT_X)]
        return self.blocks

    def step_four(self, *deps, cost=None):
        half = self.columns // 2
        moves = []
        for got, part, lead in [(j, k, m) for j in range(2) for k in range(2) for m in range(2)]:
            side, y = (lead, got) if part == 0 else (got, lead)
            column = side * self.columns + part * half
            moves.append((2 * got + part, lead, 0, (slice(y * 256, y * 256 + 256), slice(column, column + half))))
        (self.block,) = place_blocks([*self.blocks, *self.moving], [(512, 2 * self.columns)], moves, deps, cost)
        self.moving = exchange(self.block, BIT_CORE)
        return self.block

    def finish(self, *deps):
        moves = [(got, ..., 0, slice(got * 512, got * 512 + 512)) for got in range(2)]
        return place_blocks([self.block, self.moving], [(1024, 2 * self.columns)], moves, deps, FREE)[0]


def relative_weights(gathered, ranges, *deps):
    deps = leaves(deps)

    def kernel(*refs):
        source, outs, sem = refs[0], refs[1 + len(deps) : -1], refs[-1]
        device = lax.axis_index("dp") * 2 + lax.axis_index("tensor")
        copies = []
        for row in range(16):
            for side in range(2):
                apart = side + 2 * (row // 8) + 4 * (row // 4 % 2) + 8 * (row // 2 % 2) + 16 * (row % 2)
                for out, (lo, hi) in zip(outs, ranges):
                    width = hi - lo
                    copies.append(
                        pltpu.make_async_copy(
                            source.at[device ^ apart, :, lo:hi],
                            out.at[row * 64 : row * 64 + 64, side * width : side * width + width],
                            sem.at[len(copies)],
                        )
                    )
        for copy in copies:
            copy.start()
        for copy in copies:
            copy.wait()

    return pl.pallas_call(
        kernel,
        in_specs=[ANYWHERE] * (1 + len(deps)),
        out_specs=[pl.BlockSpec(memory_space=pltpu.VMEM)] * len(ranges),
        out_shape=[jax.ShapeDtypeStruct((1024, 2 * (hi - lo)), jnp.bfloat16) for lo, hi in ranges],
        scratch_shapes=[pltpu.SemaphoreType.DMA((32 * len(ranges),))],
        compiler_params=pltpu.CompilerParams(vmem_limit_bytes=44 << 20),
        cost_estimate=FREE,
    )(gathered, *deps)


def hidden_grads(cot, gathered, first, rest, slope, *deps):
    deps = leaves(deps)
    columns = slope.shape[1] // 2
    later = rest.shape[1] // 2
    width = columns - later
    blocks = []
    for side in range(2):
        middle = side * columns + width // 2
        blocks += [(side, side * columns, middle), (side, middle, side * columns + width)]
        blocks.insert(side, (side + 2, side * columns + width, (side + 1) * columns))

    def kernel(cot_ref, slope_ref, rest_ref, source, *refs):
        out_ref, sum_ref, weights_ref, sem = refs[-4:]
        device = lax.axis_index("dp") * 2 + lax.axis_index("tensor")
        copies = [[], [], [], []]
        for side in range(2):
            start = side * columns
            copies[side + 2].append(
                pltpu.make_async_copy(
                    rest_ref.at[:, side * later : (side + 1) * later],
                    weights_ref.at[:, start + width : start + columns],
                    sem.at[32 + side],
                )
            )
            for row in range(16):
                apart = side + 2 * (row // 8) + 4 * (row // 4 % 2) + 8 * (row // 2 % 2) + 16 * (row % 2)
                copies[side].append(
                    pltpu.make_async_copy(
                        source.at[device ^ apart, :, first : first + width],
                        weights_ref.at[row * 64 : row * 64 + 64, start : start + width],
                        sem.at[side * 16 + row],
                    )
                )
        for group in (2, 3, 0, 1):
            for copy in copies[group]:
                copy.start()
        for group, start, stop in blocks:
            for copy in copies[group]:
                copy.wait()
            copies[group] = []
            at = slice(start, stop)
            product = jnp.dot(cot_ref[...], weights_ref[:, at], preferred_element_type=jnp.float32)
            result = (product * slope_ref[:, at].astype(jnp.float32)).astype(jnp.bfloat16)
            out_ref[:, at] = result
            sum_ref[:, at] = jnp.sum(result.astype(jnp.float32), axis=0, keepdims=True)

    return pl.pallas_call(
        kernel,
        in_specs=[VMEM, VMEM] + [ANYWHERE] * (2 + len(deps)),
        out_specs=[VMEM, VMEM, VMEM],
        out_shape=[
            jax.ShapeDtypeStruct(slope.shape, jnp.bfloat16),
            jax.ShapeDtypeStruct((1, slope.shape[1]), jnp.float32),
            jax.ShapeDtypeStruct((1024, slope.shape[1]), jnp.bfloat16),
        ],
        scratch_shapes=[pltpu.SemaphoreType.DMA((34,))],
        compiler_params=pltpu.CompilerParams(vmem_limit_bytes=12 << 20),
        cost_estimate=FREE,
    )(cot, slope, rest, gathered, *deps)


def bias_rows(own, other):
    width = own.shape[1] - 1024

    def kernel(own_ref, other_ref, first_ref, second_ref, hidden_ref):
        for side, ref in enumerate((own_ref, other_ref)):
            for half, out_ref in enumerate((first_ref, second_ref)):
                start = side * 768
                out_ref[:, start : start + 256] = ref[:, half * 256 : half * 256 + 256]
                out_ref[:, start + 256 : start + 512] = jnp.zeros((1, 256), jnp.float32)
                out_ref[:, start + 512 : start + 768] = ref[:, 512 + half * 256 : 768 + half * 256]
            hidden_ref[:, side * width : side * width + width] = ref[:, 1024:]

    return pl.pallas_call(
        kernel,
        in_specs=[VMEM] * 2,
        out_specs=[VMEM] * 3,
        out_shape=[jax.ShapeDtypeStruct((1, size), jnp.float32) for size in (1536, 1536, 2 * width)],
        compiler_params=pltpu.CompilerParams(vmem_limit_bytes=2 << 20),
        cost_estimate=FREE,
    )(own, other)


def vector_rows(vectors, place, head_sums, hidden_sums, *deps):
    deps = leaves(deps)
    width = hidden_sums.shape[1] // 2

    def kernel(vectors_ref, place_ref, first_ref, second_ref, hidden_ref, *refs):
        left = vectors_ref[...]
        restored = jnp.zeros_like(left)
        for _ in range(3):
            part = left.astype(jnp.bfloat16)
            restored += lax.dot_general(
                part, place_ref[...], (((1,), (1,)), ((), ())), preferred_element_type=jnp.float32
            )
            left = left - part.astype(jnp.float32)
        for side, ref in enumerate(refs[-2:]):
            ref[0:8, :] = restored
            ref[8:16, :] = jnp.zeros_like(restored)
            for i, c in enumerate((0, 2)):
                for half, sums_ref in enumerate((first_ref, second_ref)):
                    source, target = side * 768 + c * 256, i * 512 + half * 256
                    ref[8:9, target : target + 256] = sums_ref[:, source : source + 256]
            for i in range(width // 1024):
                source = side * width + i * 1024
                ref[9 + i : 10 + i, :] = hidden_ref[:, source : source + 1024]

    return pl.pallas_call(
        kernel,
        in_specs=[VMEM] * 5 + [ANYWHERE] * len(deps),
        out_specs=[VMEM] * 2,
        out_shape=[jax.ShapeDtypeStruct((16, 1024), jnp.float32)] * 2,
        compiler_params=pltpu.CompilerParams(vmem_limit_bytes=8 << 20),
        cost_estimate=FREE,
    )(vectors, place, *head_sums, hidden_sums, *deps)


def weight_grads(left, right, keep, *deps):
    deps = leaves(deps)
    columns = right.shape[1]
    width = columns // (4 if columns > 2048 else 2)

    def kernel(left_ref, right_ref, *refs):
        out_ref = refs[-1]
        part = left_ref[:, :512] if keep else left_ref[:, 512:]

        @pl.loop(0, columns // width)
        def _(block):
            at = pl.ds(pl.multiple_of(block * width, width), width)
            product = lax.dot_general(
                part, right_ref[:, at], (((0,), (0,)), ((), ())), preferred_element_type=jnp.float32
            )
            out_ref[:, at] = product.astype(jnp.bfloat16)

    return pl.pallas_call(
        kernel,
        in_specs=[VMEM, VMEM] + [ANYWHERE] * len(deps),
        out_specs=VMEM,
        out_shape=jax.ShapeDtypeStruct((512, columns), jnp.bfloat16),
        compiler_params=pltpu.CompilerParams(vmem_limit_bytes=10 << 20),
        cost_estimate=FREE,
    )(left, right, *deps)


def back_through(grads, weights, *deps):
    deps = leaves(deps)
    width = 512

    def kernel(grads_ref, weights_ref, *refs):
        out_ref = refs[-1]
        for block in range(1024 // width):
            at = slice(block * width, block * width + width)
            out_ref[:, at] = lax.dot_general(
                grads_ref[...], weights_ref[at], (((1,), (1,)), ((), ())), preferred_element_type=jnp.float32
            )

    return pl.pallas_call(
        kernel,
        in_specs=[VMEM, VMEM] + [ANYWHERE] * len(deps),
        out_specs=VMEM,
        out_shape=jax.ShapeDtypeStruct((grads.shape[0], 1024), jnp.float32),
        compiler_params=pltpu.CompilerParams(vmem_limit_bytes=10 << 20),
        cost_estimate=FREE,
    )(grads, weights, *deps)


class Scatter:
    def __init__(self, pieces):
        width, moves = 0, []
        for i, piece in enumerate(pieces):
            moves.append((i, ..., 0, (slice(None), slice(width, width + piece.shape[1]))))
            width += piece.shape[1]
        self.sent = place_blocks(pieces, [(512, width)], moves, (), FREE)[0] if len(pieces) > 1 else pieces[0]
        self.got = exchange(self.sent, BIT_CORE)

    def call(self, kernel, ins, deps, shapes, dtype=jnp.bfloat16):
        deps = leaves(deps)
        outs = [jax.ShapeDtypeStruct(shape, dtype) for shape in shapes]
        size = 2 * sum(v.size for v in ins) + dtype(0).nbytes * sum(v.size for v in outs)
        count = len(ins)
        return pl.pallas_call(
            lambda *refs: kernel(refs[:count], refs[count + len(deps) :]),
            in_specs=[pl.BlockSpec(memory_space=pltpu.VMEM)] * count + [ANYWHERE] * len(deps),
            out_specs=[pl.BlockSpec(memory_space=pltpu.VMEM)] * len(outs),
            out_shape=outs,
            compiler_params=pltpu.CompilerParams(vmem_limit_bytes=4 << 20),
            cost_estimate=STEP,
        )(*ins, *deps)

    def step_one(self, pieces, *deps):
        widths = [piece.shape[1] // 2 for piece in pieces]
        self.columns = sum(widths)
        half = self.columns // 2

        def kernel(ins, outs):
            first = 0
            for i, width in enumerate(widths):
                for part in range(2):
                    start, stop = max(first, part * half), min(first + width, part * half + half)
                    if start >= stop:
                        continue
                    to = slice(start - part * half, stop - part * half)
                    for side in range(2):
                        columns = slice(side * width + start - first, side * width + stop - first)
                        came = slice(2 * first + columns.start, 2 * first + columns.stop)
                        for y in range(2):
                            rows = slice(y * 256, y * 256 + 256)
                            lead, send = (side, y) if part == 0 else (y, side)
                            value = ins[i][rows, columns] + ins[-1][rows, came]
                            outs[2 * part + send][lead, :, to] = value
                first += width

        outs = self.call(kernel, [*pieces, self.got], deps, [(2, 256, half)] * 4)
        self.kept = outs[0::2]
        self.moving = [exchange(outs[1], BIT_Y), exchange(outs[3], BIT_X)]
        return outs

    def step_two(self, *deps):
        half = self.columns // 2

        def kernel(ins, outs):
            for part in range(2):
                for send in range(2):
                    outs[2 * part + send][...] = ins[part][send] + ins[2 + part][send]

        outs = self.call(kernel, [*self.kept, *self.moving], deps, [(256, half)] * 4)
        self.kept = outs[0::2]
        self.moving = [exchange(outs[1], BIT_X), exchange(outs[3], BIT_Y)]
        return outs

    def step_three(self, *deps):
        half = self.columns // 2

        def kernel(ins, outs):
            for part in range(2):
                for send in range(2):
                    rows = slice(send * 128, send * 128 + 128)
                    outs[send][:, part * half : part * half + half] = ins[part][rows] + ins[2 + part][rows]

        outs = self.call(kernel, [*self.kept, *self.moving], deps, [(128, self.columns)] * 2)
        self.kept, self.moving = outs[0], exchange(outs[1], BIT_Z_LOW)
        return outs

    def step_four(self, *deps):
        def kernel(ins, outs):
            for send in range(2):
                rows = slice(send * 64, send * 64 + 64)
                outs[send][...] = ins[0][rows] + ins[1][rows]

        outs = self.call(kernel, [self.kept, self.moving], deps, [(64, self.columns)] * 2)
        self.kept, self.moving = outs[0], exchange(outs[1], BIT_Z_HIGH)
        return outs

    def step_last(self, *deps):
        half = self.columns // 2

        def kernel(ins, outs):
            for part in range(2):
                for block in range(4):
                    rows = slice(block * 64, block * 64 + 64)
                    outs[block][:, part * half : part * half + half] = ins[part][rows] + ins[2 + part][rows]

        outs = self.call(kernel, [*self.kept, *self.moving], deps, [(64, self.columns)] * 4)
        bits = (BIT_Z_HIGH, BIT_Z_LOW, BIT_Z_LOW | BIT_Z_HIGH)
        self.kept, self.moving = outs[0], [exchange(v, bit) for v, bit in zip(outs[1:], bits)]
        return outs

    def finish(self, *deps):
        def kernel(ins, outs):
            total = ins[0][...].astype(jnp.float32)
            for other in ins[1:]:
                total += other[...].astype(jnp.float32)
            outs[0][...] = total

        ins = [self.kept, *jax.tree.leaves(self.moving)]
        return self.call(kernel, ins, deps, [(64, self.columns)], jnp.float32)[0]


def place_matrix():
    relative = lax.broadcasted_iota(jnp.int32, (1024, 1024), 1)
    feature = lax.broadcasted_iota(jnp.int32, (1024, 1024), 0)
    block = relative // 64
    shard = (block // 8) + 2 * (block // 4 % 2) + 4 * (block // 2 % 2) + 8 * (block % 2)
    shard = shard ^ lax.axis_index("dp")
    return (feature == shard * 64 + relative % 64).astype(jnp.bfloat16)


def head_scores(queries, keys, lane, head):
    spare = (1 - head) * 64
    position = lax.broadcasted_iota(jnp.int32, keys.shape, 0)
    mask = jnp.where((lane == spare) & (position >= VALID), masked_score, 0.0).astype(keys.dtype)
    keys = jnp.where((lane // 64) == head, keys, mask)
    queries = jnp.where(lane == spare, jnp.ones_like(queries), queries)
    return lax.dot_general(keys, queries, (((1,), (1,)), ((), ())), preferred_element_type=jnp.float32)


def attend_kernel(q_ref, k_ref, v_ref, *refs):
    o_ref, lse_ref = refs[-2:]
    queries, keys, values = q_ref[...], k_ref[...], v_ref[...]
    queries = queries * jnp.bfloat16(0.125)
    lane = lax.broadcasted_iota(jnp.int32, keys.shape, 1)
    mixed = []
    for head in range(2):
        scores = head_scores(queries, keys, lane, head)
        top = jnp.max(scores, axis=0, keepdims=True)
        expo = jnp.exp(scores - top)
        norm = jnp.sum(expo, axis=0, keepdims=True)
        out = lax.dot_general(
            values, expo.astype(jnp.bfloat16), (((0,), (0,)), ((), ())), preferred_element_type=jnp.float32
        )
        mixed.append(out[head * 64 : head * 64 + 64] / norm)
        lse_ref[0, head : head + 1, :] = top + jnp.log(norm)
    o_ref[...] = jnp.concatenate(mixed, axis=0).T.astype(jnp.bfloat16)


def head_specs():
    return [pl.BlockSpec((SEQ, 128), lambda image, pair, c=c: (image, pair // 2 * 6 + 2 * c + pair % 2)) for c in range(3)]


def mixed_spec(half):
    return pl.BlockSpec((SEQ, 128), lambda image, pair: (image, pair // 2 * 4 + 2 * half + pair % 2))


def attend_pairs(projected, half, mixed, *deps):
    deps = ([] if mixed is None else [mixed]) + leaves(deps)
    rows = projected.shape[0]
    images = rows // SEQ
    return pl.pallas_call(
        attend_kernel,
        grid=(images, 4),
        in_specs=head_specs() + [ANYWHERE] * len(deps),
        out_specs=[
            mixed_spec(half),
            pl.BlockSpec((1, 2, SEQ), lambda image, pair: (image * 4 + pair, 0, 0)),
        ],
        out_shape=[
            jax.ShapeDtypeStruct((rows, 1024), jnp.bfloat16),
            jax.ShapeDtypeStruct((images * 4, 2, SEQ), jnp.float32),
        ],
        input_output_aliases={} if mixed is None else {3: 0},
        compiler_params=pltpu.CompilerParams(vmem_limit_bytes=14 << 20),
        cost_estimate=FREE,
    )(projected, projected, projected, *deps)


def attend_back_kernel(q_ref, k_ref, v_ref, do_ref, lse_ref, *refs):
    out_ref, sum_ref = refs[-2:]
    queries, keys, values, mixed_grad = q_ref[...], k_ref[...], v_ref[...], do_ref[...]
    queries = queries * jnp.bfloat16(0.125)
    lane = lax.broadcasted_iota(jnp.int32, keys.shape, 1)
    dq, dk, dv = [], [], []
    for head in range(2):
        own = (lane // 64) == head
        probs = jnp.exp(head_scores(queries, keys, lane, head) - lse_ref[0, head : head + 1, :])
        dv.append(jnp.dot(probs.astype(jnp.bfloat16), mixed_grad, preferred_element_type=jnp.float32))
        back = lax.dot_general(
            jnp.where(own, values, 0), mixed_grad, (((1,), (1,)), ((), ())), preferred_element_type=jnp.float32
        )
        row = jnp.sum(probs * back, axis=0, keepdims=True)
        score_grad = (probs * (back - row)).astype(jnp.bfloat16)
        dk.append(jnp.dot(score_grad, queries, preferred_element_type=jnp.float32))
        out = lax.dot_general(
            keys, score_grad, (((0,), (0,)), ((), ())), preferred_element_type=jnp.float32
        )
        dq.append(out[head * 64 : head * 64 + 64] * 0.125)
    low = lane < 64
    results = (
        jnp.concatenate(dq, axis=0).T.astype(jnp.bfloat16),
        jnp.where(low, dk[0], dk[1]).astype(jnp.bfloat16),
        jnp.where(low, dv[0], dv[1]).astype(jnp.bfloat16),
    )
    pair = pl.program_id(1)
    for c, result in enumerate(results):
        column = (pair // 2 * 6 + 2 * c + pair % 2) * 128
        at = pl.ds(pl.multiple_of(column, 128), 128)
        out_ref[:, at] = result
        total = jnp.sum(result.astype(jnp.float32), axis=0, keepdims=True)
        sum_ref[0, :, at] = total


def attend_back_pairs(projected, mixed_grad, lse, half, *deps):
    deps = leaves(deps)
    rows = projected.shape[0]
    images = rows // SEQ
    return pl.pallas_call(
        attend_back_kernel,
        grid=(images, 4),
        in_specs=head_specs()
        + [
            mixed_spec(half),
            pl.BlockSpec((1, 2, SEQ), lambda image, pair: (image * 4 + pair, 0, 0)),
        ]
        + [ANYWHERE] * len(deps),
        out_specs=[
            pl.BlockSpec((SEQ, 1536), lambda image, pair: (image, 0)),
            pl.BlockSpec((1, 1, 1536), lambda image, pair: (image, 0, 0)),
        ],
        out_shape=[
            jax.ShapeDtypeStruct((rows, 1536), jnp.bfloat16),
            jax.ShapeDtypeStruct((images, 1, 1536), jnp.float32),
        ],
        compiler_params=pltpu.CompilerParams(vmem_limit_bytes=20 << 20),
        cost_estimate=FREE,
    )(projected, projected, projected, mixed_grad, lse, *deps)


def own_images(
    block_input,
    image_mask,
    w_qkv,
    b_qv,
    w_out,
    b_out,
    w_fc1,
    b_fc1,
    w_fc2,
    b_fc2,
    ln1_gain,
    ln1_bias,
    ln2_gain,
    ln2_bias,
    grad_out,
):
    f32, low = jnp.float32, jnp.bfloat16
    both = range(2)
    rows = block_input.shape[0]
    tensor_index = lax.axis_index("tensor")
    token_index = tensor_index * rows + jnp.arange(rows)
    image_pick = ((token_index // SEQ)[:, None] == jnp.arange(image_mask.shape[0])[None, :]).astype(f32)
    token_keep = jnp.sum(image_pick * image_mask.astype(f32)[None, :], axis=1)
    token_keep = token_keep * (token_index % SEQ < VALID).astype(f32)

    def rows_of(left, right):
        return lax.dot_general(left, right, (((0,), (0,)), ((), ())), preferred_element_type=f32)

    def cols_of(left, right):
        return lax.dot_general(left, right, (((1,), (1,)), ((), ())), preferred_element_type=f32)

    def dot(left, right):
        return jnp.dot(left, right, preferred_element_type=f32)

    def qkv_columns(half):
        part = slice(half * 256, half * 256 + 256)
        return jnp.concatenate([w_qkv[0][:, part], w_qkv[1][:, part], w_qkv[2][:, part]], axis=1)

    bias_own = jnp.concatenate([b_qv.reshape(-1), b_fc1])[None, :]
    *b_heads, b_hidden = bias_rows(bias_own, exchange(bias_own, BIT_X))
    qkv = [Gather(qkv_columns(0))]
    gathered = lax.all_gather(jnp.concatenate([w_fc1, w_fc2.T[:, :1536]], axis=1), AXES, axis=0, tiled=False)

    go = qkv[0].step_one(b_hidden)
    place = after(place_matrix(), go)
    vectors = jnp.stack([b_out, b_fc2, ln1_gain, ln1_bias, ln2_gain, ln2_bias])
    vectors = jnp.dot(vectors, place.astype(f32), precision=lax.Precision.HIGHEST)
    b_out, b_fc2, ln1_gain, ln1_bias, ln2_gain, ln2_bias = vectors
    signal = dot(block_input, place)
    cot_low = dot(grad_out * token_keep.astype(low)[:, None], place).astype(low)
    cot = cot_low.astype(f32)
    normed_one = normalize(signal, ln1_gain, ln1_bias).astype(low)

    qkv.append(Gather(qkv_columns(1), go))
    go = qkv[0].step_two(qkv[1].shard, normed_one, cot_low, b_fc2)
    go = qkv[1].step_one(go)
    go = qkv[0].step_three(go)
    go = qkv[1].step_two(go)
    out = Gather(w_out.T, go)
    go = qkv[0].step_four(out.shard)
    w_heads, projected, lse = [], [], []

    def project(half, *deps):
        w_heads.append(qkv[half].finish(*deps))
        projected.append((dot(normed_one, w_heads[half]) + b_heads[half]).astype(low))
        return projected[half]

    go = project(0, go)
    go = qkv[1].step_three(go)
    go = out.step_one(go)
    mixed, lse_half = attend_pairs(projected[0], 0, None, go)
    lse.append(lse_half)
    go = out.step_two(mixed)
    go = qkv[1].step_four(go, cost=FREE)
    go = project(1, go)
    go = out.step_three(go)
    two = Gather(w_fc2.T[:, 1536:], go)
    mixed, lse_half = attend_pairs(projected[1], 1, mixed, go, two.shard)
    lse.append(lse_half)
    go = two.step_one(mixed)
    go = out.step_four(go)
    w_mix = out.finish(go)
    attn = cols_of(mixed, w_mix)
    resid = signal + (attn + b_out)
    normed_two = normalize(resid, ln2_gain, ln2_bias).astype(low)
    go = two.step_two(normed_two)
    (w_one,) = relative_weights(gathered, [(0, 2048)], go)
    pre = dot(normed_two, w_one) + b_hidden
    phi = 0.5 * (1.0 + lax.erf(pre * (0.5**0.5)))
    hidden = (pre * phi).astype(low)
    slope = (phi + pre * (jnp.exp(-0.5 * pre * pre) * (0.5 / 3.141592653589793) ** 0.5)).astype(low)

    go = two.step_three(hidden)
    fc2_far = weight_grads(cot_low, hidden, False, go)
    fc2_sum = Scatter([fc2_far])
    go = fc2_sum.step_one([weight_grads(cot_low, hidden, True, fc2_far)])
    go = two.step_four(go)
    pre_grad, fc1_bias_grad, w_two = hidden_grads(cot_low, gathered, 2048, two.finish(go), slope)
    fc1_far = weight_grads(normed_two, pre_grad, False)
    normed_two_grad = back_through(pre_grad, w_one, fc1_far)
    go = fc2_sum.step_two(normed_two_grad)
    fc1_sum = Scatter([after(fc1_far, go)])
    fc1_near = weight_grads(normed_two, pre_grad, True, go)
    go = fc1_sum.step_one([fc1_near])
    go = fc2_sum.step_three(go)
    _, norm_two_back = jax.vjp(normalize, resid, ln2_gain, ln2_bias)
    resid_back, gain_two_grad, bias_two_grad = norm_two_back(after(normed_two_grad, go))
    resid_grad = cot + resid_back
    resid_low = resid_grad.astype(low)
    mixed_grad = dot(resid_low, w_mix).astype(low)
    grads, sums = attend_back_pairs(projected[0], mixed_grad, lse[0], 0)
    head_grads, head_sums = [grads], [sums.sum(0)]
    go = fc2_sum.step_four(grads)
    go = fc1_sum.step_two(go)

    def first_pieces(keep, go):
        heads_part = weight_grads(normed_one, head_grads[0], keep, go)
        return [heads_part, weight_grads(resid_low, mixed, keep, heads_part)]

    heads_sum = [Scatter(first_pieces(False, go))]
    go = heads_sum[0].step_one(first_pieces(True, heads_sum[0].sent))
    grads, sums = attend_back_pairs(projected[1], mixed_grad, lse[1], 1, go)
    head_grads.append(grads)
    head_sums.append(sums.sum(0))
    fc2_grad = fc2_sum.finish(head_grads[1])
    go = fc1_sum.step_three(fc2_grad)
    heads_far = weight_grads(normed_one, head_grads[1], False, go)
    heads_sum.append(Scatter([heads_far]))
    heads_near = weight_grads(normed_one, head_grads[1], True, heads_far)
    go = heads_sum[0].step_two(heads_near)
    go = heads_sum[1].step_one([heads_near], go)
    normed_one_grad = sum(
        cols_of(head_grads[half], w_heads[half]) * one_after(go) for half in both
    )
    go = fc1_sum.step_four(normed_one_grad)
    go = heads_sum[0].step_three(go)
    _, norm_one_back = jax.vjp(normalize, signal, ln1_gain, ln1_bias)
    input_back, gain_one_grad, bias_one_grad = norm_one_back(normed_one_grad)
    out_sum, cot_sum = jnp.sum(resid_grad, axis=0), jnp.sum(cot, axis=0)
    zeros = jnp.zeros_like(out_sum)
    vectors = jnp.stack(
        [gain_one_grad, bias_one_grad, gain_two_grad, bias_two_grad, out_sum, cot_sum, zeros, zeros]
    )
    own, other = vector_rows(vectors, place, head_sums, fc1_bias_grad, go)
    sums = own + exchange(other, BIT_X)
    go = heads_sum[1].step_two(own)
    input_grad = cols_of((resid_grad + input_back).astype(low), place).astype(low)
    sums = after(sums, go)
    sums = sums + exchange(sums, BIT_Y)
    fc1_grad = fc1_sum.finish(go)
    go = heads_sum[0].step_four(fc1_grad)
    go = heads_sum[1].step_three(input_grad, go)
    sums = after(sums, go)
    sums = sums + exchange(sums, BIT_Z_HIGH) + exchange(sums, BIT_Z_LOW) + exchange(sums, BIT_Z_HIGH | BIT_Z_LOW)
    mlp = back_through(hidden, w_two, go)
    go = heads_sum[1].step_four(mlp)
    sums = after(sums, go)
    sums = sums + exchange(sums, BIT_CORE)
    layer_output = ((resid + (mlp + b_fc2)) * token_keep[:, None]).astype(low)
    layer_output = cols_of(layer_output, place).astype(low)
    heads_grad = [heads_sum[0].finish(go), heads_sum[1].finish()]
    side_sums = sums[8:11].reshape(3072)
    qkv_grad = jnp.concatenate([g[:, :768].reshape(64, 3, 256) for g in heads_grad], axis=2)
    return (
        layer_output,
        input_grad,
        qkv_grad.transpose(1, 0, 2),
        side_sums[:1024].reshape(2, 512),
        heads_grad[0][:, 768:].T,
        sums[4],
        fc1_grad,
        side_sums[1024:],
        fc2_grad.T,
        sums[5],
        sums[0],
        sums[1],
        sums[2],
        sums[3],
    )


def solution(mesh):
    def plan(block_input, *others):
        whole_images = block_input.shape[0] % SEQ == 0
        if whole_images and mesh.shape["dp"] == 16 and mesh.shape["tensor"] == 2:
            return own_images(block_input, *others)
        return split_heads(block_input, *others)

    return jax.shard_map(
        plan,
        mesh=mesh,
        in_specs=(
            P(("dp", "tensor"), None),
            P("dp"),
            P(None, "dp", "tensor"),
            P(None, "tensor"),
            P("tensor", "dp"),
            P(),
            P("dp", "tensor"),
            P("tensor"),
            P("tensor", "dp"),
            P(),
            P(),
            P(),
            P(),
            P(),
            P(("dp", "tensor"), None),
        ),
        out_specs=(
            P(("dp", "tensor"), None),
            P(("dp", "tensor"), None),
            P(None, "dp", "tensor"),
            P(None, "tensor"),
            P("tensor", "dp"),
            P(),
            P("dp", "tensor"),
            P("tensor"),
            P("tensor", "dp"),
            P(),
            P(),
            P(),
            P(),
            P(),
        ),
        check_vma=False,
    )
```

```python
import functools

import jax
import jax.numpy as jnp
from jax import lax
from jax.experimental import pallas as pl
from jax.experimental.pallas import tpu as pltpu
from jax.sharding import PartitionSpec as P

HEADS = 16
SEQ = 584
VALID = 577


layer_eps = 1e-06
masked_score = -1e30


def normalize(signal, gain_vec, bias_vec):
    row_mean = jnp.mean(signal, axis=-1, keepdims=True)
    centred = signal - row_mean
    row_spread = jnp.mean(centred * centred, axis=-1, keepdims=True)
    return centred * lax.rsqrt(row_spread + layer_eps) * gain_vec + bias_vec


def gelu_exact(signal):
    return jax.nn.gelu(signal, approximate=False)


def masked_scores(queries, key_proj):
    score_scale = queries.shape[-1] ** (-0.5)
    scores = (
        jnp.einsum("qhe,khe->hqk", queries, key_proj, preferred_element_type=jnp.float32)
        * score_scale
    )
    valid_keys = jnp.arange(scores.shape[-1]) < VALID
    return jnp.where(valid_keys[None, None, :], scores, masked_score)


def attend_image(operands):
    queries, key_proj, value_proj = operands
    logits = masked_scores(queries, key_proj)
    row_top = jnp.max(logits, axis=-1, keepdims=True)
    row_expo = jnp.exp(logits - row_top)
    row_total = jnp.sum(row_expo, axis=-1, keepdims=True)
    weights = (row_expo / row_total).astype(jnp.bfloat16)
    head_mixed = jnp.einsum("hqk,khe->qhe", weights, value_proj, preferred_element_type=jnp.float32)
    return (head_mixed.astype(jnp.bfloat16), (row_top + jnp.log(row_total))[..., 0])


def attend_back(operands):
    queries, key_proj, value_proj, mixed_grad, row_lse = operands
    score_scale = queries.shape[-1] ** (-0.5)
    logits = masked_scores(queries, key_proj)
    probs = jnp.exp(logits - row_lse[..., None])
    value_grad = jnp.einsum(
        "hqk,qhe->khe", probs.astype(jnp.bfloat16), mixed_grad, preferred_element_type=jnp.float32
    )
    prob_grad = jnp.einsum(
        "qhe,khe->hqk", mixed_grad, value_proj, preferred_element_type=jnp.float32
    )
    score_grad = probs * (prob_grad - jnp.sum(probs * prob_grad, axis=-1, keepdims=True))
    score_grad = score_grad.astype(jnp.bfloat16)
    query_grad = (
        jnp.einsum("hqk,khe->qhe", score_grad, key_proj, preferred_element_type=jnp.float32)
        * score_scale
    )
    key_grad = (
        jnp.einsum("hqk,qhe->khe", score_grad, queries, preferred_element_type=jnp.float32)
        * score_scale
    )
    return (
        query_grad.astype(jnp.bfloat16),
        key_grad.astype(jnp.bfloat16),
        value_grad.astype(jnp.bfloat16),
    )


def split_heads(
    block_input,
    image_mask,
    w_qkv,
    b_qv,
    w_out,
    b_out,
    w_fc1,
    b_fc1,
    w_fc2,
    b_fc2,
    ln1_gain,
    ln1_bias,
    ln2_gain,
    ln2_bias,
    grad_out,
):
    local_rows = block_input.shape[0]
    model_width = block_input.shape[1]
    image_count = image_mask.shape[0]
    head_dim = model_width // HEADS
    local_width = w_qkv.shape[2]
    local_heads = local_width // head_dim
    tensor_index = lax.axis_index("tensor")
    token_index = tensor_index * local_rows + jnp.arange(local_rows)
    image_of = token_index // SEQ
    position = token_index % SEQ
    image_pick = (image_of[:, None] == jnp.arange(image_count)[None, :]).astype(jnp.float32)
    token_keep = jnp.sum(image_pick * image_mask.astype(jnp.float32)[None, :], axis=1)
    token_keep = token_keep * (position < VALID).astype(jnp.float32)
    contract_rows = (((0,), (0,)), ((), ()))
    contract_cols = (((1,), (1,)), ((), ()))
    full_qkv, full_out, full_fc1, full_fc2 = (
        lax.all_gather(w_qkv, "dp", axis=1, tiled=True),
        lax.all_gather(w_out, "dp", axis=1, tiled=True),
        lax.all_gather(w_fc1, "dp", axis=0, tiled=True),
        lax.all_gather(w_fc2, "dp", axis=1, tiled=True),
    )
    input_float = block_input.astype(jnp.float32)
    normed_one = normalize(input_float, ln1_gain, ln1_bias).astype(jnp.bfloat16)
    inputs_one = lax.all_gather(normed_one, "tensor", axis=0, tiled=True)
    group_rows = inputs_one.shape[0]
    projected = jnp.einsum("td,cde->cte", inputs_one, full_qkv, preferred_element_type=jnp.float32)
    queries = (projected[0] + b_qv[0]).astype(jnp.bfloat16)
    key_proj = projected[1].astype(jnp.bfloat16)
    value_proj = (projected[2] + b_qv[1]).astype(jnp.bfloat16)
    head_shape = (group_rows // SEQ, SEQ, local_heads, head_dim)
    query_heads = queries.reshape(head_shape)
    key_heads = key_proj.reshape(head_shape)
    value_heads = value_proj.reshape(head_shape)
    head_mixed, row_lse = lax.map(attend_image, (query_heads, key_heads, value_heads))
    head_mixed = head_mixed.reshape(group_rows, local_width)
    row_block = head_mixed
    attn_sum = lax.psum_scatter(
        jnp.dot(row_block, full_out, preferred_element_type=jnp.float32),
        "tensor",
        scatter_dimension=0,
        tiled=True,
    )
    resid = input_float + (attn_sum + b_out)
    normed_two = normalize(resid, ln2_gain, ln2_bias).astype(jnp.bfloat16)
    inputs_two = lax.all_gather(normed_two, "tensor", axis=0, tiled=True)
    hidden_pre = jnp.dot(inputs_two, full_fc1, preferred_element_type=jnp.float32) + b_fc1
    hidden = gelu_exact(hidden_pre).astype(jnp.bfloat16)
    row_block = hidden
    mlp_sum = lax.psum_scatter(
        jnp.dot(row_block, full_fc2, preferred_element_type=jnp.float32).astype(jnp.bfloat16),
        "tensor",
        scatter_dimension=0,
        tiled=True,
    ).astype(jnp.float32)
    layer_output = ((resid + (mlp_sum + b_fc2)) * token_keep[:, None]).astype(jnp.bfloat16)
    cot_rows = grad_out * token_keep.astype(jnp.bfloat16)[:, None]
    cot_float = cot_rows.astype(jnp.float32)
    cot_group = lax.all_gather(cot_rows, "tensor", axis=0, tiled=True)
    fc2_grad_group = lax.dot_general(
        hidden, cot_group, contract_rows, preferred_element_type=jnp.float32
    )
    hidden_grad = lax.dot_general(
        cot_group, full_fc2, contract_cols, preferred_element_type=jnp.float32
    )
    gelu_value, gelu_back = jax.vjp(gelu_exact, hidden_pre)
    pre_grad = gelu_back(hidden_grad)[0].astype(jnp.bfloat16)
    fc1_bias_grad = jnp.sum(pre_grad, axis=0, dtype=jnp.float32)
    fc1_grad_group = lax.dot_general(
        inputs_two, pre_grad, contract_rows, preferred_element_type=jnp.float32
    )
    row_block = pre_grad
    normed_two_grad = lax.psum_scatter(
        lax.dot_general(row_block, full_fc1, contract_cols, preferred_element_type=jnp.float32),
        "tensor",
        scatter_dimension=0,
        tiled=True,
    )
    norm_two_value, norm_two_back = jax.vjp(normalize, resid, ln2_gain, ln2_bias)
    resid_back, gain_two_grad, bias_two_grad = norm_two_back(normed_two_grad)
    resid_grad = cot_float + resid_back
    out_bias_grad = jnp.sum(resid_grad, axis=0)
    fc2_bias_grad = jnp.sum(cot_float, axis=0)
    resid_low = resid_grad.astype(jnp.bfloat16)
    resid_group = lax.all_gather(resid_low, "tensor", axis=0, tiled=True)
    out_grad_group = lax.dot_general(
        head_mixed, resid_group, contract_rows, preferred_element_type=jnp.float32
    )
    mixed_grad = lax.dot_general(
        resid_group, full_out, contract_cols, preferred_element_type=jnp.float32
    ).astype(jnp.bfloat16)
    query_grad, key_grad, value_grad = lax.map(
        attend_back, (query_heads, key_heads, value_heads, mixed_grad.reshape(head_shape), row_lse)
    )
    stacked_grads = jnp.stack(
        [
            query_grad.reshape(group_rows, local_width),
            key_grad.reshape(group_rows, local_width),
            value_grad.reshape(group_rows, local_width),
        ]
    )
    qkv_grad_group = jnp.einsum(
        "td,cte->cde", inputs_one, stacked_grads, preferred_element_type=jnp.float32
    )
    qv_bias_grad = jnp.stack(
        [
            jnp.sum(stacked_grads[0], axis=0, dtype=jnp.float32),
            jnp.sum(stacked_grads[2], axis=0, dtype=jnp.float32),
        ]
    )
    row_block = stacked_grads
    normed_one_grad = lax.psum_scatter(
        jnp.einsum("cte,cde->td", row_block, full_qkv, preferred_element_type=jnp.float32),
        "tensor",
        scatter_dimension=0,
        tiled=True,
    )
    norm_one_value, norm_one_back = jax.vjp(normalize, input_float, ln1_gain, ln1_bias)
    input_back, gain_one_grad, bias_one_grad = norm_one_back(normed_one_grad)
    input_grad = (resid_grad + input_back).astype(jnp.bfloat16)
    grad_w_qkv, grad_w_out, grad_w_fc1, grad_w_fc2 = (
        lax.psum_scatter(qkv_grad_group, "dp", scatter_dimension=1, tiled=True),
        lax.psum_scatter(out_grad_group, "dp", scatter_dimension=1, tiled=True),
        lax.psum_scatter(fc1_grad_group, "dp", scatter_dimension=0, tiled=True),
        lax.psum_scatter(fc2_grad_group, "dp", scatter_dimension=1, tiled=True),
    )
    vector_sums = lax.psum(
        (gain_one_grad, bias_one_grad, gain_two_grad, bias_two_grad, out_bias_grad, fc2_bias_grad),
        ("dp", "tensor"),
    )
    qv_sum, fc1_sum = lax.psum((qv_bias_grad, fc1_bias_grad), "dp")
    return (
        layer_output,
        input_grad,
        grad_w_qkv,
        qv_sum,
        grad_w_out,
        vector_sums[4],
        grad_w_fc1,
        fc1_sum,
        grad_w_fc2,
        vector_sums[5],
        vector_sums[0],
        vector_sums[1],
        vector_sums[2],
        vector_sums[3],
    )


BIT_X, BIT_CORE, BIT_Y, BIT_Z_LOW, BIT_Z_HIGH = 1, 2, 4, 8, 16
AXES = ("dp", "tensor")


def exchange(block, bit):
    return lax.ppermute(block, AXES, [(src, src ^ bit) for src in range(32)])


def leaves(deps):
    return jax.tree.leaves(deps)


ANYWHERE = pl.BlockSpec(memory_space=pl.ANY)
VMEM = pl.BlockSpec(memory_space=pltpu.VMEM)
FREE = pl.CostEstimate(flops=2 * 10**8, bytes_accessed=1, transcendentals=0)
STEP = pl.CostEstimate(flops=10**10, bytes_accessed=1, transcendentals=0)


def after(value, *deps):
    deps = leaves(deps)
    return pl.pallas_call(
        lambda *refs: None,
        in_specs=[ANYWHERE] * (1 + len(deps)),
        out_specs=ANYWHERE,
        out_shape=jax.ShapeDtypeStruct(value.shape, value.dtype),
        input_output_aliases={0: 0},
        compiler_params=pltpu.CompilerParams(vmem_limit_bytes=1 << 20),
    )(value, *deps)


def one_after(*deps):
    deps = leaves(deps)

    def kernel(*refs):
        refs[-1][...] = jnp.ones_like(refs[-1])

    return pl.pallas_call(
        kernel,
        in_specs=[ANYWHERE] * len(deps),
        out_shape=jax.ShapeDtypeStruct((1, 128), jnp.float32),
        compiler_params=pltpu.CompilerParams(vmem_limit_bytes=1 << 20),
    )(*deps)[0, 0]


def place_blocks(arrays, shapes, moves, deps=(), cost=None):
    deps = leaves(deps)

    def kernel(*refs):
        outs, sem = refs[len(arrays) + len(deps) : -1], refs[-1]
        copies = [
            pltpu.make_async_copy(refs[src].at[at], outs[dst].at[to], sem.at[i])
            for i, (src, at, dst, to) in enumerate(moves)
        ]
        for copy in copies:
            copy.start()
        for copy in copies:
            copy.wait()

    size = 4 * sum(v.size for v in arrays)
    return pl.pallas_call(
        kernel,
        in_specs=[ANYWHERE] * (len(arrays) + len(deps)),
        out_specs=[ANYWHERE] * len(shapes),
        out_shape=[jax.ShapeDtypeStruct(shape, jnp.bfloat16) for shape in shapes],
        scratch_shapes=[pltpu.SemaphoreType.DMA((len(moves),))],
        compiler_params=pltpu.CompilerParams(vmem_limit_bytes=1 << 20),
        cost_estimate=cost or STEP,
    )(*arrays, *deps)


class Gather:
    def __init__(self, shard, *deps):
        self.columns = shard.shape[1]
        self.shard = place_blocks([shard], [shard.shape], [(0, ..., 0, ...)], deps, FREE)[0] if deps else shard
        self.moving = exchange(self.shard, BIT_Z_HIGH)

    def step_one(self, *deps):
        rows = self.shard.shape[0]
        moves = [(got, ..., 0, slice(got * rows, got * rows + rows)) for got in range(2)]
        (self.block,) = place_blocks([self.shard, self.moving], [(2 * rows, self.columns)], moves, deps)
        self.moving = exchange(self.block, BIT_Z_LOW)
        return self.block

    def step_two(self, *deps):
        half = self.columns // 2
        moves = []
        for got in range(2):
            for part in range(2):
                columns = slice(part * half, part * half + half)
                moves.append((got, (slice(None), columns), part, slice(got * 128, got * 128 + 128)))
        self.blocks = place_blocks([self.block, self.moving], [(256, half)] * 2, moves, deps)
        self.moving = [exchange(self.blocks[0], BIT_X), exchange(self.blocks[1], BIT_Y)]
        return self.blocks

    def step_three(self, *deps):
        half = self.columns // 2
        moves = [(2 * got + part, ..., part, got) for got in range(2) for part in range(2)]
        self.blocks = place_blocks([*self.blocks, *self.moving], [(2, 256, half)] * 2, moves, deps)
        self.moving = [exchange(self.blocks[0], BIT_Y), exchange(self.blocks[1], BIT_X)]
        return self.blocks

    def step_four(self, *deps, cost=None):
        half = self.columns // 2
        moves = []
        for got, part, lead in [(j, k, m) for j in range(2) for k in range(2) for m in range(2)]:
            side, y = (lead, got) if part == 0 else (got, lead)
            column = side * self.columns + part * half
            moves.append((2 * got + part, lead, 0, (slice(y * 256, y * 256 + 256), slice(column, column + half))))
        (self.block,) = place_blocks([*self.blocks, *self.moving], [(512, 2 * self.columns)], moves, deps, cost)
        self.moving = exchange(self.block, BIT_CORE)
        return self.block

    def finish(self, *deps):
        moves = [(got, ..., 0, slice(got * 512, got * 512 + 512)) for got in range(2)]
        return place_blocks([self.block, self.moving], [(1024, 2 * self.columns)], moves, deps, FREE)[0]


def relative_weights(gathered, ranges, *deps):
    deps = leaves(deps)

    def kernel(*refs):
        source, outs, sem = refs[0], refs[1 + len(deps) : -1], refs[-1]
        device = lax.axis_index("dp") * 2 + lax.axis_index("tensor")
        copies = []
        for row in range(16):
            for side in range(2):
                apart = side + 2 * (row // 8) + 4 * (row // 4 % 2) + 8 * (row // 2 % 2) + 16 * (row % 2)
                for out, (lo, hi) in zip(outs, ranges):
                    width = hi - lo
                    copies.append(
                        pltpu.make_async_copy(
                            source.at[device ^ apart, :, lo:hi],
                            out.at[row * 64 : row * 64 + 64, side * width : side * width + width],
                            sem.at[len(copies)],
                        )
                    )
        for copy in copies:
            copy.start()
        for copy in copies:
            copy.wait()

    return pl.pallas_call(
        kernel,
        in_specs=[ANYWHERE] * (1 + len(deps)),
        out_specs=[pl.BlockSpec(memory_space=pltpu.VMEM)] * len(ranges),
        out_shape=[jax.ShapeDtypeStruct((1024, 2 * (hi - lo)), jnp.bfloat16) for lo, hi in ranges],
        scratch_shapes=[pltpu.SemaphoreType.DMA((32 * len(ranges),))],
        compiler_params=pltpu.CompilerParams(vmem_limit_bytes=44 << 20),
        cost_estimate=FREE,
    )(gathered, *deps)


def hidden_grads(cot, gathered, first, rest, slope, *deps):
    deps = leaves(deps)
    columns = slope.shape[1] // 2
    later = rest.shape[1] // 2
    width = columns - later
    blocks = []
    for side in range(2):
        middle = side * columns + width // 2
        blocks += [(side, side * columns, middle), (side, middle, side * columns + width)]
        blocks.insert(side, (side + 2, side * columns + width, (side + 1) * columns))

    def kernel(cot_ref, slope_ref, rest_ref, source, *refs):
        out_ref, sum_ref, weights_ref, sem = refs[-4:]
        device = lax.axis_index("dp") * 2 + lax.axis_index("tensor")
        copies = [[], [], [], []]
        for side in range(2):
            start = side * columns
            copies[side + 2].append(
                pltpu.make_async_copy(
                    rest_ref.at[:, side * later : (side + 1) * later],
                    weights_ref.at[:, start + width : start + columns],
                    sem.at[32 + side],
                )
            )
            for row in range(16):
                apart = side + 2 * (row // 8) + 4 * (row // 4 % 2) + 8 * (row // 2 % 2) + 16 * (row % 2)
                copies[side].append(
                    pltpu.make_async_copy(
                        source.at[device ^ apart, :, first : first + width],
                        weights_ref.at[row * 64 : row * 64 + 64, start : start + width],
                        sem.at[side * 16 + row],
                    )
                )
        for group in (2, 3, 0, 1):
            for copy in copies[group]:
                copy.start()
        for group, start, stop in blocks:
            for copy in copies[group]:
                copy.wait()
            copies[group] = []
            at = slice(start, stop)
            product = jnp.dot(cot_ref[...], weights_ref[:, at], preferred_element_type=jnp.float32)
            result = (product * slope_ref[:, at].astype(jnp.float32)).astype(jnp.bfloat16)
            out_ref[:, at] = result
            sum_ref[:, at] = jnp.sum(result.astype(jnp.float32), axis=0, keepdims=True)

    return pl.pallas_call(
        kernel,
        in_specs=[VMEM, VMEM] + [ANYWHERE] * (2 + len(deps)),
        out_specs=[VMEM, VMEM, VMEM],
        out_shape=[
            jax.ShapeDtypeStruct(slope.shape, jnp.bfloat16),
            jax.ShapeDtypeStruct((1, slope.shape[1]), jnp.float32),
            jax.ShapeDtypeStruct((1024, slope.shape[1]), jnp.bfloat16),
        ],
        scratch_shapes=[pltpu.SemaphoreType.DMA((34,))],
        compiler_params=pltpu.CompilerParams(vmem_limit_bytes=12 << 20),
        cost_estimate=FREE,
    )(cot, slope, rest, gathered, *deps)


def bias_rows(own, other):
    width = own.shape[1] - 1024

    def kernel(own_ref, other_ref, first_ref, second_ref, hidden_ref):
        for side, ref in enumerate((own_ref, other_ref)):
            for half, out_ref in enumerate((first_ref, second_ref)):
                start = side * 768
                out_ref[:, start : start + 256] = ref[:, half * 256 : half * 256 + 256]
                out_ref[:, start + 256 : start + 512] = jnp.zeros((1, 256), jnp.float32)
                out_ref[:, start + 512 : start + 768] = ref[:, 512 + half * 256 : 768 + half * 256]
            hidden_ref[:, side * width : side * width + width] = ref[:, 1024:]

    return pl.pallas_call(
        kernel,
        in_specs=[VMEM] * 2,
        out_specs=[VMEM] * 3,
        out_shape=[jax.ShapeDtypeStruct((1, size), jnp.float32) for size in (1536, 1536, 2 * width)],
        compiler_params=pltpu.CompilerParams(vmem_limit_bytes=2 << 20),
        cost_estimate=FREE,
    )(own, other)


def vector_rows(vectors, place, head_sums, hidden_sums, *deps):
    deps = leaves(deps)
    width = hidden_sums.shape[1] // 2

    def kernel(vectors_ref, place_ref, first_ref, second_ref, hidden_ref, *refs):
        left = vectors_ref[...]
        restored = jnp.zeros_like(left)
        for _ in range(3):
            part = left.astype(jnp.bfloat16)
            restored += lax.dot_general(
                part, place_ref[...], (((1,), (1,)), ((), ())), preferred_element_type=jnp.float32
            )
            left = left - part.astype(jnp.float32)
        for side, ref in enumerate(refs[-2:]):
            ref[0:8, :] = restored
            ref[8:16, :] = jnp.zeros_like(restored)
            for i, c in enumerate((0, 2)):
                for half, sums_ref in enumerate((first_ref, second_ref)):
                    source, target = side * 768 + c * 256, i * 512 + half * 256
                    ref[8:9, target : target + 256] = sums_ref[:, source : source + 256]
            for i in range(width // 1024):
                source = side * width + i * 1024
                ref[9 + i : 10 + i, :] = hidden_ref[:, source : source + 1024]

    return pl.pallas_call(
        kernel,
        in_specs=[VMEM] * 5 + [ANYWHERE] * len(deps),
        out_specs=[VMEM] * 2,
        out_shape=[jax.ShapeDtypeStruct((16, 1024), jnp.float32)] * 2,
        compiler_params=pltpu.CompilerParams(vmem_limit_bytes=8 << 20),
        cost_estimate=FREE,
    )(vectors, place, *head_sums, hidden_sums, *deps)


def weight_grads(left, right, keep, *deps):
    deps = leaves(deps)
    columns = right.shape[1]
    width = columns // (4 if columns > 2048 else 2)

    def kernel(left_ref, right_ref, *refs):
        out_ref = refs[-1]
        part = left_ref[:, :512] if keep else left_ref[:, 512:]

        @pl.loop(0, columns // width)
        def _(block):
            at = pl.ds(pl.multiple_of(block * width, width), width)
            product = lax.dot_general(
                part, right_ref[:, at], (((0,), (0,)), ((), ())), preferred_element_type=jnp.float32
            )
            out_ref[:, at] = product.astype(jnp.bfloat16)

    return pl.pallas_call(
        kernel,
        in_specs=[VMEM, VMEM] + [ANYWHERE] * len(deps),
        out_specs=VMEM,
        out_shape=jax.ShapeDtypeStruct((512, columns), jnp.bfloat16),
        compiler_params=pltpu.CompilerParams(vmem_limit_bytes=10 << 20),
        cost_estimate=FREE,
    )(left, right, *deps)


def back_through(grads, weights, *deps):
    deps = leaves(deps)
    width = 512

    def kernel(grads_ref, weights_ref, *refs):
        out_ref = refs[-1]
        for block in range(1024 // width):
            at = slice(block * width, block * width + width)
            out_ref[:, at] = lax.dot_general(
                grads_ref[...], weights_ref[at], (((1,), (1,)), ((), ())), preferred_element_type=jnp.float32
            )

    return pl.pallas_call(
        kernel,
        in_specs=[VMEM, VMEM] + [ANYWHERE] * len(deps),
        out_specs=VMEM,
        out_shape=jax.ShapeDtypeStruct((grads.shape[0], 1024), jnp.float32),
        compiler_params=pltpu.CompilerParams(vmem_limit_bytes=10 << 20),
        cost_estimate=FREE,
    )(grads, weights, *deps)


class Scatter:
    def __init__(self, pieces):
        width, moves = 0, []
        for i, piece in enumerate(pieces):
            moves.append((i, ..., 0, (slice(None), slice(width, width + piece.shape[1]))))
            width += piece.shape[1]
        self.sent = place_blocks(pieces, [(512, width)], moves, (), FREE)[0] if len(pieces) > 1 else pieces[0]
        self.got = exchange(self.sent, BIT_CORE)

    def call(self, kernel, ins, deps, shapes, dtype=jnp.bfloat16):
        deps = leaves(deps)
        outs = [jax.ShapeDtypeStruct(shape, dtype) for shape in shapes]
        size = 2 * sum(v.size for v in ins) + dtype(0).nbytes * sum(v.size for v in outs)
        count = len(ins)
        return pl.pallas_call(
            lambda *refs: kernel(refs[:count], refs[count + len(deps) :]),
            in_specs=[pl.BlockSpec(memory_space=pltpu.VMEM)] * count + [ANYWHERE] * len(deps),
            out_specs=[pl.BlockSpec(memory_space=pltpu.VMEM)] * len(outs),
            out_shape=outs,
            compiler_params=pltpu.CompilerParams(vmem_limit_bytes=4 << 20),
            cost_estimate=STEP,
        )(*ins, *deps)

    def step_one(self, pieces, *deps):
        widths = [piece.shape[1] // 2 for piece in pieces]
        self.columns = sum(widths)
        half = self.columns // 2

        def kernel(ins, outs):
            first = 0
            for i, width in enumerate(widths):
                for part in range(2):
                    start, stop = max(first, part * half), min(first + width, part * half + half)
                    if start >= stop:
                        continue
                    to = slice(start - part * half, stop - part * half)
                    for side in range(2):
                        columns = slice(side * width + start - first, side * width + stop - first)
                        came = slice(2 * first + columns.start, 2 * first + columns.stop)
                        for y in range(2):
                            rows = slice(y * 256, y * 256 + 256)
                            lead, send = (side, y) if part == 0 else (y, side)
                            value = ins[i][rows, columns] + ins[-1][rows, came]
                            outs[2 * part + send][lead, :, to] = value
                first += width

        outs = self.call(kernel, [*pieces, self.got], deps, [(2, 256, half)] * 4)
        self.kept = outs[0::2]
        self.moving = [exchange(outs[1], BIT_Y), exchange(outs[3], BIT_X)]
        return outs

    def step_two(self, *deps):
        half = self.columns // 2

        def kernel(ins, outs):
            for part in range(2):
                for send in range(2):
                    outs[2 * part + send][...] = ins[part][send] + ins[2 + part][send]

        outs = self.call(kernel, [*self.kept, *self.moving], deps, [(256, half)] * 4)
        self.kept = outs[0::2]
        self.moving = [exchange(outs[1], BIT_X), exchange(outs[3], BIT_Y)]
        return outs

    def step_three(self, *deps):
        half = self.columns // 2

        def kernel(ins, outs):
            for part in range(2):
                for send in range(2):
                    rows = slice(send * 128, send * 128 + 128)
                    outs[send][:, part * half : part * half + half] = ins[part][rows] + ins[2 + part][rows]

        outs = self.call(kernel, [*self.kept, *self.moving], deps, [(128, self.columns)] * 2)
        self.kept, self.moving = outs[0], exchange(outs[1], BIT_Z_LOW)
        return outs

    def step_four(self, *deps):
        def kernel(ins, outs):
            for send in range(2):
                rows = slice(send * 64, send * 64 + 64)
                outs[send][...] = ins[0][rows] + ins[1][rows]

        outs = self.call(kernel, [self.kept, self.moving], deps, [(64, self.columns)] * 2)
        self.kept, self.moving = outs[0], exchange(outs[1], BIT_Z_HIGH)
        return outs

    def step_last(self, *deps):
        half = self.columns // 2

        def kernel(ins, outs):
            for part in range(2):
                for block in range(4):
                    rows = slice(block * 64, block * 64 + 64)
                    outs[block][:, part * half : part * half + half] = ins[part][rows] + ins[2 + part][rows]

        outs = self.call(kernel, [*self.kept, *self.moving], deps, [(64, self.columns)] * 4)
        bits = (BIT_Z_HIGH, BIT_Z_LOW, BIT_Z_LOW | BIT_Z_HIGH)
        self.kept, self.moving = outs[0], [exchange(v, bit) for v, bit in zip(outs[1:], bits)]
        return outs

    def finish(self, *deps):
        def kernel(ins, outs):
            total = ins[0][...].astype(jnp.float32)
            for other in ins[1:]:
                total += other[...].astype(jnp.float32)
            outs[0][...] = total

        ins = [self.kept, *jax.tree.leaves(self.moving)]
        return self.call(kernel, ins, deps, [(64, self.columns)], jnp.float32)[0]


def place_matrix():
    relative = lax.broadcasted_iota(jnp.int32, (1024, 1024), 1)
    feature = lax.broadcasted_iota(jnp.int32, (1024, 1024), 0)
    block = relative // 64
    shard = (block // 8) + 2 * (block // 4 % 2) + 4 * (block // 2 % 2) + 8 * (block % 2)
    shard = shard ^ lax.axis_index("dp")
    return (feature == shard * 64 + relative % 64).astype(jnp.bfloat16)


def head_scores(queries, keys, lane, head):
    spare = (1 - head) * 64
    position = lax.broadcasted_iota(jnp.int32, keys.shape, 0)
    mask = jnp.where((lane == spare) & (position >= VALID), masked_score, 0.0).astype(keys.dtype)
    keys = jnp.where((lane // 64) == head, keys, mask)
    queries = jnp.where(lane == spare, jnp.ones_like(queries), queries)
    return lax.dot_general(keys, queries, (((1,), (1,)), ((), ())), preferred_element_type=jnp.float32)


def attend_kernel(q_ref, k_ref, v_ref, *refs):
    o_ref, lse_ref = refs[-2:]
    queries, keys, values = q_ref[...], k_ref[...], v_ref[...]
    queries = queries * jnp.bfloat16(0.125)
    lane = lax.broadcasted_iota(jnp.int32, keys.shape, 1)
    mixed = []
    for head in range(2):
        scores = head_scores(queries, keys, lane, head)
        top = jnp.max(scores, axis=0, keepdims=True)
        expo = jnp.exp(scores - top)
        norm = jnp.sum(expo, axis=0, keepdims=True)
        out = lax.dot_general(
            values, expo.astype(jnp.bfloat16), (((0,), (0,)), ((), ())), preferred_element_type=jnp.float32
        )
        mixed.append(out[head * 64 : head * 64 + 64] / norm)
        lse_ref[0, head : head + 1, :] = top + jnp.log(norm)
    o_ref[...] = jnp.concatenate(mixed, axis=0).T.astype(jnp.bfloat16)


def head_specs():
    return [pl.BlockSpec((SEQ, 128), lambda image, pair, c=c: (image, pair // 2 * 6 + 2 * c + pair % 2)) for c in range(3)]


def mixed_spec(half):
    return pl.BlockSpec((SEQ, 128), lambda image, pair: (image, pair // 2 * 4 + 2 * half + pair % 2))


def attend_pairs(projected, half, mixed, *deps):
    deps = ([] if mixed is None else [mixed]) + leaves(deps)
    rows = projected.shape[0]
    images = rows // SEQ
    return pl.pallas_call(
        attend_kernel,
        grid=(images, 4),
        in_specs=head_specs() + [ANYWHERE] * len(deps),
        out_specs=[
            mixed_spec(half),
            pl.BlockSpec((1, 2, SEQ), lambda image, pair: (image * 4 + pair, 0, 0)),
        ],
        out_shape=[
            jax.ShapeDtypeStruct((rows, 1024), jnp.bfloat16),
            jax.ShapeDtypeStruct((images * 4, 2, SEQ), jnp.float32),
        ],
        input_output_aliases={} if mixed is None else {3: 0},
        compiler_params=pltpu.CompilerParams(vmem_limit_bytes=14 << 20),
        cost_estimate=FREE,
    )(projected, projected, projected, *deps)


def attend_back_kernel(q_ref, k_ref, v_ref, do_ref, lse_ref, *refs):
    out_ref, sum_ref = refs[-2:]
    queries, keys, values, mixed_grad = q_ref[...], k_ref[...], v_ref[...], do_ref[...]
    queries = queries * jnp.bfloat16(0.125)
    lane = lax.broadcasted_iota(jnp.int32, keys.shape, 1)
    dq, dk, dv = [], [], []
    for head in range(2):
        own = (lane // 64) == head
        probs = jnp.exp(head_scores(queries, keys, lane, head) - lse_ref[0, head : head + 1, :])
        dv.append(jnp.dot(probs.astype(jnp.bfloat16), mixed_grad, preferred_element_type=jnp.float32))
        back = lax.dot_general(
            jnp.where(own, values, 0), mixed_grad, (((1,), (1,)), ((), ())), preferred_element_type=jnp.float32
        )
        row = jnp.sum(probs * back, axis=0, keepdims=True)
        score_grad = (probs * (back - row)).astype(jnp.bfloat16)
        dk.append(jnp.dot(score_grad, queries, preferred_element_type=jnp.float32))
        out = lax.dot_general(
            keys, score_grad, (((0,), (0,)), ((), ())), preferred_element_type=jnp.float32
        )
        dq.append(out[head * 64 : head * 64 + 64] * 0.125)
    low = lane < 64
    results = (
        jnp.concatenate(dq, axis=0).T.astype(jnp.bfloat16),
        jnp.where(low, dk[0], dk[1]).astype(jnp.bfloat16),
        jnp.where(low, dv[0], dv[1]).astype(jnp.bfloat16),
    )
    pair = pl.program_id(1)
    for c, result in enumerate(results):
        column = (pair // 2 * 6 + 2 * c + pair % 2) * 128
        at = pl.ds(pl.multiple_of(column, 128), 128)
        out_ref[:, at] = result
        total = jnp.sum(result.astype(jnp.float32), axis=0, keepdims=True)
        sum_ref[0, :, at] = total


def attend_back_pairs(projected, mixed_grad, lse, half, *deps):
    deps = leaves(deps)
    rows = projected.shape[0]
    images = rows // SEQ
    return pl.pallas_call(
        attend_back_kernel,
        grid=(images, 4),
        in_specs=head_specs()
        + [
            mixed_spec(half),
            pl.BlockSpec((1, 2, SEQ), lambda image, pair: (image * 4 + pair, 0, 0)),
        ]
        + [ANYWHERE] * len(deps),
        out_specs=[
            pl.BlockSpec((SEQ, 1536), lambda image, pair: (image, 0)),
            pl.BlockSpec((1, 1, 1536), lambda image, pair: (image, 0, 0)),
        ],
        out_shape=[
            jax.ShapeDtypeStruct((rows, 1536), jnp.bfloat16),
            jax.ShapeDtypeStruct((images, 1, 1536), jnp.float32),
        ],
        compiler_params=pltpu.CompilerParams(vmem_limit_bytes=20 << 20),
        cost_estimate=FREE,
    )(projected, projected, projected, mixed_grad, lse, *deps)


def own_images(
    block_input,
    image_mask,
    w_qkv,
    b_qv,
    w_out,
    b_out,
    w_fc1,
    b_fc1,
    w_fc2,
    b_fc2,
    ln1_gain,
    ln1_bias,
    ln2_gain,
    ln2_bias,
    grad_out,
):
    f32, low = jnp.float32, jnp.bfloat16
    both = range(2)
    rows = block_input.shape[0]
    tensor_index = lax.axis_index("tensor")
    token_index = tensor_index * rows + jnp.arange(rows)
    image_pick = ((token_index // SEQ)[:, None] == jnp.arange(image_mask.shape[0])[None, :]).astype(f32)
    token_keep = jnp.sum(image_pick * image_mask.astype(f32)[None, :], axis=1)
    token_keep = token_keep * (token_index % SEQ < VALID).astype(f32)

    def rows_of(left, right):
        return lax.dot_general(left, right, (((0,), (0,)), ((), ())), preferred_element_type=f32)

    def cols_of(left, right):
        return lax.dot_general(left, right, (((1,), (1,)), ((), ())), preferred_element_type=f32)

    def dot(left, right):
        return jnp.dot(left, right, preferred_element_type=f32)

    def qkv_columns(half):
        part = slice(half * 256, half * 256 + 256)
        return jnp.concatenate([w_qkv[0][:, part], w_qkv[1][:, part], w_qkv[2][:, part]], axis=1)

    bias_own = jnp.concatenate([b_qv.reshape(-1), b_fc1])[None, :]
    *b_heads, b_hidden = bias_rows(bias_own, exchange(bias_own, BIT_X))
    qkv = [Gather(qkv_columns(0))]
    gathered = lax.all_gather(jnp.concatenate([w_fc1, w_fc2.T[:, :1280]], axis=1), AXES, axis=0, tiled=False)

    go = qkv[0].step_one(b_hidden)
    place = after(place_matrix(), go)
    vectors = jnp.stack([b_out, b_fc2, ln1_gain, ln1_bias, ln2_gain, ln2_bias])
    vectors = jnp.dot(vectors, place.astype(f32), precision=lax.Precision.HIGHEST)
    b_out, b_fc2, ln1_gain, ln1_bias, ln2_gain, ln2_bias = vectors
    signal = dot(block_input, place)
    cot_low = dot(grad_out * token_keep.astype(low)[:, None], place).astype(low)
    cot = cot_low.astype(f32)
    normed_one = normalize(signal, ln1_gain, ln1_bias).astype(low)

    qkv.append(Gather(qkv_columns(1), go))
    go = qkv[0].step_two(qkv[1].shard, normed_one, cot_low, b_fc2)
    go = qkv[1].step_one(go)
    go = qkv[0].step_three(go)
    go = qkv[1].step_two(go)
    out = Gather(w_out.T, go)
    go = qkv[0].step_four(out.shard)
    w_heads, projected, lse = [], [], []

    def project(half, *deps):
        w_heads.append(qkv[half].finish(*deps))
        projected.append((dot(normed_one, w_heads[half]) + b_heads[half]).astype(low))
        return projected[half]

    go = project(0, go)
    go = qkv[1].step_three(go)
    go = out.step_one(go)
    mixed, lse_half = attend_pairs(projected[0], 0, None, go)
    lse.append(lse_half)
    go = out.step_two(mixed)
    go = qkv[1].step_four(go, cost=FREE)
    go = project(1, go)
    go = out.step_three(go)
    two = Gather(w_fc2.T[:, 1280:], go)
    mixed, lse_half = attend_pairs(projected[1], 1, mixed, go, two.shard)
    lse.append(lse_half)
    go = two.step_one(mixed)
    go = out.step_four(go)
    w_mix = out.finish(go)
    attn = cols_of(mixed, w_mix)
    resid = signal + (attn + b_out)
    normed_two = normalize(resid, ln2_gain, ln2_bias).astype(low)
    go = two.step_two(normed_two)
    (w_one,) = relative_weights(gathered, [(0, 2048)], go)
    pre = dot(normed_two, w_one) + b_hidden
    phi = 0.5 * (1.0 + lax.erf(pre * (0.5**0.5)))
    hidden = (pre * phi).astype(low)
    slope = (phi + pre * (jnp.exp(-0.5 * pre * pre) * (0.5 / 3.141592653589793) ** 0.5)).astype(low)

    go = two.step_three(hidden)
    fc2_far = weight_grads(cot_low, hidden, False, go)
    fc2_sum = Scatter([fc2_far])
    go = fc2_sum.step_one([weight_grads(cot_low, hidden, True, fc2_far)])
    go = two.step_four(go)
    pre_grad, fc1_bias_grad, w_two = hidden_grads(cot_low, gathered, 2048, two.finish(go), slope)
    fc1_far = weight_grads(normed_two, pre_grad, False)
    normed_two_grad = back_through(pre_grad, w_one, fc1_far)
    go = fc2_sum.step_two(normed_two_grad)
    fc1_sum = Scatter([after(fc1_far, go)])
    fc1_near = weight_grads(normed_two, pre_grad, True, go)
    go = fc1_sum.step_one([fc1_near])
    go = fc2_sum.step_three(go)
    _, norm_two_back = jax.vjp(normalize, resid, ln2_gain, ln2_bias)
    resid_back, gain_two_grad, bias_two_grad = norm_two_back(after(normed_two_grad, go))
    resid_grad = cot + resid_back
    resid_low = resid_grad.astype(low)
    mixed_grad = dot(resid_low, w_mix).astype(low)
    grads, sums = attend_back_pairs(projected[0], mixed_grad, lse[0], 0)
    head_grads, head_sums = [grads], [sums.sum(0)]
    go = fc2_sum.step_four(grads)
    go = fc1_sum.step_two(go)

    def first_pieces(keep, go):
        heads_part = weight_grads(normed_one, head_grads[0], keep, go)
        return [heads_part, weight_grads(resid_low, mixed, keep, heads_part)]

    heads_sum = [Scatter(first_pieces(False, go))]
    go = heads_sum[0].step_one(first_pieces(True, heads_sum[0].sent))
    grads, sums = attend_back_pairs(projected[1], mixed_grad, lse[1], 1, go)
    head_grads.append(grads)
    head_sums.append(sums.sum(0))
    fc2_grad = fc2_sum.finish(head_grads[1])
    go = fc1_sum.step_three(fc2_grad)
    heads_far = weight_grads(normed_one, head_grads[1], False, go)
    heads_sum.append(Scatter([heads_far]))
    heads_near = weight_grads(normed_one, head_grads[1], True, heads_far)
    go = heads_sum[0].step_two(heads_near)
    go = heads_sum[1].step_one([heads_near], go)
    normed_one_grad = sum(
        cols_of(head_grads[half], w_heads[half]) * one_after(go) for half in both
    )
    go = fc1_sum.step_four(normed_one_grad)
    go = heads_sum[0].step_three(go)
    _, norm_one_back = jax.vjp(normalize, signal, ln1_gain, ln1_bias)
    input_back, gain_one_grad, bias_one_grad = norm_one_back(normed_one_grad)
    out_sum, cot_sum = jnp.sum(resid_grad, axis=0), jnp.sum(cot, axis=0)
    zeros = jnp.zeros_like(out_sum)
    vectors = jnp.stack(
        [gain_one_grad, bias_one_grad, gain_two_grad, bias_two_grad, out_sum, cot_sum, zeros, zeros]
    )
    own, other = vector_rows(vectors, place, head_sums, fc1_bias_grad, go)
    sums = own + exchange(other, BIT_X)
    go = heads_sum[1].step_two(own)
    input_grad = cols_of((resid_grad + input_back).astype(low), place).astype(low)
    sums = after(sums, go)
    sums = sums + exchange(sums, BIT_Y)
    fc1_grad = fc1_sum.finish(go)
    go = heads_sum[0].step_four(fc1_grad)
    go = heads_sum[1].step_three(input_grad, go)
    sums = after(sums, go)
    sums = sums + exchange(sums, BIT_Z_HIGH) + exchange(sums, BIT_Z_LOW) + exchange(sums, BIT_Z_HIGH | BIT_Z_LOW)
    mlp = back_through(hidden, w_two, go)
    go = heads_sum[1].step_four(mlp)
    sums = after(sums, go)
    sums = sums + exchange(sums, BIT_CORE)
    layer_output = ((resid + (mlp + b_fc2)) * token_keep[:, None]).astype(low)
    layer_output = cols_of(layer_output, place).astype(low)
    heads_grad = [heads_sum[0].finish(go), heads_sum[1].finish()]
    side_sums = sums[8:11].reshape(3072)
    qkv_grad = jnp.concatenate([g[:, :768].reshape(64, 3, 256) for g in heads_grad], axis=2)
    return (
        layer_output,
        input_grad,
        qkv_grad.transpose(1, 0, 2),
        side_sums[:1024].reshape(2, 512),
        heads_grad[0][:, 768:].T,
        sums[4],
        fc1_grad,
        side_sums[1024:],
        fc2_grad.T,
        sums[5],
        sums[0],
        sums[1],
        sums[2],
        sums[3],
    )


def solution(mesh):
    def plan(block_input, *others):
        whole_images = block_input.shape[0] % SEQ == 0
        if whole_images and mesh.shape["dp"] == 16 and mesh.shape["tensor"] == 2:
            return own_images(block_input, *others)
        return split_heads(block_input, *others)

    return jax.shard_map(
        plan,
        mesh=mesh,
        in_specs=(
            P(("dp", "tensor"), None),
            P("dp"),
            P(None, "dp", "tensor"),
            P(None, "tensor"),
            P("tensor", "dp"),
            P(),
            P("dp", "tensor"),
            P("tensor"),
            P("tensor", "dp"),
            P(),
            P(),
            P(),
            P(),
            P(),
            P(("dp", "tensor"), None),
        ),
        out_specs=(
            P(("dp", "tensor"), None),
            P(("dp", "tensor"), None),
            P(None, "dp", "tensor"),
            P(None, "tensor"),
            P("tensor", "dp"),
            P(),
            P("dp", "tensor"),
            P("tensor"),
            P("tensor", "dp"),
            P(),
            P(),
            P(),
            P(),
            P(),
        ),
        check_vma=False,
    )
```
